128 devices in a mesh: member: 2 (over z_lo), grid: 64 (over y, x, z_hi, core).
Axes of the slice: x: 4, y: 4, z: 4 (z_hi: 2, z_lo: 2; z = z_hi * 2 + z_lo), core: 2. Of those that a mesh axis runs over, the one named last changes fastest.
Arguments:
- latent: bfloat16 [8, 8192, 1024], P('member', 'grid'), may hold values from -6 to 6
- grid_in: bfloat16 [8, 8192, 1024], P('member', 'grid'), may hold values from -6 to 6
- w_src: bfloat16 [1024, 1024], replicated, may hold values from -0.1875 to 0.1875
- w_tgt: bfloat16 [1024, 1024], replicated, may hold values from -0.1875 to 0.1875
- w_mix: bfloat16 [1024, 1024], replicated, may hold values from -0.1875 to 0.1875
- w_out: bfloat16 [1024, 100], replicated, may hold values from -0.1875 to 0.1875
- truth: float32 [100, 8192], P(None, 'grid'), may hold values from -6 to 6
- area: float32 [8192], P('grid'), may hold values from 0.2 to 30, as said below
- nbr: int32 [16, 8192], P(None, 'grid'), may hold values from 0 to 255
- mask: int32 [16, 8192], P(None, 'grid'), may hold values 0 or 1
Outputs:
- d_latent: bfloat16 [8, 8192, 1024], P('member', 'grid')
- d_grid: bfloat16 [8, 8192, 1024], P('member', 'grid')
- grad_src: float32 [1024, 1024], P('grid')
- grad_tgt: float32 [1024, 1024], P('grid')
- grad_mix: float32 [1024, 1024], P('grid')
- grad_out: float32 [1024, 100], P('grid')
The draws below stay inside these ranges and needn't reach their ends.
Inputs may be any that keep to these rules, and one draw needn't show every extreme that they name: area weights are positive.
All inputs are finite; a program needn't handle non-finite values. No bound on the sum of `mask` on one device may be relied on, other than what follows from the above.
Results may differ from the reference program's by a relative error of at most 0.039.
Values may be sent and summed in bfloat16 or wider, within the bound.
A program may use at most 128 MiB of HBM per device.

```python
import math
import jax
import jax.numpy as jnp
from jax import lax

D = 1024
F = 100
NBR = 16
HALO = 64
GRID_DEV = 128
SRC_DEV = 128
MEMBERS = 8
NGRID = 8192
NSRC = 8192


def draw_area(key, part):
    key = jax.random.fold_in(key, 7)
    ramp = jnp.arange(NGRID, dtype=jnp.float32) / jnp.float32(max(NGRID - 1, 1))
    noise = jax.random.uniform(key, (NGRID,), jnp.float32, -1.0, 1.0)
    return (1.0 + 2.0 * ramp) * jnp.exp(1.15 * noise)


def place_ends(drawn, key, low, largest):
    index_at = [jax.random.randint(jax.random.fold_in(key, axis), (), 0, length) for axis, length in enumerate(drawn.shape)]
    widest = drawn.shape.index(max(drawn.shape))
    next_to = index_at[:widest] + [(index_at[widest] + 1) % drawn.shape[widest]] + index_at[widest + 1:]
    return drawn.at[tuple(index_at)].set(low).at[tuple(next_to)].set(largest)


def shard_levels(rng, shape, pieces, least, largest):
    def one(axis_at, shards_of):
        draws = jax.random.uniform(jax.random.fold_in(jax.random.fold_in(rng, 6), axis_at), (shards_of,), jnp.float32, least / len(pieces), largest / len(pieces))
        return jnp.repeat(jnp.exp(draws), shape[axis_at] // shards_of).reshape((-1,) + (1,) * (len(shape) - axis_at - 1))

    loudness = one(*pieces[0])
    for cut in pieces[1:]:
        loudness = loudness * one(*cut)
    return loudness


def normal_values(own_key, shape, scale, limit, pieces=(), kind=jnp.bfloat16):
    entries = jax.random.normal(own_key, shape, jnp.float32) * scale
    if len(pieces) > 0:
        entries = shard_levels(own_key, shape, pieces, -0.22, 0.18) * entries
    return jnp.clip(entries, min=-limit, max=limit).astype(kind)


def setup_inputs(seed: int = 0) -> dict:
    keys = jax.random.split(jax.random.key(seed), 11)
    return {
        "latent": normal_values(keys[0], (MEMBERS, NSRC, D), 1.0, 6.0, ((0, 2), (1, 64))),
        "grid_in": normal_values(keys[1], (MEMBERS, NGRID, D), 1.0, 6.0, ((0, 2), (1, 64))),
        "w_src": normal_values(keys[2], (D, D), D ** -0.5, 0.1875),
        "w_tgt": normal_values(keys[3], (D, D), D ** -0.5, 0.1875),
        "w_mix": normal_values(keys[4], (D, D), D ** -0.5, 0.1875),
        "w_out": normal_values(keys[5], (D, F), D ** -0.5, 0.1875),
        "truth": normal_values(keys[6], (F, NGRID), 1.0, 6.0, ((1, 64),), jnp.float32),
        "area": draw_area(jax.random.fold_in(keys[10], 71), 0),
        "nbr": place_ends(jax.random.randint(keys[8], (NBR, NGRID), 0, SRC_DEV + 2 * HALO), jax.random.fold_in(keys[8], 1), 0, (SRC_DEV + 2 * HALO) - 1).astype(jnp.int32),
        "mask": place_ends((jax.random.randint(keys[9], (NBR, NGRID), 0, 4) < 3).astype(jnp.int32), jax.random.fold_in(keys[9], 1), 0, 1),
    }


smooth_sq = 0.0025
fair_weight = 0.95
norm_eps = 1e-05

def silu_grad(value):
    sig = jax.nn.sigmoid(value)
    return sig * (1.0 + value * (1.0 - sig))

def layer_stats(hsum):
    centre = hsum - lax.optimization_barrier(jnp.mean(hsum, axis=-1, keepdims=True))
    var = lax.optimization_barrier(jnp.mean(centre * centre, axis=-1, keepdims=True))
    inv_std = lax.rsqrt(var + norm_eps)
    return (centre * inv_std, inv_std)

def fdot(left, right):
    return jnp.dot(left.astype(jnp.float32), right.astype(jnp.float32), preferred_element_type=jnp.float32, precision=lax.Precision.HIGHEST)

def reference(latent, grid_in, w_src, w_tgt, w_mix, w_out, truth, area, nbr, mask):
    tiles = jnp.arange(NGRID, dtype=jnp.int32) // GRID_DEV
    source = (tiles[None, :] * SRC_DEV - HALO + nbr) % NSRC
    source = source.astype(jnp.int32)
    maskf = mask.astype(jnp.float32)

    def projections(z_one, x_one):
        proj_src = fdot(z_one, w_src).astype(jnp.bfloat16)
        proj_tgt = fdot(x_one, w_tgt).astype(jnp.bfloat16)
        return (proj_src, proj_tgt)

    def forward_one(items):
        z_one, x_one = items
        proj_src, proj_tgt = projections(z_one, x_one)
        tgt_f = proj_tgt.astype(jnp.float32)

        def step(acc, slot):
            index, weight = slot
            pre = proj_src[index].astype(jnp.float32) + tgt_f
            return (acc + weight[:, None] * jax.nn.silu(pre), None)
        acc, _ = lax.scan(step, jnp.zeros((NGRID, D), jnp.float32), (source, maskf))
        agg = (0.25 * acc).astype(jnp.bfloat16)
        hsum = x_one.astype(jnp.float32) + fdot(agg, w_mix)
        normed = layer_stats(hsum)[0].astype(jnp.bfloat16)
        out = fdot(normed, w_out)
        return (agg, hsum, normed, out.T)
    agg, hsum, normed, y = lax.map(forward_one, (latent, grid_in))
    count = MEMBERS
    skill = jnp.sqrt((y - truth[None]) ** 2 + smooth_sq)
    pair_grad = jnp.zeros_like(y)
    for other in range(count):
        diff = y - y[other][None]
        root = jnp.sqrt(diff * diff + smooth_sq)
        pair_grad = pair_grad + diff / root
    skill_grad = (y - truth[None]) / skill
    dy = (area[None, None, :] * (skill_grad / count - fair_weight / (count * (count - 1)) * pair_grad)).astype(jnp.bfloat16)

    def backward_one(items):
        z_one, x_one, agg_one, h_one, n_one, dy_one = items
        proj_src, proj_tgt = projections(z_one, x_one)
        tgt_f = proj_tgt.astype(jnp.float32)
        g_out = fdot(n_one.T, dy_one.T)
        dnorm = fdot(dy_one.T, w_out.T)
        nh, inv_std = layer_stats(h_one)
        dh = inv_std * (dnorm - lax.optimization_barrier(jnp.mean(dnorm, axis=-1, keepdims=True)) - nh * lax.optimization_barrier(jnp.mean(dnorm * nh, axis=-1, keepdims=True)))
        dh = dh.astype(jnp.bfloat16)
        g_mix = fdot(agg_one.T, dh)
        dagg = fdot(dh, w_mix.T).astype(jnp.bfloat16).astype(jnp.float32)

        def step(carry, slot):
            dq_acc, dp_acc = carry
            index, weight = slot
            pre = proj_src[index].astype(jnp.float32) + tgt_f
            dpre = 0.25 * weight[:, None] * dagg * silu_grad(pre)
            return ((dq_acc + dpre, dp_acc.at[index].add(dpre)), None)
        init = (jnp.zeros((NGRID, D), jnp.float32), jnp.zeros((NSRC, D), jnp.float32))
        (dq_acc, dp_acc), _ = lax.scan(step, init, (source, maskf))
        dq = dq_acc.astype(jnp.bfloat16)
        dp = dp_acc.astype(jnp.bfloat16)
        g_tgt = fdot(x_one.T, dq)
        g_src = fdot(z_one.T, dp)
        d_grid = (dh.astype(jnp.float32) + fdot(dq, w_tgt.T)).astype(jnp.bfloat16)
        d_latent = fdot(dp, w_src.T).astype(jnp.bfloat16)
        return (d_latent, d_grid, g_src, g_tgt, g_mix, g_out)
    d_latent, d_grid, g_src, g_tgt, g_mix, g_out = lax.map(backward_one, (latent, grid_in, agg, hsum, normed, dy))
    scale = 1.0 / math.sqrt(NGRID * MEMBERS)
    return (d_latent, d_grid, lax.optimization_barrier(jnp.sum(g_src, axis=0)) * scale, lax.optimization_barrier(jnp.sum(g_tgt, axis=0)) * scale, lax.optimization_barrier(jnp.sum(g_mix, axis=0)) * scale, lax.optimization_barrier(jnp.sum(g_out, axis=0)) * scale)
```

```python
import math

import jax
import jax.numpy as jnp
from jax import lax
from jax.experimental import pallas as pl
from jax.experimental.pallas import tpu as pltpu
from jax.sharding import PartitionSpec as P

HALO = 64
SMOOTH = 0.0025
FAIR = 0.95
EPS = 1e-05
BF = jnp.bfloat16
F32 = jnp.float32
MESH = pl.DeviceIdType.MESH
CW = 256
NY, NX, NZ, NC = 4, 4, 2, 2
FP = 128


def dot(a, b):
    return lax.dot_general(a, b, (((1,), (0,)), ((), ())), preferred_element_type=F32)


def dot_nt(a, b):
    return lax.dot_general(a, b, (((1,), (1,)), ((), ())), preferred_element_type=F32)


def dot_tn(a, b):
    return lax.dot_general(a, b, (((0,), (0,)), ((), ())), preferred_element_type=F32)


class Place:
    def __init__(self):
        self.me = lax.axis_index("member")
        t = lax.axis_index("grid")
        tiles = NY * NX * NZ * NC
        self.y, self.x, self.z, self.c = t // 16, (t // 4) % 4, (t // 2) % 2, t % 2
        self.up = (self.me, (t + 1) % tiles)
        self.down = (self.me, (t + tiles - 1) % tiles)
        self.mate = (1 - self.me, t)
        self.core = self.at(c=1 - self.c)
        self.y_ring = (self.at(y=(self.y + 1) % 4), self.at(y=(self.y + 3) % 4))
        self.x_ring = (self.at(x=(self.x + 1) % 4), self.at(x=(self.x + 3) % 4))
        self.z_far = (self.me, self.at(z=1 - self.z)[1])
        self.z_both = (1 - self.me, self.z_far[1])
        self.partners = (self.up, self.down, self.core, *self.y_ring, *self.x_ring,
                         self.mate, self.z_far, self.z_both)

    def at(self, y=None, x=None, z=None, c=None):
        y = self.y if y is None else y
        x = self.x if x is None else x
        z = self.z if z is None else z
        c = self.c if c is None else c
        return (self.me, y * 16 + x * 4 + z * 2 + c)


class Wire:
    def __init__(self, send, recv):
        self.send, self.recv, self.used = send, recv, 0

    def copy(self, src, dst, device):
        at = self.used
        self.used += 1
        return pltpu.make_async_remote_copy(
            src_ref=src, dst_ref=dst, send_sem=self.send.at[at], recv_sem=self.recv.at[at],
            device_id=device, device_id_type=MESH)


def add_into(dst, *others):
    total = dst[...].astype(F32)
    for o in others:
        total = total + o[...].astype(F32)
    dst[...] = total.astype(BF)


class Ring:
    def __init__(self, wire, p, ring, block, a, b, d):
        self.wire, self.p, self.ring, self.block = wire, p, ring, block
        self.a, self.b, self.d = a, b, d
        self.nxt, self.prv = (p + 1) % 4, (p + 3) % 4

    def start(self):
        w, (plus, minus), block = self.wire, self.ring, self.block
        opp = (self.p + 2) % 4
        self.first = [w.copy(block(opp, 0), self.a.at[0], plus),
                      w.copy(block(opp, 1), self.a.at[1], minus)]
        self.second = [w.copy(block(self.nxt, 1), self.b.at[0], plus),
                       w.copy(block(self.prv, 0), self.b.at[1], minus)]
        for one in self.first + self.second:
            one.start()

    def middle(self):
        w, (plus, minus), block = self.wire, self.ring, self.block
        self.third = [w.copy(block(self.nxt, 0), self.d.at[0], plus),
                      w.copy(block(self.prv, 1), self.d.at[1], minus)]
        self.first[0].wait()
        add_into(block(self.nxt, 0), self.a.at[0])
        self.third[0].start()
        self.first[1].wait()
        add_into(block(self.prv, 1), self.a.at[1])
        self.third[1].start()

    def finish(self):
        for one in self.second + self.third:
            one.wait()
        add_into(self.block(self.p, 0), self.b.at[1], self.d.at[0])
        add_into(self.block(self.p, 1), self.b.at[0], self.d.at[1])


class Half:
    def __init__(self, place, wire, part, held, cols, y_first, bufs, zbuf):
        self.place, self.wire, self.zbuf, self.cols = place, wire, zbuf, cols
        self.part, self.held = part, held
        y, x = place.y, place.x

        def wide_y(d, h):
            return held.at[d, pl.ds(2 * h, 2), :, :, cols]

        def wide_x(d, h):
            return held.at[pl.ds(2 * h, 2), d, :, :, cols]

        def thin_x(d, h):
            return held.at[y, d, h, :, cols]

        def thin_y(d, h):
            return held.at[d, x, h, :, cols]

        on_y, on_x = (y, place.y_ring), (x, place.x_ring)
        if y_first:
            self.one = Ring(wire, *on_y, wide_y, *bufs[:3])
            self.two = Ring(wire, *on_x, thin_x, *bufs[3:])
        else:
            self.one = Ring(wire, *on_x, wide_x, *bufs[:3])
            self.two = Ring(wire, *on_y, thin_y, *bufs[3:])

    def start(self):
        cols = self.cols
        self.cross = [self.wire.copy(self.part.at[1 - self.place.c, yy, :, :, :, cols],
                                     self.held.at[yy, :, :, :, cols], self.place.core) for yy in range(NY)]
        for one in self.cross:
            one.start()

    def s1(self):
        for one in self.cross:
            one.wait()
        cols = self.cols

        def add(yy, _):
            add_into(self.held.at[yy, :, :, :, cols], self.part.at[self.place.c, yy, :, :, :, cols])
            return 0

        lax.fori_loop(0, NY, add, 0)
        self.one.start()

    def s2(self):
        self.one.middle()

    def s3(self):
        self.one.finish()
        self.two.start()

    def s4(self):
        self.two.middle()

    def s5(self):
        self.two.finish()
        p = self.place
        mine = self.held.at[p.y, p.x]
        self.last = [self.wire.copy(mine.at[p.z, :, self.cols], self.zbuf.at[0], p.mate),
                     self.wire.copy(mine.at[1 - p.z, :, self.cols], self.zbuf.at[1], p.z_far),
                     self.wire.copy(mine.at[1 - p.z, :, self.cols], self.zbuf.at[2], p.z_both)]
        for one in self.last:
            one.start()

    def s6(self, scale):
        p = self.place
        for one in self.last:
            one.wait()
        total = self.held[p.y, p.x, p.z, :, self.cols].astype(F32)
        for k in range(3):
            total = total + self.zbuf[k].astype(F32)
        return total * scale


def put(part, block, cols):
    for b in range(NY * NX * NZ * NC):
        part[b % 2, b // 16, (b // 4) % 4, (b // 2) % 2, :, cols] = block[b * 16:(b + 1) * 16]


def body(scale, lat, grid, wsrc_in, wtgt_in, wmix_in, wout_in, truth_in, area_in, nbr, mask,
         d_latent, d_grid, o_src, o_tgt, o_mix, o_out,
         wsrc, wtgt, wmix, wout, truth, area,
         pick, pick_t, hits, hits_t, maskb, proj, tgt, slope, slope_sum, agg, normed, inv, ys, dys, dh, dq, dpe,
         agg_x, normed_x, grid_x, lat_x,
         halo, rims, part_src, part_tgt, part_mix, held_src, held_tgt, held_mix, *rest):
    send_sem, recv_sem, halo_send, halo_recv, rim_send, rim_recv, y_send, y_recv, load_sem = rest[-9:]
    bufs = rest[:-9]
    members, rows, width = grid.shape
    nbrs = nbr.shape[0]
    fields = wout_in.shape[0]
    ext = rows + 2 * HALO
    tiles = width // CW
    flat = members * rows
    place = Place()
    wire = Wire(send_sem, recv_sem)

    barrier = pltpu.get_barrier_semaphore()
    for partner in place.partners:
        pl.semaphore_signal(barrier, inc=1, device_id=partner, device_id_type=MESH)
    loads = [pltpu.make_async_copy(src, dst, load_sem.at[i])
             for i, (src, dst) in enumerate(((wtgt_in, wtgt), (wsrc_in, wsrc), (wmix_in, wmix)))]
    for one in loads:
        one.start()

    def copies(src_up, src_down, dst, sems, m):
        return (
            pltpu.make_async_remote_copy(
                src_ref=src_up, dst_ref=dst.at[m, pl.ds(0, HALO)],
                send_sem=sems[0].at[0, m], recv_sem=sems[1].at[0, m],
                device_id=place.up, device_id_type=MESH),
            pltpu.make_async_remote_copy(
                src_ref=src_down, dst_ref=dst.at[m, pl.ds(HALO, HALO)],
                send_sem=sems[0].at[1, m], recv_sem=sems[1].at[1, m],
                device_id=place.down, device_id_type=MESH),
        )

    def halo_copies(m):
        return copies(lat.at[m, pl.ds(rows - HALO, HALO)], lat.at[m, pl.ds(0, HALO)], halo,
                      (halo_send, halo_recv), m)

    def rim_copies(m):
        return copies(dpe.at[m, pl.ds(HALO + rows, HALO)], dpe.at[m, pl.ds(0, HALO)], rims,
                      (rim_send, rim_recv), m)

    def y_copy(m):
        return pltpu.make_async_remote_copy(
            src_ref=ys.at[m], dst_ref=ys.at[members + m],
            send_sem=y_send.at[m], recv_sem=y_recv.at[m],
            device_id=place.mate, device_id_type=MESH)

    pl.semaphore_wait(barrier, len(place.partners))
    for m in range(members):
        for one in halo_copies(m):
            one.start()

    truth[...] = jnp.zeros_like(truth)
    truth[0:fields, :] = truth_in[...]
    truth[...] = truth[...].T
    area[...] = jnp.broadcast_to(area_in[...], (rows, FP)).T
    wout[...] = jnp.zeros_like(wout)
    wout[0:fields, :] = wout_in[...]

    code = jnp.where(mask[...] != 0, nbr[...], -1).astype(F32)
    code_t = jnp.concatenate([code, jnp.zeros((rows - nbrs, rows), F32)], axis=0).T
    lane = lax.broadcasted_iota(jnp.int32, (rows, ext), 1).astype(F32)
    sub = lax.broadcasted_iota(jnp.int32, (ext, rows), 0).astype(F32)
    count = jnp.zeros((rows, 1), F32)
    for k in range(nbrs):
        col = code_t[:, k:k + 1]
        on = jnp.where(col >= 0.0, 1.0, 0.0)
        one = (col == lane).astype(F32).astype(BF)
        one_t = (code[k:k + 1, :] == sub).astype(F32).astype(BF)
        pick[k] = one
        maskb[k] = jnp.broadcast_to(on, (rows, 128)).astype(BF)
        count = count + on
        pick_t[:, k * rows:(k + 1) * rows] = one_t
        if k == 0:
            hits[...] = one
            hits_t[...] = one_t
        else:
            hits[...] += one
            hits_t[...] += one_t

    def columns(step, first=0, last=tiles):
        def inner(c, _):
            step(pl.ds(pl.multiple_of(c * CW, CW), CW))
            return 0

        lax.fori_loop(first, last, inner, 0)

    def own_tgt(cols):
        got = (0.5 * dot(grid[...].reshape(flat, width), wtgt[:, cols]).astype(BF)).astype(BF)
        tgt[:, :, cols] = got.reshape(members, rows, CW)

    def own_src(cols):
        got = (0.5 * dot(lat[...].reshape(flat, width), wsrc[:, cols]).astype(BF)).astype(BF)
        proj[:, HALO:HALO + rows, cols] = got.reshape(members, rows, CW)

    loads[0].wait()
    columns(own_tgt)
    loads[1].wait()
    columns(own_src)

    def turn_grid(m, _):
        grid_x[:, pl.ds(pl.multiple_of(m * rows, rows), rows)] = grid[m].T
        return 0

    lax.fori_loop(0, members, turn_grid, 0)
    loads[2].wait()

    gb = 16

    def forward(m, _):
        for one in halo_copies(m):
            one.wait()
        edge = (0.5 * dot(halo[m], wsrc[...]).astype(BF)).astype(BF)
        proj[m, 0:HALO] = edge[0:HALO]
        proj[m, HALO + rows:ext] = edge[HALO:2 * HALO]

        def column(cols):
            table = proj[m, :, cols]
            linear = dot(hits[...], table) + count * tgt[m, :, cols].astype(F32)
            for at in range(0, rows, gb):
                got = dot(pick[:, at:at + gb, :].reshape(nbrs * gb, ext), table).astype(BF)
                got = got.reshape(nbrs, gb, CW)
                base = tgt[m, at:at + gb, cols]
                acc = None
                acc_s = None
                for k in range(nbrs):
                    on = maskb[k, at:at + gb, :]
                    u = got[k] + jnp.concatenate([on] * (CW // 128), axis=1) * base
                    t = jnp.tanh(u)
                    p = u * t
                    s = (t + u) - t * p
                    acc = p if k == 0 else acc + p
                    acc_s = s if k == 0 else acc_s + s
                    slope[m, k, at:at + gb, cols] = s
                agg[m, at:at + gb, cols] = (0.25 * (linear[at:at + gb] + acc.astype(F32))).astype(BF)
                slope_sum[m, at:at + gb, cols] = (acc_s.astype(F32) + count[at:at + gb]).astype(BF)

        columns(column)
        h = grid[m].astype(F32) + dot(agg[m], wmix[...])
        mean = jnp.sum(h, axis=1, keepdims=True) * (1.0 / width)
        centre = h - mean
        var = jnp.sum(centre * centre, axis=1, keepdims=True) * (1.0 / width)
        r = lax.rsqrt(var + EPS)
        inv[m] = jnp.broadcast_to(r, (rows, 128))
        normed[m] = (centre * r).astype(BF)
        ys[m] = dot_nt(normed[m], wout[...])
        y_copy(m).start()
        return 0

    lax.fori_loop(0, members, forward, 0)

    def turn(m, _):
        at = pl.ds(pl.multiple_of(m * rows, rows), rows)
        agg_x[:, at] = agg[m].T
        normed_x[:, at] = normed[m].T
        around = jnp.concatenate([halo[m, 0:HALO], lat[m], halo[m, HALO:2 * HALO]], axis=0)
        lat_x[:, pl.ds(pl.multiple_of(m * ext, ext), ext)] = around.T
        return 0

    lax.fori_loop(0, members, turn, 0)

    def y_wait(m, _):
        y_copy(m).wait()
        return 0

    lax.fori_loop(0, members, y_wait, 0)

    total = 2 * members

    def head(m, _):
        y = ys[m]
        miss = y - truth[...]
        pair = jnp.zeros_like(y)
        for o in range(total):
            diff = y - ys[o]
            pair = pair + diff * lax.rsqrt(diff * diff + SMOOTH)
        grad = miss * lax.rsqrt(miss * miss + SMOOTH) * (1.0 / total)
        dy = (area[...] * (grad - (FAIR / (total * (total - 1))) * pair)).astype(BF)
        dys[m] = dy
        dn = dot(dy, wout[...])
        nh = normed[m].astype(F32)
        m1 = jnp.sum(dn, axis=1, keepdims=True) * (1.0 / width)
        m2 = jnp.sum(dn * nh, axis=1, keepdims=True) * (1.0 / width)
        dh[m] = (inv[m][:, 0:1] * (dn - m1 - nh * m2)).astype(BF)
        return 0

    lax.fori_loop(0, members, head, 0)

    halves = []
    left = pl.ds(0, 512)
    at = 0
    for part, held in ((part_mix, held_mix), (part_tgt, held_tgt), (part_src, held_src)):
        wide = part.shape[-1]
        halves.append(Half(place, wire, part, held, left, True, bufs[at:at + 6], bufs[at + 6]))
        halves.append(Half(place, wire, part, held, pl.ds(512, wide - 512), False,
                           bufs[at + 7:at + 13], bufs[at + 13]))
        at += 14
    mix_l, mix_r, tgt_l, tgt_r, src_l, src_r = halves

    def product(turned, right):
        return dot(turned[...], right.reshape(-1, right.shape[-1])).astype(BF)

    def mix_grad(cols):
        put(part_mix, product(agg_x, dh[:, :, cols]), cols)

    columns(mix_grad, 0, 2)
    mix_l.start()
    columns(mix_grad, 2, 4)
    put(part_mix, product(normed_x, dys[...]), pl.ds(width, FP))
    mix_r.start()

    def mix_back(cols):
        dagg = (0.125 * dot_nt(dh[...].reshape(flat, width), wmix[cols, :])).astype(BF)
        dagg = dagg.reshape(members, rows, CW)
        tgt[:, :, cols] = dagg
        dq[:, :, cols] = dagg * slope_sum[:, :, cols]

    columns(mix_back)

    def tgt_grad(cols):
        put(part_tgt, product(grid_x, dq[:, :, cols]), cols)

    columns(tgt_grad, 0, 2)
    tgt_l.start()
    mix_l.s1()
    columns(tgt_grad, 2, 4)
    tgt_r.start()
    mix_r.s1()

    def spread(m):
        def column(cols):
            d = tgt[m, :, cols]
            edges = [slope[m, k, :, cols] * d for k in range(nbrs)]
            got = dot(pick_t[...], jnp.concatenate(edges, axis=0)) + dot(hits_t[...], d)
            dpe[m, :, cols] = got.astype(BF)

        columns(column)
        for one in rim_copies(m):
            one.start()

    spread(0)
    tgt_l.s1()
    mix_l.s2()
    mix_r.s2()
    tgt_r.s1()
    spread(1)
    mix_l.s3()
    mix_r.s3()
    spread(2)
    tgt_l.s2()
    tgt_r.s2()
    mix_l.s4()
    mix_r.s4()
    spread(3)
    tgt_l.s3()
    tgt_r.s3()
    mix_l.s5()
    mix_r.s5()

    def src_grad(cols):
        put(part_src, product(lat_x, dpe[:, :, cols]), cols)

    columns(src_grad, 0, 2)
    src_l.start()
    tgt_l.s4()
    tgt_r.s4()
    columns(src_grad, 2, 4)
    src_r.start()
    src_l.s1()

    def grid_back(cols):
        got = dot_nt(dq[...].reshape(flat, width), wtgt[cols, :]).reshape(members, rows, CW)
        d_grid[:, :, cols] = (dh[:, :, cols].astype(F32) + got).astype(BF)

    columns(grid_back, 0, 2)
    src_r.s1()
    tgt_l.s5()
    tgt_r.s5()
    columns(grid_back, 2, 4)
    src_l.s2()
    src_r.s2()
    o_mix[:, 0:512] = mix_l.s6(scale)
    last = mix_r.s6(scale)
    o_mix[:, 512:width] = last[:, 0:width - 512]
    o_out[...] = last[:, width - 512:width - 512 + fields]

    def sum_rims(m, _):
        for one in rim_copies(m):
            one.wait()
        dq[m] = (dpe[m, HALO:HALO + rows].astype(F32) + rims[m].astype(F32)).astype(BF)
        return 0

    lax.fori_loop(0, members, sum_rims, 0)

    def latent_back(cols):
        got = dot_nt(dq[...].reshape(flat, width), wsrc[cols, :]).reshape(members, rows, CW)
        d_latent[:, :, cols] = got.astype(BF)

    src_l.s3()
    src_r.s3()
    columns(latent_back, 0, 2)
    src_l.s4()
    src_r.s4()
    columns(latent_back, 2, 4)
    src_l.s5()
    src_r.s5()
    o_tgt[:, 0:512] = tgt_l.s6(scale)
    o_tgt[:, 512:width] = tgt_r.s6(scale)
    o_src[:, 0:512] = src_l.s6(scale)
    o_src[:, 512:width] = src_r.s6(scale)


def hand_over(arrays):
    count = len(arrays)

    def move(*refs):
        sems = refs[-1]
        moves = [pltpu.make_async_copy(refs[i], refs[count + i], sems.at[i]) for i in range(count)]
        for one in moves:
            one.start()
        for one in moves:
            one.wait()

    anywhere = pl.BlockSpec(memory_space=pl.ANY)
    return pl.pallas_call(
        move,
        out_shape=[jax.ShapeDtypeStruct(a.shape, a.dtype) for a in arrays],
        in_specs=[anywhere] * count,
        out_specs=[anywhere] * count,
        scratch_shapes=[pltpu.SemaphoreType.DMA((count,))],
    )(*arrays)


def on_device(latent, grid_in, w_src, w_tgt, w_mix, w_out, truth, area, nbr, mask):
    members, rows, width = grid_in.shape
    nbrs = nbr.shape[0]
    fields = w_out.shape[1]
    ext = rows + 2 * HALO
    tiles = lax.axis_size("grid")
    count = members * lax.axis_size("member")
    scale = 1.0 / math.sqrt(rows * tiles * count)

    def body_(*refs):
        body(scale, *refs)

    def ring_bufs(cols):
        return ([pltpu.VMEM((2, 2, 2, 16, cols), BF)] * 3 + [pltpu.VMEM((2, 16, cols), BF)] * 3
                + [pltpu.VMEM((3, 16, cols), BF)])

    vm = pl.BlockSpec(memory_space=pltpu.VMEM)
    hbm = pl.BlockSpec(memory_space=pl.ANY)
    sds = jax.ShapeDtypeStruct
    wide = width + FP
    halves = (512, wide - 512, 512, width - 512, 512, width - 512)
    ncopies = 19 * len(halves)
    results = pl.pallas_call(
        body_,
        out_shape=[
            sds((members, rows, width), BF),
            sds((members, rows, width), BF),
            sds((16, width), F32),
            sds((16, width), F32),
            sds((16, width), F32),
            sds((16, fields), F32),
        ],
        in_specs=[vm, vm, hbm, hbm, hbm, vm, vm, vm, vm, vm],
        out_specs=[vm] * 6,
        scratch_shapes=[
            pltpu.VMEM((width, width), BF),
            pltpu.VMEM((width, width), BF),
            pltpu.VMEM((width, width), BF),
            pltpu.VMEM((FP, width), BF),
            pltpu.VMEM((FP, rows), F32),
            pltpu.VMEM((rows, FP), F32),
            pltpu.VMEM((nbrs, rows, ext), BF),
            pltpu.VMEM((ext, nbrs * rows), BF),
            pltpu.VMEM((rows, ext), BF),
            pltpu.VMEM((ext, rows), BF),
            pltpu.VMEM((nbrs, rows, 128), BF),
            pltpu.VMEM((members, ext, width), BF),
            pltpu.VMEM((members, rows, width), BF),
            pltpu.VMEM((members, nbrs, rows, width), BF),
            pltpu.VMEM((members, rows, width), BF),
            pltpu.VMEM((members, rows, width), BF),
            pltpu.VMEM((members, rows, width), BF),
            pltpu.VMEM((members, rows, 128), F32),
            pltpu.VMEM((2 * members, rows, FP), F32),
            pltpu.VMEM((members, rows, FP), BF),
            pltpu.VMEM((members, rows, width), BF),
            pltpu.VMEM((members, rows, width), BF),
            pltpu.VMEM((members, ext, width), BF),
            pltpu.VMEM((width, members * rows), BF),
            pltpu.VMEM((width, members * rows), BF),
            pltpu.VMEM((width, members * rows), BF),
            pltpu.VMEM((width, members * ext), BF),
            pltpu.VMEM((members, 2 * HALO, width), BF),
            pltpu.VMEM((members, 2 * HALO, width), BF),
            pltpu.VMEM((NC, NY, NX, NZ, 16, width), BF),
            pltpu.VMEM((NC, NY, NX, NZ, 16, width), BF),
            pltpu.VMEM((NC, NY, NX, NZ, 16, wide), BF),
            pltpu.VMEM((NY, NX, NZ, 16, width), BF),
            pltpu.VMEM((NY, NX, NZ, 16, width), BF),
            pltpu.VMEM((NY, NX, NZ, 16, wide), BF),
            *[buf for cols in halves for buf in ring_bufs(cols)],
            pltpu.SemaphoreType.DMA((ncopies,)),
            pltpu.SemaphoreType.DMA((ncopies,)),
            pltpu.SemaphoreType.DMA((2, members)),
            pltpu.SemaphoreType.DMA((2, members)),
            pltpu.SemaphoreType.DMA((2, members)),
            pltpu.SemaphoreType.DMA((2, members)),
            pltpu.SemaphoreType.DMA((members,)),
            pltpu.SemaphoreType.DMA((members,)),
            pltpu.SemaphoreType.DMA((3,)),
        ],
        compiler_params=pltpu.CompilerParams(
            collective_id=0, has_side_effects=True, vmem_limit_bytes=63 * 2**20
        ),
        cost_estimate=pl.CostEstimate(flops=40 * 10**9, bytes_accessed=30 * 10**6, transcendentals=0),
    )(latent, grid_in, w_src, w_tgt, w_mix, w_out.T, truth, area.reshape(1, rows), nbr, mask)
    return hand_over(results)


def solution(mesh):
    in_specs = (
        P("member", "grid", None), P("member", "grid", None), P(), P(), P(), P(),
        P(None, "grid"), P("grid"), P(None, "grid"), P(None, "grid"),
    )
    out_specs = (
        P("member", "grid", None), P("member", "grid", None),
        P("grid", None), P("grid", None), P("grid", None), P("grid", None),
    )
    return jax.shard_map(
        on_device, mesh=mesh, in_specs=in_specs, out_specs=out_specs, check_vma=False
    )
```

```python
import math

import jax
import jax.numpy as jnp
from jax import lax
from jax.experimental import pallas as pl
from jax.experimental.pallas import tpu as pltpu
from jax.sharding import PartitionSpec as P

HALO = 64
SMOOTH = 0.0025
FAIR = 0.95
EPS = 1e-05
BF = jnp.bfloat16
F32 = jnp.float32
MESH = pl.DeviceIdType.MESH
CW = 512
NY, NX, NZ, NC = 4, 4, 2, 2
FP = 128


def dot(a, b):
    return lax.dot_general(a, b, (((1,), (0,)), ((), ())), preferred_element_type=F32)


def dot_nt(a, b):
    return lax.dot_general(a, b, (((1,), (1,)), ((), ())), preferred_element_type=F32)


def dot_tn(a, b):
    return lax.dot_general(a, b, (((0,), (0,)), ((), ())), preferred_element_type=F32)


class Place:
    def __init__(self):
        self.me = lax.axis_index("member")
        t = lax.axis_index("grid")
        tiles = NY * NX * NZ * NC
        self.y, self.x, self.z, self.c = t // 16, (t // 4) % 4, (t // 2) % 2, t % 2
        self.up = (self.me, (t + 1) % tiles)
        self.down = (self.me, (t + tiles - 1) % tiles)
        self.mate = (1 - self.me, t)
        self.core = self.at(c=1 - self.c)
        self.y_ring = (self.at(y=(self.y + 1) % 4), self.at(y=(self.y + 3) % 4))
        self.x_ring = (self.at(x=(self.x + 1) % 4), self.at(x=(self.x + 3) % 4))
        self.z_far = (self.me, self.at(z=1 - self.z)[1])
        self.z_both = (1 - self.me, self.z_far[1])
        self.partners = (self.up, self.down, self.core, *self.y_ring, *self.x_ring,
                         self.mate, self.z_far, self.z_both)

    def at(self, y=None, x=None, z=None, c=None):
        y = self.y if y is None else y
        x = self.x if x is None else x
        z = self.z if z is None else z
        c = self.c if c is None else c
        return (self.me, y * 16 + x * 4 + z * 2 + c)


class Wire:
    def __init__(self, send, recv):
        self.send, self.recv, self.used = send, recv, 0

    def copy(self, src, dst, device):
        at = self.used
        self.used += 1
        return pltpu.make_async_remote_copy(
            src_ref=src, dst_ref=dst, send_sem=self.send.at[at], recv_sem=self.recv.at[at],
            device_id=device, device_id_type=MESH)


def add_into(dst, *others):
    total = dst[...].astype(F32)
    for o in others:
        total = total + o[...].astype(F32)
    dst[...] = total.astype(BF)


class Ring:
    def __init__(self, wire, p, ring, block, a, b, d):
        self.wire, self.p, self.ring, self.block = wire, p, ring, block
        self.a, self.b, self.d = a, b, d
        self.nxt, self.prv = (p + 1) % 4, (p + 3) % 4

    def start(self):
        w, (plus, minus), block = self.wire, self.ring, self.block
        opp = (self.p + 2) % 4
        self.first = [w.copy(block(opp, 0), self.a.at[0], plus),
                      w.copy(block(opp, 1), self.a.at[1], minus)]
        self.second = [w.copy(block(self.nxt, 1), self.b.at[0], plus),
                       w.copy(block(self.prv, 0), self.b.at[1], minus)]
        for one in self.first + self.second:
            one.start()

    def middle(self):
        w, (plus, minus), block = self.wire, self.ring, self.block
        self.third = [w.copy(block(self.nxt, 0), self.d.at[0], plus),
                      w.copy(block(self.prv, 1), self.d.at[1], minus)]
        self.first[0].wait()
        add_into(block(self.nxt, 0), self.a.at[0])
        self.third[0].start()
        self.first[1].wait()
        add_into(block(self.prv, 1), self.a.at[1])
        self.third[1].start()

    def finish(self):
        for one in self.second + self.third:
            one.wait()
        add_into(self.block(self.p, 0), self.b.at[1], self.d.at[0])
        add_into(self.block(self.p, 1), self.b.at[0], self.d.at[1])


class Half:
    def __init__(self, place, wire, part, cols, y_first, cross_first, bufs):
        self.place, self.wire, self.cols, self.part = place, wire, cols, part
        self.cross_first = cross_first
        self.held, self.zbuf = bufs[6:]
        y, x, c = place.y, place.x, place.c
        cc = c if cross_first else slice(None)

        def wide_y(d, h):
            return part.at[d, pl.ds(2 * h, 2), :, cc, :, cols]

        def wide_x(d, h):
            return part.at[pl.ds(2 * h, 2), d, :, cc, :, cols]

        def thin_x(d, h):
            return part.at[y, d, h, cc, :, cols]

        def thin_y(d, h):
            return part.at[d, x, h, cc, :, cols]

        on_y, on_x = (y, place.y_ring), (x, place.x_ring)
        if y_first:
            self.one = Ring(wire, *on_y, wide_y, *bufs[:3])
            self.two = Ring(wire, *on_x, thin_x, *bufs[3:6])
        else:
            self.one = Ring(wire, *on_x, wide_x, *bufs[:3])
            self.two = Ring(wire, *on_y, thin_y, *bufs[3:6])

    def start(self):
        if not self.cross_first:
            self.one.start()
            return
        self.cross = self.wire.copy(self.part.at[:, :, :, 1 - self.place.c, :, self.cols], self.held,
                                    self.place.core)
        self.cross.start()

    def s1(self):
        if not self.cross_first:
            return
        self.cross.wait()

        def add(yy, _):
            add_into(self.part.at[yy, :, :, self.place.c, :, self.cols], self.held.at[yy])
            return 0

        lax.fori_loop(0, NY, add, 0)
        self.one.start()

    def s2(self):
        self.one.middle()

    def s3(self):
        self.one.finish()
        self.two.start()

    def s4(self):
        self.two.middle()

    def s5(self):
        self.two.finish()
        p = self.place
        if self.cross_first:
            self.to_z()
            return
        mine = self.part.at[p.y, p.x]
        self.cross = self.wire.copy(mine.at[:, 1 - p.c, :, self.cols], self.held, p.core)
        self.cross.start()

    def s6(self):
        if self.cross_first:
            return
        p = self.place
        self.cross.wait()
        add_into(self.part.at[p.y, p.x, :, p.c, :, self.cols], self.held)
        self.to_z()

    def to_z(self):
        p = self.place
        mine, far = self.part.at[p.y, p.x, p.z, p.c], self.part.at[p.y, p.x, 1 - p.z, p.c]
        self.last = [self.wire.copy(mine.at[:, self.cols], self.zbuf.at[0], p.mate),
                     self.wire.copy(far.at[:, self.cols], self.zbuf.at[1], p.z_far),
                     self.wire.copy(far.at[:, self.cols], self.zbuf.at[2], p.z_both)]
        for one in self.last:
            one.start()

    def s7(self, scale):
        p = self.place
        for one in self.last:
            one.wait()
        total = self.part[p.y, p.x, p.z, p.c, :, self.cols].astype(F32)
        for k in range(3):
            total = total + self.zbuf[k].astype(F32)
        return total * scale


def put(part, block, cols):
    for b in range(NY * NX * NZ * NC):
        part[b // 16, (b // 4) % 4, (b // 2) % 2, b % 2, :, cols] = block[b * 16:(b + 1) * 16]


def body(scale, lat, grid, wsrc_in, wtgt_in, wmix_in, wout_in, truth_in, area_in, nbr, mask,
         d_latent, d_grid, o_src, o_tgt, o_mix, o_out,
         wsrc, wtgt, wmix, wout, truth, area,
         pick, pick_t, hits, hits_t, maskb, proj, tgt, slope, slope_sum, agg, normed, inv, ys, dys, dh, dq, dpe,
         agg_x, normed_x, grid_x, lat_x,
         halo, rims, part_src, part_tgt, part_mix, *rest):
    send_sem, recv_sem, halo_send, halo_recv, rim_send, rim_recv, y_send, y_recv, load_sem = rest[-9:]
    bufs = rest[:-9]
    members, rows, width = grid.shape
    nbrs = nbr.shape[0]
    fields = wout_in.shape[0]
    ext = rows + 2 * HALO
    tiles = width // CW
    flat = members * rows
    place = Place()
    wire = Wire(send_sem, recv_sem)

    barrier = pltpu.get_barrier_semaphore()
    for partner in place.partners:
        pl.semaphore_signal(barrier, inc=1, device_id=partner, device_id_type=MESH)
    loads = [pltpu.make_async_copy(src, dst, load_sem.at[i])
             for i, (src, dst) in enumerate(((wtgt_in, wtgt), (wsrc_in, wsrc), (wmix_in, wmix)))]
    for one in loads:
        one.start()

    def copies(src_up, src_down, dst, sems, m):
        return (
            pltpu.make_async_remote_copy(
                src_ref=src_up, dst_ref=dst.at[m, pl.ds(0, HALO)],
                send_sem=sems[0].at[0, m], recv_sem=sems[1].at[0, m],
                device_id=place.up, device_id_type=MESH),
            pltpu.make_async_remote_copy(
                src_ref=src_down, dst_ref=dst.at[m, pl.ds(HALO, HALO)],
                send_sem=sems[0].at[1, m], recv_sem=sems[1].at[1, m],
                device_id=place.down, device_id_type=MESH),
        )

    def halo_copies(m):
        return copies(lat.at[m, pl.ds(rows - HALO, HALO)], lat.at[m, pl.ds(0, HALO)], halo,
                      (halo_send, halo_recv), m)

    def rim_copies(m):
        return copies(dpe.at[m, pl.ds(HALO + rows, HALO)], dpe.at[m, pl.ds(0, HALO)], rims,
                      (rim_send, rim_recv), m)

    def y_copy(m):
        return pltpu.make_async_remote_copy(
            src_ref=ys.at[m], dst_ref=ys.at[members + m],
            send_sem=y_send.at[m], recv_sem=y_recv.at[m],
            device_id=place.mate, device_id_type=MESH)

    pl.semaphore_wait(barrier, len(place.partners))
    for m in range(members):
        for one in halo_copies(m):
            one.start()

    truth[...] = jnp.zeros_like(truth)
    truth[0:fields, :] = truth_in[...]
    truth[...] = truth[...].T
    area[...] = jnp.broadcast_to(area_in[...], (rows, FP)).T
    wout[...] = jnp.zeros_like(wout)
    wout[0:fields, :] = wout_in[...]

    code = jnp.where(mask[...] != 0, nbr[...], -1).astype(F32)
    code_t = jnp.concatenate([code, jnp.zeros((rows - nbrs, rows), F32)], axis=0).T
    lane = lax.broadcasted_iota(jnp.int32, (rows, ext), 1).astype(F32)
    sub = lax.broadcasted_iota(jnp.int32, (ext, rows), 0).astype(F32)
    count = jnp.zeros((rows, 1), F32)
    for k in range(nbrs):
        col = code_t[:, k:k + 1]
        on = jnp.where(col >= 0.0, 1.0, 0.0)
        one = (col == lane).astype(F32).astype(BF)
        one_t = (code[k:k + 1, :] == sub).astype(F32).astype(BF)
        pick[k] = one
        maskb[k] = jnp.broadcast_to(on, (rows, 128)).astype(BF)
        count = count + on
        pick_t[:, k * rows:(k + 1) * rows] = one_t
        if k == 0:
            hits[...] = one
            hits_t[...] = one_t
        else:
            hits[...] += one
            hits_t[...] += one_t

    def columns(step, first=0, last=tiles):
        def inner(c, _):
            step(pl.ds(pl.multiple_of(c * CW, CW), CW))
            return 0

        lax.fori_loop(first, last, inner, 0)

    def own_tgt(cols):
        got = (0.5 * dot(grid[...].reshape(flat, width), wtgt[:, cols]).astype(BF)).astype(BF)
        tgt[:, :, cols] = got.reshape(members, rows, CW)

    def own_src(cols):
        got = (0.5 * dot(lat[...].reshape(flat, width), wsrc[:, cols]).astype(BF)).astype(BF)
        proj[:, HALO:HALO + rows, cols] = got.reshape(members, rows, CW)

    loads[0].wait()
    columns(own_tgt)
    loads[1].wait()
    columns(own_src)

    def turn_grid(m, _):
        grid_x[:, pl.ds(pl.multiple_of(m * rows, rows), rows)] = grid[m].T
        return 0

    lax.fori_loop(0, members, turn_grid, 0)
    loads[2].wait()

    gb = 32

    def forward(m, _):
        for one in halo_copies(m):
            one.wait()
        edge = (0.5 * dot(halo[m], wsrc[...]).astype(BF)).astype(BF)
        proj[m, 0:HALO] = edge[0:HALO]
        proj[m, HALO + rows:ext] = edge[HALO:2 * HALO]

        linear = dot(hits[...], proj[m]) + count * tgt[m].astype(F32)
        for at in range(0, rows, gb):
            got = dot(pick[:, at:at + gb, :].reshape(nbrs * gb, ext), proj[m]).astype(BF)
            got = got.reshape(nbrs, gb, width)
            for c in range(0, width, 256):
                cols = slice(c, c + 256)
                base = tgt[m, at:at + gb, cols]
                acc = None
                acc_s = None
                for k in range(nbrs):
                    on = maskb[k, at:at + gb, :]
                    u = got[k, :, cols] + jnp.concatenate([on, on], axis=1) * base
                    t = jnp.tanh(u)
                    p = u * t
                    s = (t + u) - t * p
                    acc = p if k == 0 else acc + p
                    acc_s = s if k == 0 else acc_s + s
                    slope[m, k, at:at + gb, cols] = s
                total = linear[at:at + gb, cols] + acc.astype(F32)
                agg[m, at:at + gb, cols] = (0.25 * total).astype(BF)
                slope_sum[m, at:at + gb, cols] = (acc_s.astype(F32) + count[at:at + gb]).astype(BF)

        h = grid[m].astype(F32) + dot(agg[m], wmix[...])
        mean = jnp.sum(h, axis=1, keepdims=True) * (1.0 / width)
        centre = h - mean
        var = jnp.sum(centre * centre, axis=1, keepdims=True) * (1.0 / width)
        r = lax.rsqrt(var + EPS)
        inv[m] = jnp.broadcast_to(r, (rows, 128))
        normed[m] = (centre * r).astype(BF)
        ys[m] = dot_nt(normed[m], wout[...])
        y_copy(m).start()
        return 0

    lax.fori_loop(0, members, forward, 0)

    def turn(m, _):
        at = pl.ds(pl.multiple_of(m * rows, rows), rows)
        agg_x[:, at] = agg[m].T
        normed_x[:, at] = normed[m].T
        around = jnp.concatenate([halo[m, 0:HALO], lat[m], halo[m, HALO:2 * HALO]], axis=0)
        lat_x[:, pl.ds(pl.multiple_of(m * ext, ext), ext)] = around.T
        return 0

    lax.fori_loop(0, members, turn, 0)

    def y_wait(m, _):
        y_copy(m).wait()
        return 0

    lax.fori_loop(0, members, y_wait, 0)

    total = 2 * members

    def head(m, _):
        y = ys[m]
        miss = y - truth[...]
        pair = jnp.zeros_like(y)
        for o in range(total):
            diff = y - ys[o]
            pair = pair + diff * lax.rsqrt(diff * diff + SMOOTH)
        grad = miss * lax.rsqrt(miss * miss + SMOOTH) * (1.0 / total)
        dy = (area[...] * (grad - (FAIR / (total * (total - 1))) * pair)).astype(BF)
        dys[m] = dy
        dn = dot(dy, wout[...])
        nh = normed[m].astype(F32)
        m1 = jnp.sum(dn, axis=1, keepdims=True) * (1.0 / width)
        m2 = jnp.sum(dn * nh, axis=1, keepdims=True) * (1.0 / width)
        dh[m] = (inv[m][:, 0:1] * (dn - m1 - nh * m2)).astype(BF)
        return 0

    lax.fori_loop(0, members, head, 0)

    halves = []
    left = pl.ds(0, 512)
    for i, part in enumerate((part_mix, part_tgt, part_src)):
        wide = part.shape[-1]
        at = 16 * i
        halves.append(Half(place, wire, part, left, i != 1, True, bufs[at:at + 8]))
        halves.append(Half(place, wire, part, pl.ds(512, wide - 512), i == 1, False, bufs[at + 8:at + 16]))
    mix_l, mix_r, tgt_l, tgt_r, src_l, src_r = halves

    def product(turned, right):
        return dot(turned[...], right.reshape(-1, right.shape[-1])).astype(BF)

    def mix_grad(cols):
        put(part_mix, product(agg_x, dh[:, :, cols]), cols)

    columns(mix_grad, 1, 2)
    put(part_mix, product(normed_x, dys[...]), pl.ds(width, FP))
    mix_r.start()
    columns(mix_grad, 0, 1)
    mix_l.start()

    def mix_back(cols):
        dagg = (0.125 * dot_nt(dh[...].reshape(flat, width), wmix[cols, :])).astype(BF)
        dagg = dagg.reshape(members, rows, CW)
        tgt[:, :, cols] = dagg
        dq[:, :, cols] = dagg * slope_sum[:, :, cols]

    columns(mix_back)

    def tgt_grad(cols):
        put(part_tgt, product(grid_x, dq[:, :, cols]), cols)

    columns(tgt_grad, 1, 2)
    tgt_r.start()
    columns(tgt_grad, 0, 1)
    tgt_l.start()
    mix_l.s1()

    def spread(m):
        def column(cols):
            d = tgt[m, :, cols]
            for k in range(nbrs):
                slope[m, k, :, cols] = slope[m, k, :, cols] * d
            edges = slope[m, :, :, cols].reshape(nbrs * rows, CW)
            got = dot(pick_t[...], edges) + dot(hits_t[...], d)
            dpe[m, :, cols] = got.astype(BF)

        columns(column)
        for one in rim_copies(m):
            one.start()

    spread(0)
    mix_r.s2()
    tgt_l.s1()
    spread(1)
    mix_l.s2()
    mix_r.s3()
    tgt_r.s2()
    spread(2)
    mix_l.s3()
    mix_r.s4()
    tgt_l.s2()
    spread(3)
    mix_l.s4()
    mix_r.s5()
    tgt_r.s3()
    tgt_l.s3()

    def src_grad(cols):
        put(part_src, product(lat_x, dpe[:, :, cols]), cols)

    columns(src_grad, 1, 2)
    src_r.start()
    mix_l.s5()
    mix_r.s6()
    tgt_l.s4()
    tgt_r.s4()
    columns(src_grad, 0, 1)
    src_l.start()
    tgt_l.s5()
    tgt_r.s5()

    def grid_back(cols):
        got = dot_nt(dq[...].reshape(flat, width), wtgt[cols, :]).reshape(members, rows, CW)
        d_grid[:, :, cols] = (dh[:, :, cols].astype(F32) + got).astype(BF)

    columns(grid_back, 0, 1)
    src_l.s1()
    tgt_r.s6()
    columns(grid_back, 1, 2)
    src_r.s2()
    src_l.s2()
    o_mix[:, 0:512] = mix_l.s7(scale)
    last = mix_r.s7(scale)
    o_mix[:, 512:width] = last[:, 0:width - 512]
    o_out[...] = last[:, width - 512:width - 512 + fields]

    def sum_rims(m, _):
        for one in rim_copies(m):
            one.wait()
        dq[m] = (dpe[m, HALO:HALO + rows].astype(F32) + rims[m].astype(F32)).astype(BF)
        return 0

    lax.fori_loop(0, members, sum_rims, 0)

    def latent_back(cols):
        got = dot_nt(dq[...].reshape(flat, width), wsrc[cols, :]).reshape(members, rows, CW)
        d_latent[:, :, cols] = got.astype(BF)

    columns(latent_back, 0, 1)
    src_l.s3()
    src_r.s3()
    columns(latent_back, 1, 2)
    src_l.s4()
    src_r.s4()
    src_l.s5()
    src_r.s5()
    src_r.s6()
    o_tgt[:, 0:512] = tgt_l.s7(scale)
    o_tgt[:, 512:width] = tgt_r.s7(scale)
    o_src[:, 0:512] = src_l.s7(scale)
    o_src[:, 512:width] = src_r.s7(scale)


def hand_over(arrays):
    count = len(arrays)

    def move(*refs):
        sems = refs[-1]
        moves = [pltpu.make_async_copy(refs[i], refs[count + i], sems.at[i]) for i in range(count)]
        for one in moves:
            one.start()
        for one in moves:
            one.wait()

    anywhere = pl.BlockSpec(memory_space=pl.ANY)
    return pl.pallas_call(
        move,
        out_shape=[jax.ShapeDtypeStruct(a.shape, a.dtype) for a in arrays],
        in_specs=[pl.BlockSpec(memory_space=pltpu.VMEM)] * count,
        out_specs=[anywhere] * count,
        scratch_shapes=[pltpu.SemaphoreType.DMA((count,))],
    )(*arrays)


def on_device(latent, grid_in, w_src, w_tgt, w_mix, w_out, truth, area, nbr, mask):
    members, rows, width = grid_in.shape
    nbrs = nbr.shape[0]
    fields = w_out.shape[1]
    ext = rows + 2 * HALO
    tiles = lax.axis_size("grid")
    count = members * lax.axis_size("member")
    scale = 1.0 / math.sqrt(rows * tiles * count)

    def body_(*refs):
        body(scale, *refs)

    def half_bufs(cols, cross_first):
        both = () if cross_first else (NC,)
        held = (NY, NX, NZ, 16, cols) if cross_first else (NZ, 16, cols)
        return ([pltpu.VMEM((2, 2, 2, *both, 16, cols), BF)] * 3 + [pltpu.VMEM((2, *both, 16, cols), BF)] * 3
                + [pltpu.VMEM(held, BF), pltpu.VMEM((3, 16, cols), BF)])

    vm = pl.BlockSpec(memory_space=pltpu.VMEM)
    hbm = pl.BlockSpec(memory_space=pl.ANY)
    sds = jax.ShapeDtypeStruct
    wide = width + FP
    halves = (512, wide - 512, 512, width - 512, 512, width - 512)
    ncopies = 16 * len(halves)
    results = pl.pallas_call(
        body_,
        out_shape=[
            sds((members, rows, width), BF),
            sds((members, rows, width), BF),
            sds((16, width), F32),
            sds((16, width), F32),
            sds((16, width), F32),
            sds((16, fields), F32),
        ],
        in_specs=[vm, vm, hbm, hbm, hbm, vm, vm, vm, vm, vm],
        out_specs=[vm] * 6,
        scratch_shapes=[
            pltpu.VMEM((width, width), BF),
            pltpu.VMEM((width, width), BF),
            pltpu.VMEM((width, width), BF),
            pltpu.VMEM((FP, width), BF),
            pltpu.VMEM((FP, rows), F32),
            pltpu.VMEM((rows, FP), F32),
            pltpu.VMEM((nbrs, rows, ext), BF),
            pltpu.VMEM((ext, nbrs * rows), BF),
            pltpu.VMEM((rows, ext), BF),
            pltpu.VMEM((ext, rows), BF),
            pltpu.VMEM((nbrs, rows, 128), BF),
            pltpu.VMEM((members, ext, width), BF),
            pltpu.VMEM((members, rows, width), BF),
            pltpu.VMEM((members, nbrs, rows, width), BF),
            pltpu.VMEM((members, rows, width), BF),
            pltpu.VMEM((members, rows, width), BF),
            pltpu.VMEM((members, rows, width), BF),
            pltpu.VMEM((members, rows, 128), F32),
            pltpu.VMEM((2 * members, rows, FP), F32),
            pltpu.VMEM((members, rows, FP), BF),
            pltpu.VMEM((members, rows, width), BF),
            pltpu.VMEM((members, rows, width), BF),
            pltpu.VMEM((members, ext, width), BF),
            pltpu.VMEM((width, members * rows), BF),
            pltpu.VMEM((width, members * rows), BF),
            pltpu.VMEM((width, members * rows), BF),
            pltpu.VMEM((width, members * ext), BF),
            pltpu.VMEM((members, 2 * HALO, width), BF),
            pltpu.VMEM((members, 2 * HALO, width), BF),
            pltpu.VMEM((NY, NX, NZ, NC, 16, width), BF),
            pltpu.VMEM((NY, NX, NZ, NC, 16, width), BF),
            pltpu.VMEM((NY, NX, NZ, NC, 16, wide), BF),
            *[buf for i, cols in enumerate(halves) for buf in half_bufs(cols, i % 2 == 0)],
            pltpu.SemaphoreType.DMA((ncopies,)),
            pltpu.SemaphoreType.DMA((ncopies,)),
            pltpu.SemaphoreType.DMA((2, members)),
            pltpu.SemaphoreType.DMA((2, members)),
            pltpu.SemaphoreType.DMA((2, members)),
            pltpu.SemaphoreType.DMA((2, members)),
            pltpu.SemaphoreType.DMA((members,)),
            pltpu.SemaphoreType.DMA((members,)),
            pltpu.SemaphoreType.DMA((3,)),
        ],
        compiler_params=pltpu.CompilerParams(
            collective_id=0, has_side_effects=True, vmem_limit_bytes=63 * 2**20
        ),
        cost_estimate=pl.CostEstimate(flops=40 * 10**9, bytes_accessed=30 * 10**6, transcendentals=0),
    )(latent, grid_in, w_src, w_tgt, w_mix, w_out.T, truth, area.reshape(1, rows), nbr, mask)
    return hand_over(results)


def solution(mesh):
    in_specs = (
        P("member", "grid", None), P("member", "grid", None), P(), P(), P(), P(),
        P(None, "grid"), P("grid"), P(None, "grid"), P(None, "grid"),
    )
    out_specs = (
        P("member", "grid", None), P("member", "grid", None),
        P("grid", None), P("grid", None), P("grid", None), P("grid", None),
    )
    return jax.shard_map(
        on_device, mesh=mesh, in_specs=in_specs, out_specs=out_specs, check_vma=False
    )
```

```python
import math

import jax
import jax.numpy as jnp
from jax import lax
from jax.experimental import pallas as pl
from jax.experimental.pallas import tpu as pltpu
from jax.sharding import PartitionSpec as P

HALO = 64
SMOOTH = 0.0025
FAIR = 0.95
EPS = 1e-05
BF = jnp.bfloat16
F32 = jnp.float32
MESH = pl.DeviceIdType.MESH
CW = 512
NY, NX, NZ, NC = 4, 4, 2, 2
FP = 128


def dot(a, b):
    return lax.dot_general(a, b, (((1,), (0,)), ((), ())), preferred_element_type=F32)


def dot_nt(a, b):
    return lax.dot_general(a, b, (((1,), (1,)), ((), ())), preferred_element_type=F32)


def dot_tn(a, b):
    return lax.dot_general(a, b, (((0,), (0,)), ((), ())), preferred_element_type=F32)


class Place:
    def __init__(self):
        self.me = lax.axis_index("member")
        t = lax.axis_index("grid")
        tiles = NY * NX * NZ * NC
        self.y, self.x, self.z, self.c = t // 16, (t // 4) % 4, (t // 2) % 2, t % 2
        self.up = (self.me, (t + 1) % tiles)
        self.down = (self.me, (t + tiles - 1) % tiles)
        self.mate = (1 - self.me, t)
        self.core = self.at(c=1 - self.c)
        self.y_ring = tuple(self.at(y=(self.y + k) % 4) for k in (1, 2, 3))
        self.x_ring = tuple(self.at(x=(self.x + k) % 4) for k in (1, 2, 3))
        self.z_far = (self.me, self.at(z=1 - self.z)[1])
        self.z_both = (1 - self.me, self.z_far[1])
        self.partners = (self.up, self.down, self.core, *self.y_ring, *self.x_ring,
                         self.mate, self.z_far, self.z_both)

    def at(self, y=None, x=None, z=None, c=None):
        y = self.y if y is None else y
        x = self.x if x is None else x
        z = self.z if z is None else z
        c = self.c if c is None else c
        return (self.me, y * 16 + x * 4 + z * 2 + c)


class Wire:
    def __init__(self, send, recv):
        self.send, self.recv, self.used = send, recv, 0

    def copy(self, src, dst, device):
        at = self.used
        self.used += 1
        return pltpu.make_async_remote_copy(
            src_ref=src, dst_ref=dst, send_sem=self.send.at[at], recv_sem=self.recv.at[at],
            device_id=device, device_id_type=MESH)


def add_into(dst, *others):
    total = dst[...].astype(F32)
    for o in others:
        total = total + o[...].astype(F32)
    dst[...] = total.astype(BF)


class Swap:
    def __init__(self, wire, p, others, block, buf):
        self.wire, self.p, self.others, self.block, self.buf = wire, p, others, block, buf

    def start(self):
        self.moves = [self.wire.copy(self.block((self.p + k) % 4), self.buf.at[k - 1], self.others[k - 1])
                      for k in (1, 3, 2)]
        for one in self.moves:
            one.start()

    def finish(self):
        for one in self.moves:
            one.wait()
        add_into(self.block(self.p), *[self.buf.at[k] for k in range(3)])


class Half:
    def __init__(self, place, wire, part, held, cols, y_first, bufs, zbuf):
        self.place, self.wire, self.zbuf, self.cols = place, wire, zbuf, cols
        self.part, self.held = part, held
        y, x = place.y, place.x

        on_y, on_x = (y, place.y_ring), (x, place.x_ring)
        if y_first:
            self.one = Swap(wire, *on_y, lambda d: held.at[d, :, :, :, cols], bufs[0])
            self.two = Swap(wire, *on_x, lambda d: held.at[y, d, :, :, cols], bufs[1])
        else:
            self.one = Swap(wire, *on_x, lambda d: held.at[:, d, :, :, cols], bufs[0])
            self.two = Swap(wire, *on_y, lambda d: held.at[d, x, :, :, cols], bufs[1])

    def start(self):
        cols = self.cols
        self.cross = self.wire.copy(self.part.at[1 - self.place.c, :, :, :, :, cols],
                                    self.held.at[:, :, :, :, cols], self.place.core)
        self.cross.start()

    def s1(self):
        self.cross.wait()
        cols = self.cols

        def add(yy, _):
            add_into(self.held.at[yy, :, :, :, cols], self.part.at[self.place.c, yy, :, :, :, cols])
            return 0

        lax.fori_loop(0, NY, add, 0)
        self.one.start()

    def s2(self):
        self.one.finish()
        self.two.start()

    def s3(self):
        self.two.finish()
        p = self.place
        mine = self.held.at[p.y, p.x]
        self.last = [self.wire.copy(mine.at[p.z, :, self.cols], self.zbuf.at[0], p.mate),
                     self.wire.copy(mine.at[1 - p.z, :, self.cols], self.zbuf.at[1], p.z_far),
                     self.wire.copy(mine.at[1 - p.z, :, self.cols], self.zbuf.at[2], p.z_both)]
        for one in self.last:
            one.start()

    def s4(self, scale):
        p = self.place
        for one in self.last:
            one.wait()
        total = self.held[p.y, p.x, p.z, :, self.cols].astype(F32)
        for k in range(3):
            total = total + self.zbuf[k].astype(F32)
        return total * scale


def put(part, block, cols):
    for b in range(NY * NX * NZ * NC):
        part[b % 2, b // 16, (b // 4) % 4, (b // 2) % 2, :, cols] = block[b * 16:(b + 1) * 16]


def body(scale, lat, grid, wsrc_in, wtgt_in, wmix_in, wout_in, truth_in, area_in, nbr, mask,
         d_latent, d_grid, o_src, o_tgt, o_mix, o_out,
         wsrc, wtgt, wmix, wout, truth, area,
         pick, pick_t, hits, hits_t, maskb, proj, tgt, slope, slope_sum, agg, normed, inv, ys, dys, dh, dq, dpe,
         agg_x, normed_x, grid_x, lat_x,
         halo, rims, part_src, part_tgt, part_mix, held_src, held_tgt, held_mix, *rest):
    send_sem, recv_sem, halo_send, halo_recv, rim_send, rim_recv, y_send, y_recv, load_sem = rest[-9:]
    bufs = rest[:-9]
    members, rows, width = grid.shape
    nbrs = nbr.shape[0]
    fields = wout_in.shape[0]
    ext = rows + 2 * HALO
    tiles = width // CW
    flat = members * rows
    place = Place()
    wire = Wire(send_sem, recv_sem)

    barrier = pltpu.get_barrier_semaphore()
    for partner in place.partners:
        pl.semaphore_signal(barrier, inc=1, device_id=partner, device_id_type=MESH)
    loads = [pltpu.make_async_copy(src, dst, load_sem.at[i])
             for i, (src, dst) in enumerate(((wtgt_in, wtgt), (wsrc_in, wsrc), (wmix_in, wmix)))]
    for one in loads:
        one.start()

    def copies(src_up, src_down, dst, sems, m):
        return (
            pltpu.make_async_remote_copy(
                src_ref=src_up, dst_ref=dst.at[m, pl.ds(0, HALO)],
                send_sem=sems[0].at[0, m], recv_sem=sems[1].at[0, m],
                device_id=place.up, device_id_type=MESH),
            pltpu.make_async_remote_copy(
                src_ref=src_down, dst_ref=dst.at[m, pl.ds(HALO, HALO)],
                send_sem=sems[0].at[1, m], recv_sem=sems[1].at[1, m],
                device_id=place.down, device_id_type=MESH),
        )

    def halo_copies(m):
        return copies(lat.at[m, pl.ds(rows - HALO, HALO)], lat.at[m, pl.ds(0, HALO)], halo,
                      (halo_send, halo_recv), m)

    def rim_copies(m):
        return copies(dpe.at[m, pl.ds(HALO + rows, HALO)], dpe.at[m, pl.ds(0, HALO)], rims,
                      (rim_send, rim_recv), m)

    def y_copy(m):
        return pltpu.make_async_remote_copy(
            src_ref=ys.at[m], dst_ref=ys.at[members + m],
            send_sem=y_send.at[m], recv_sem=y_recv.at[m],
            device_id=place.mate, device_id_type=MESH)

    pl.semaphore_wait(barrier, len(place.partners))
    for m in range(members):
        for one in halo_copies(m):
            one.start()

    truth[...] = jnp.zeros_like(truth)
    truth[0:fields, :] = truth_in[...]
    truth[...] = truth[...].T
    area[...] = jnp.broadcast_to(area_in[...], (rows, FP)).T
    wout[...] = jnp.zeros_like(wout)
    wout[0:fields, :] = wout_in[...]

    code = jnp.where(mask[...] != 0, nbr[...], -1).astype(F32)
    code_t = jnp.concatenate([code, jnp.zeros((rows - nbrs, rows), F32)], axis=0).T
    lane = lax.broadcasted_iota(jnp.int32, (rows, ext), 1).astype(F32)
    sub = lax.broadcasted_iota(jnp.int32, (ext, rows), 0).astype(F32)
    count = jnp.zeros((rows, 1), F32)
    for k in range(nbrs):
        col = code_t[:, k:k + 1]
        on = jnp.where(col >= 0.0, 1.0, 0.0)
        one = (col == lane).astype(F32).astype(BF)
        one_t = (code[k:k + 1, :] == sub).astype(F32).astype(BF)
        pick[k] = one
        maskb[k] = jnp.broadcast_to(on, (rows, 128)).astype(BF)
        count = count + on
        pick_t[:, k * rows:(k + 1) * rows] = one_t
        if k == 0:
            hits[...] = one
            hits_t[...] = one_t
        else:
            hits[...] += one
            hits_t[...] += one_t

    def columns(step, first=0, last=tiles):
        def inner(c, _):
            step(pl.ds(pl.multiple_of(c * CW, CW), CW))
            return 0

        lax.fori_loop(first, last, inner, 0)

    def own_tgt(cols):
        got = (0.5 * dot(grid[...].reshape(flat, width), wtgt[:, cols]).astype(BF)).astype(BF)
        tgt[:, :, cols] = got.reshape(members, rows, CW)

    def own_src(cols):
        got = (0.5 * dot(lat[...].reshape(flat, width), wsrc[:, cols]).astype(BF)).astype(BF)
        proj[:, HALO:HALO + rows, cols] = got.reshape(members, rows, CW)

    loads[0].wait()
    columns(own_tgt)
    loads[1].wait()
    columns(own_src)

    def turn_grid(m, _):
        grid_x[:, pl.ds(pl.multiple_of(m * rows, rows), rows)] = grid[m].T
        return 0

    lax.fori_loop(0, members, turn_grid, 0)
    loads[2].wait()

    gb = 32

    def forward(m, _):
        for one in halo_copies(m):
            one.wait()
        edge = (0.5 * dot(halo[m], wsrc[...]).astype(BF)).astype(BF)
        proj[m, 0:HALO] = edge[0:HALO]
        proj[m, HALO + rows:ext] = edge[HALO:2 * HALO]

        linear = dot(hits[...], proj[m]) + count * tgt[m].astype(F32)
        for at in range(0, rows, gb):
            got = dot(pick[:, at:at + gb, :].reshape(nbrs * gb, ext), proj[m]).astype(BF)
            got = got.reshape(nbrs, gb, width)
            for c in range(0, width, 256):
                cols = slice(c, c + 256)
                base = tgt[m, at:at + gb, cols]
                acc = None
                acc_s = None
                for k in range(nbrs):
                    on = maskb[k, at:at + gb, :]
                    u = got[k, :, cols] + jnp.concatenate([on, on], axis=1) * base
                    t = jnp.tanh(u)
                    p = u * t
                    s = (t + u) - t * p
                    acc = p if k == 0 else acc + p
                    acc_s = s if k == 0 else acc_s + s
                    slope[m, k, at:at + gb, cols] = s
                total = linear[at:at + gb, cols] + acc.astype(F32)
                agg[m, at:at + gb, cols] = (0.25 * total).astype(BF)
                slope_sum[m, at:at + gb, cols] = (acc_s.astype(F32) + count[at:at + gb]).astype(BF)

        h = grid[m].astype(F32) + dot(agg[m], wmix[...])
        mean = jnp.sum(h, axis=1, keepdims=True) * (1.0 / width)
        centre = h - mean
        var = jnp.sum(centre * centre, axis=1, keepdims=True) * (1.0 / width)
        r = lax.rsqrt(var + EPS)
        inv[m] = jnp.broadcast_to(r, (rows, 128))
        normed[m] = (centre * r).astype(BF)
        ys[m] = dot_nt(normed[m], wout[...])
        y_copy(m).start()
        return 0

    lax.fori_loop(0, members, forward, 0)

    def turn(m, _):
        at = pl.ds(pl.multiple_of(m * rows, rows), rows)
        agg_x[:, at] = agg[m].T
        normed_x[:, at] = normed[m].T
        around = jnp.concatenate([halo[m, 0:HALO], lat[m], halo[m, HALO:2 * HALO]], axis=0)
        lat_x[:, pl.ds(pl.multiple_of(m * ext, ext), ext)] = around.T
        return 0

    lax.fori_loop(0, members, turn, 0)

    def y_wait(m, _):
        y_copy(m).wait()
        return 0

    lax.fori_loop(0, members, y_wait, 0)

    total = 2 * members

    def head(m, _):
        y = ys[m]
        miss = y - truth[...]
        pair = jnp.zeros_like(y)
        for o in range(total):
            diff = y - ys[o]
            pair = pair + diff * lax.rsqrt(diff * diff + SMOOTH)
        grad = miss * lax.rsqrt(miss * miss + SMOOTH) * (1.0 / total)
        dy = (area[...] * (grad - (FAIR / (total * (total - 1))) * pair)).astype(BF)
        dys[m] = dy
        dn = dot(dy, wout[...])
        nh = normed[m].astype(F32)
        m1 = jnp.sum(dn, axis=1, keepdims=True) * (1.0 / width)
        m2 = jnp.sum(dn * nh, axis=1, keepdims=True) * (1.0 / width)
        dh[m] = (inv[m][:, 0:1] * (dn - m1 - nh * m2)).astype(BF)
        return 0

    lax.fori_loop(0, members, head, 0)

    halves = []
    left = pl.ds(0, 512)
    at = 0
    for part, held in ((part_mix, held_mix), (part_tgt, held_tgt), (part_src, held_src)):
        wide = part.shape[-1]
        halves.append(Half(place, wire, part, held, left, True, bufs[at:at + 2], bufs[at + 2]))
        halves.append(Half(place, wire, part, held, pl.ds(512, wide - 512), False,
                           bufs[at + 3:at + 5], bufs[at + 5]))
        at += 6
    mix_l, mix_r, tgt_l, tgt_r, src_l, src_r = halves

    def product(turned, right):
        return dot(turned[...], right.reshape(-1, right.shape[-1])).astype(BF)

    def mix_grad(cols):
        put(part_mix, product(agg_x, dh[:, :, cols]), cols)

    columns(mix_grad, 0, 1)
    mix_l.start()
    columns(mix_grad, 1, 2)
    put(part_mix, product(normed_x, dys[...]), pl.ds(width, FP))
    mix_r.start()

    def mix_back(cols):
        dagg = (0.125 * dot_nt(dh[...].reshape(flat, width), wmix[cols, :])).astype(BF)
        dagg = dagg.reshape(members, rows, CW)
        tgt[:, :, cols] = dagg
        dq[:, :, cols] = dagg * slope_sum[:, :, cols]

    columns(mix_back)

    def tgt_grad(cols):
        put(part_tgt, product(grid_x, dq[:, :, cols]), cols)

    columns(tgt_grad, 0, 1)
    tgt_l.start()
    columns(tgt_grad, 1, 2)
    tgt_r.start()
    mix_l.s1()
    mix_r.s1()

    def spread(m):
        def column(cols):
            d = tgt[m, :, cols]
            for k in range(nbrs):
                slope[m, k, :, cols] = slope[m, k, :, cols] * d
            edges = slope[m, :, :, cols].reshape(nbrs * rows, CW)
            got = dot(pick_t[...], edges) + dot(hits_t[...], d)
            dpe[m, :, cols] = got.astype(BF)

        columns(column)
        for one in rim_copies(m):
            one.start()

    spread(0)
    tgt_l.s1()
    tgt_r.s1()
    spread(1)
    spread(2)
    mix_l.s2()
    mix_r.s2()
    spread(3)

    def src_grad(cols):
        put(part_src, product(lat_x, dpe[:, :, cols]), cols)

    columns(src_grad, 0, 1)
    src_l.start()
    tgt_l.s2()
    tgt_r.s2()
    columns(src_grad, 1, 2)
    src_r.start()
    mix_l.s3()
    mix_r.s3()
    src_l.s1()

    def grid_back(cols):
        got = dot_nt(dq[...].reshape(flat, width), wtgt[cols, :]).reshape(members, rows, CW)
        d_grid[:, :, cols] = (dh[:, :, cols].astype(F32) + got).astype(BF)

    columns(grid_back, 0, 1)
    src_r.s1()
    columns(grid_back, 1, 2)
    tgt_l.s3()
    tgt_r.s3()
    o_mix[:, 0:512] = mix_l.s4(scale)
    last = mix_r.s4(scale)
    o_mix[:, 512:width] = last[:, 0:width - 512]
    o_out[...] = last[:, width - 512:width - 512 + fields]

    def sum_rims(m, _):
        for one in rim_copies(m):
            one.wait()
        dq[m] = (dpe[m, HALO:HALO + rows].astype(F32) + rims[m].astype(F32)).astype(BF)
        return 0

    lax.fori_loop(0, members, sum_rims, 0)

    def latent_back(cols):
        got = dot_nt(dq[...].reshape(flat, width), wsrc[cols, :]).reshape(members, rows, CW)
        d_latent[:, :, cols] = got.astype(BF)

    columns(latent_back, 0, 1)
    src_l.s2()
    columns(latent_back, 1, 2)
    src_r.s2()
    src_l.s3()
    src_r.s3()
    o_tgt[:, 0:512] = tgt_l.s4(scale)
    o_tgt[:, 512:width] = tgt_r.s4(scale)
    o_src[:, 0:512] = src_l.s4(scale)
    o_src[:, 512:width] = src_r.s4(scale)


def hand_over(arrays):
    count = len(arrays)

    def move(*refs):
        sems = refs[-1]
        moves = [pltpu.make_async_copy(refs[i], refs[count + i], sems.at[i]) for i in range(count)]
        for one in moves:
            one.start()
        for one in moves:
            one.wait()

    anywhere = pl.BlockSpec(memory_space=pl.ANY)
    return pl.pallas_call(
        move,
        out_shape=[jax.ShapeDtypeStruct(a.shape, a.dtype) for a in arrays],
        in_specs=[pl.BlockSpec(memory_space=pltpu.VMEM)] * count,
        out_specs=[anywhere] * count,
        scratch_shapes=[pltpu.SemaphoreType.DMA((count,))],
    )(*arrays)


def on_device(latent, grid_in, w_src, w_tgt, w_mix, w_out, truth, area, nbr, mask):
    members, rows, width = grid_in.shape
    nbrs = nbr.shape[0]
    fields = w_out.shape[1]
    ext = rows + 2 * HALO
    tiles = lax.axis_size("grid")
    count = members * lax.axis_size("member")
    scale = 1.0 / math.sqrt(rows * tiles * count)

    def body_(*refs):
        body(scale, *refs)

    def ring_bufs(cols):
        return [pltpu.VMEM((3, 4, 2, 16, cols), BF), pltpu.VMEM((3, 2, 16, cols), BF),
                pltpu.VMEM((3, 16, cols), BF)]

    vm = pl.BlockSpec(memory_space=pltpu.VMEM)
    hbm = pl.BlockSpec(memory_space=pl.ANY)
    sds = jax.ShapeDtypeStruct
    wide = width + FP
    halves = (512, wide - 512, 512, width - 512, 512, width - 512)
    ncopies = 10 * len(halves)
    results = pl.pallas_call(
        body_,
        out_shape=[
            sds((members, rows, width), BF),
            sds((members, rows, width), BF),
            sds((16, width), F32),
            sds((16, width), F32),
            sds((16, width), F32),
            sds((16, fields), F32),
        ],
        in_specs=[vm, vm, hbm, hbm, hbm, vm, vm, vm, vm, vm],
        out_specs=[vm] * 6,
        scratch_shapes=[
            pltpu.VMEM((width, width), BF),
            pltpu.VMEM((width, width), BF),
            pltpu.VMEM((width, width), BF),
            pltpu.VMEM((FP, width), BF),
            pltpu.VMEM((FP, rows), F32),
            pltpu.VMEM((rows, FP), F32),
            pltpu.VMEM((nbrs, rows, ext), BF),
            pltpu.VMEM((ext, nbrs * rows), BF),
            pltpu.VMEM((rows, ext), BF),
            pltpu.VMEM((ext, rows), BF),
            pltpu.VMEM((nbrs, rows, 128), BF),
            pltpu.VMEM((members, ext, width), BF),
            pltpu.VMEM((members, rows, width), BF),
            pltpu.VMEM((members, nbrs, rows, width), BF),
            pltpu.VMEM((members, rows, width), BF),
            pltpu.VMEM((members, rows, width), BF),
            pltpu.VMEM((members, rows, width), BF),
            pltpu.VMEM((members, rows, 128), F32),
            pltpu.VMEM((2 * members, rows, FP), F32),
            pltpu.VMEM((members, rows, FP), BF),
            pltpu.VMEM((members, rows, width), BF),
            pltpu.VMEM((members, rows, width), BF),
            pltpu.VMEM((members, ext, width), BF),
            pltpu.VMEM((width, members * rows), BF),
            pltpu.VMEM((width, members * rows), BF),
            pltpu.VMEM((width, members * rows), BF),
            pltpu.VMEM((width, members * ext), BF),
            pltpu.VMEM((members, 2 * HALO, width), BF),
            pltpu.VMEM((members, 2 * HALO, width), BF),
            pltpu.VMEM((NC, NY, NX, NZ, 16, width), BF),
            pltpu.VMEM((NC, NY, NX, NZ, 16, width), BF),
            pltpu.VMEM((NC, NY, NX, NZ, 16, wide), BF),
            pltpu.VMEM((NY, NX, NZ, 16, width), BF),
            pltpu.VMEM((NY, NX, NZ, 16, width), BF),
            pltpu.VMEM((NY, NX, NZ, 16, wide), BF),
            *[buf for cols in halves for buf in ring_bufs(cols)],
            pltpu.SemaphoreType.DMA((ncopies,)),
            pltpu.SemaphoreType.DMA((ncopies,)),
            pltpu.SemaphoreType.DMA((2, members)),
            pltpu.SemaphoreType.DMA((2, members)),
            pltpu.SemaphoreType.DMA((2, members)),
            pltpu.SemaphoreType.DMA((2, members)),
            pltpu.SemaphoreType.DMA((members,)),
            pltpu.SemaphoreType.DMA((members,)),
            pltpu.SemaphoreType.DMA((3,)),
        ],
        compiler_params=pltpu.CompilerParams(
            collective_id=0, has_side_effects=True, vmem_limit_bytes=63 * 2**20
        ),
        cost_estimate=pl.CostEstimate(flops=40 * 10**9, bytes_accessed=30 * 10**6, transcendentals=0),
    )(latent, grid_in, w_src, w_tgt, w_mix, w_out.T, truth, area.reshape(1, rows), nbr, mask)
    return hand_over(results)


def solution(mesh):
    in_specs = (
        P("member", "grid", None), P("member", "grid", None), P(), P(), P(), P(),
        P(None, "grid"), P("grid"), P(None, "grid"), P(None, "grid"),
    )
    out_specs = (
        P("member", "grid", None), P("member", "grid", None),
        P("grid", None), P("grid", None), P("grid", None), P("grid", None),
    )
    return jax.shard_map(
        on_device, mesh=mesh, in_specs=in_specs, out_specs=out_specs, check_vma=False
    )
```

```python
import math

import jax
import jax.numpy as jnp
from jax import lax
from jax.experimental import pallas as pl
from jax.experimental.pallas import tpu as pltpu
from jax.sharding import PartitionSpec as P

HALO = 64
SMOOTH = 0.0025
FAIR = 0.95
EPS = 1e-05
BF = jnp.bfloat16
F32 = jnp.float32
MESH = pl.DeviceIdType.MESH
CW = 512
NY, NX, NZ, NC = 4, 4, 2, 2
FP = 128


def dot(a, b):
    return lax.dot_general(a, b, (((1,), (0,)), ((), ())), preferred_element_type=F32)


def dot_nt(a, b):
    return lax.dot_general(a, b, (((1,), (1,)), ((), ())), preferred_element_type=F32)


def dot_tn(a, b):
    return lax.dot_general(a, b, (((0,), (0,)), ((), ())), preferred_element_type=F32)


class Place:
    def __init__(self):
        self.me = lax.axis_index("member")
        t = lax.axis_index("grid")
        tiles = NY * NX * NZ * NC
        self.y, self.x, self.z, self.c = t // 16, (t // 4) % 4, (t // 2) % 2, t % 2
        self.up = (self.me, (t + 1) % tiles)
        self.down = (self.me, (t + tiles - 1) % tiles)
        self.mate = (1 - self.me, t)
        self.core = self.at(c=1 - self.c)
        self.y_ring = tuple(self.at(y=(self.y + k) % 4) for k in (1, 2, 3))
        self.x_ring = tuple(self.at(x=(self.x + k) % 4) for k in (1, 2, 3))
        self.z_far = (self.me, self.at(z=1 - self.z)[1])
        self.z_both = (1 - self.me, self.z_far[1])
        self.partners = (self.up, self.down, self.core, *self.y_ring, *self.x_ring,
                         self.mate, self.z_far, self.z_both)

    def at(self, y=None, x=None, z=None, c=None):
        y = self.y if y is None else y
        x = self.x if x is None else x
        z = self.z if z is None else z
        c = self.c if c is None else c
        return (self.me, y * 16 + x * 4 + z * 2 + c)


class Wire:
    def __init__(self, send, recv):
        self.send, self.recv, self.used = send, recv, 0

    def copy(self, src, dst, device):
        at = self.used
        self.used += 1
        return pltpu.make_async_remote_copy(
            src_ref=src, dst_ref=dst, send_sem=self.send.at[at], recv_sem=self.recv.at[at],
            device_id=device, device_id_type=MESH)


def add_into(dst, *others):
    total = dst[...].astype(F32)
    for o in others:
        total = total + o[...].astype(F32)
    dst[...] = total.astype(BF)


class Swap:
    def __init__(self, wire, p, others, block, buf):
        self.wire, self.p, self.others, self.block, self.buf = wire, p, others, block, buf

    def start(self):
        self.moves = [self.wire.copy(self.block((self.p + k) % 4), self.buf.at[k - 1], self.others[k - 1])
                      for k in (1, 3, 2)]
        for one in self.moves:
            one.start()

    def finish(self):
        for one in self.moves:
            one.wait()
        add_into(self.block(self.p), *[self.buf.at[k] for k in range(3)])


class Half:
    def __init__(self, place, wire, part, held, cols, y_first, bufs, zbuf):
        self.place, self.wire, self.zbuf, self.cols = place, wire, zbuf, cols
        self.part, self.held = part, held
        y, x = place.y, place.x

        on_y, on_x = (y, place.y_ring), (x, place.x_ring)
        if y_first:
            self.one = Swap(wire, *on_y, lambda d: held.at[d, :, :, :, cols], bufs[0])
            self.two = Swap(wire, *on_x, lambda d: held.at[y, d, :, :, cols], bufs[1])
        else:
            self.one = Swap(wire, *on_x, lambda d: held.at[:, d, :, :, cols], bufs[0])
            self.two = Swap(wire, *on_y, lambda d: held.at[d, x, :, :, cols], bufs[1])

    def start(self):
        cols = self.cols
        self.cross = self.wire.copy(self.part.at[1 - self.place.c, :, :, :, :, cols],
                                    self.held.at[:, :, :, :, cols], self.place.core)
        self.cross.start()

    def s1(self):
        self.cross.wait()
        cols = self.cols

        def add(yy, _):
            add_into(self.held.at[yy, :, :, :, cols], self.part.at[self.place.c, yy, :, :, :, cols])
            return 0

        lax.fori_loop(0, NY, add, 0)
        self.one.start()

    def s2(self):
        self.one.finish()
        self.two.start()

    def s3(self):
        self.two.finish()
        p = self.place
        mine = self.held.at[p.y, p.x]
        self.last = [self.wire.copy(mine.at[p.z, :, self.cols], self.zbuf.at[0], p.mate),
                     self.wire.copy(mine.at[1 - p.z, :, self.cols], self.zbuf.at[1], p.z_far),
                     self.wire.copy(mine.at[1 - p.z, :, self.cols], self.zbuf.at[2], p.z_both)]
        for one in self.last:
            one.start()

    def s4(self, scale):
        p = self.place
        for one in self.last:
            one.wait()
        total = self.held[p.y, p.x, p.z, :, self.cols].astype(F32)
        for k in range(3):
            total = total + self.zbuf[k].astype(F32)
        return total * scale


def put(part, block, cols):
    for b in range(NY * NX * NZ * NC):
        part[b % 2, b // 16, (b // 4) % 4, (b // 2) % 2, :, cols] = block[b * 16:(b + 1) * 16]


def body(scale, lat, grid, wsrc_in, wtgt_in, wmix_in, wout_in, truth_in, area_in, nbr, mask,
         d_latent, d_grid, o_src, o_tgt, o_mix, o_out,
         wsrc, wtgt, wmix, wout, truth, area,
         pick, pick_t, hits, hits_t, maskb, proj, tgt, slope, slope_sum, agg, normed, inv, ys, dys, dh, dq, dpe,
         agg_x, normed_x, grid_x, lat_x, got,
         halo, rims, part_src, part_tgt, part_mix, held_src, held_tgt, held_mix, *rest):
    send_sem, recv_sem, halo_send, halo_recv, rim_send, rim_recv, y_send, y_recv, load_sem = rest[-9:]
    bufs = rest[:-9]
    members, rows, width = grid.shape
    nbrs = nbr.shape[0]
    fields = wout_in.shape[0]
    ext = rows + 2 * HALO
    tiles = width // CW
    flat = members * rows
    place = Place()
    wire = Wire(send_sem, recv_sem)

    barrier = pltpu.get_barrier_semaphore()
    for partner in place.partners:
        pl.semaphore_signal(barrier, inc=1, device_id=partner, device_id_type=MESH)
    loads = [pltpu.make_async_copy(src, dst, load_sem.at[i])
             for i, (src, dst) in enumerate(((wtgt_in, wtgt), (wsrc_in, wsrc), (wmix_in, wmix)))]
    for one in loads:
        one.start()

    def copies(src_up, src_down, dst, sems, m):
        return (
            pltpu.make_async_remote_copy(
                src_ref=src_up, dst_ref=dst.at[m, pl.ds(0, HALO)],
                send_sem=sems[0].at[0, m], recv_sem=sems[1].at[0, m],
                device_id=place.up, device_id_type=MESH),
            pltpu.make_async_remote_copy(
                src_ref=src_down, dst_ref=dst.at[m, pl.ds(HALO, HALO)],
                send_sem=sems[0].at[1, m], recv_sem=sems[1].at[1, m],
                device_id=place.down, device_id_type=MESH),
        )

    def halo_copies(m):
        return copies(lat.at[m, pl.ds(rows - HALO, HALO)], lat.at[m, pl.ds(0, HALO)], halo,
                      (halo_send, halo_recv), m)

    def rim_copies(m):
        return copies(dpe.at[m, pl.ds(HALO + rows, HALO)], dpe.at[m, pl.ds(0, HALO)], rims,
                      (rim_send, rim_recv), m)

    def y_copy(m):
        return pltpu.make_async_remote_copy(
            src_ref=ys.at[m], dst_ref=ys.at[members + m],
            send_sem=y_send.at[m], recv_sem=y_recv.at[m],
            device_id=place.mate, device_id_type=MESH)

    pl.semaphore_wait(barrier, len(place.partners))
    for m in range(members):
        for one in halo_copies(m):
            one.start()

    truth[...] = jnp.zeros_like(truth)
    truth[0:fields, :] = truth_in[...]
    truth[...] = truth[...].T
    area[...] = jnp.broadcast_to(area_in[...], (rows, FP)).T
    wout[...] = jnp.zeros_like(wout)
    wout[0:fields, :] = wout_in[...]

    code = jnp.where(mask[...] != 0, nbr[...], -1).astype(F32)
    code_t = jnp.concatenate([code, jnp.zeros((rows - nbrs, rows), F32)], axis=0).T
    lane = lax.broadcasted_iota(jnp.int32, (rows, ext), 1).astype(F32)
    sub = lax.broadcasted_iota(jnp.int32, (ext, rows), 0).astype(F32)
    count = jnp.zeros((rows, 1), F32)
    for k in range(nbrs):
        col = code_t[:, k:k + 1]
        on = jnp.where(col >= 0.0, 1.0, 0.0)
        one = (col == lane).astype(F32).astype(BF)
        one_t = (code[k:k + 1, :] == sub).astype(F32).astype(BF)
        pick[k] = one
        maskb[k] = jnp.broadcast_to(on, (rows, 128)).astype(BF)
        count = count + on
        pick_t[:, k * rows:(k + 1) * rows] = one_t
        if k == 0:
            hits[...] = one
            hits_t[...] = one_t
        else:
            hits[...] += one
            hits_t[...] += one_t

    def columns(step, first=0, last=tiles):
        def inner(c, _):
            step(pl.ds(pl.multiple_of(c * CW, CW), CW))
            return 0

        lax.fori_loop(first, last, inner, 0)

    def own_tgt(cols):
        got = (0.5 * dot(grid[...].reshape(flat, width), wtgt[:, cols]).astype(BF)).astype(BF)
        tgt[:, :, cols] = got.reshape(members, rows, CW)

    def own_src(cols):
        got = (0.5 * dot(lat[...].reshape(flat, width), wsrc[:, cols]).astype(BF)).astype(BF)
        proj[:, HALO:HALO + rows, cols] = got.reshape(members, rows, CW)

    loads[0].wait()
    columns(own_tgt)
    loads[1].wait()
    columns(own_src)

    loads[2].wait()

    gb = 16
    chunks = rows // gb

    def forward(m, _):
        for one in halo_copies(m):
            one.wait()
        edge = (0.5 * dot(halo[m], wsrc[...]).astype(BF)).astype(BF)
        proj[m, 0:HALO] = edge[0:HALO]
        proj[m, HALO + rows:ext] = edge[HALO:2 * HALO]

        linear = dot(hits[...], proj[m]) + count * tgt[m].astype(F32)

        def edges(i):
            at = i * gb
            for c in range(0, width, 256):
                cols = slice(c, c + 256)
                base = tgt[m, at:at + gb, cols]
                acc = None
                acc_s = None
                for k in range(nbrs):
                    on = maskb[k, at:at + gb, :]
                    u = got[i % 2, k * gb:(k + 1) * gb, cols] + jnp.concatenate([on, on], axis=1) * base
                    t = jnp.tanh(u)
                    p = u * t
                    s = (t + u) - t * p
                    acc = p if k == 0 else acc + p
                    acc_s = s if k == 0 else acc_s + s
                    slope[m, k, at:at + gb, cols] = s
                total = linear[at:at + gb, cols] + acc.astype(F32)
                agg[m, at:at + gb, cols] = (0.25 * total).astype(BF)
                slope_sum[m, at:at + gb, cols] = (acc_s.astype(F32) + count[at:at + gb]).astype(BF)

        for i in range(chunks + 1):
            if i < chunks:
                rows_i = pick[:, i * gb:(i + 1) * gb, :].reshape(nbrs * gb, ext)
                got[i % 2] = dot(rows_i, proj[m]).astype(BF)
            if i == 0:
                grid_x[:, pl.ds(pl.multiple_of(m * rows, rows), rows)] = grid[m].T
                around = jnp.concatenate([halo[m, 0:HALO], lat[m], halo[m, HALO:2 * HALO]], axis=0)
                lat_x[:, pl.ds(pl.multiple_of(m * ext, ext), ext)] = around.T
            else:
                edges(i - 1)

        h = grid[m].astype(F32) + dot(agg[m], wmix[...])
        mean = jnp.sum(h, axis=1, keepdims=True) * (1.0 / width)
        centre = h - mean
        var = jnp.sum(centre * centre, axis=1, keepdims=True) * (1.0 / width)
        r = lax.rsqrt(var + EPS)
        inv[m] = jnp.broadcast_to(r, (rows, 128))
        normed[m] = (centre * r).astype(BF)
        ys[m] = dot_nt(normed[m], wout[...])
        y_copy(m).start()
        return 0

    lax.fori_loop(0, members, forward, 0)

    def turn(m, _):
        at = pl.ds(pl.multiple_of(m * rows, rows), rows)
        agg_x[:, at] = agg[m].T
        normed_x[:, at] = normed[m].T
        return 0

    lax.fori_loop(0, members, turn, 0)

    def y_wait(m, _):
        y_copy(m).wait()
        return 0

    lax.fori_loop(0, members, y_wait, 0)

    total = 2 * members

    def head(m, _):
        y = ys[m]
        miss = y - truth[...]
        pair = jnp.zeros_like(y)
        for o in range(total):
            diff = y - ys[o]
            pair = pair + diff * lax.rsqrt(diff * diff + SMOOTH)
        grad = miss * lax.rsqrt(miss * miss + SMOOTH) * (1.0 / total)
        dy = (area[...] * (grad - (FAIR / (total * (total - 1))) * pair)).astype(BF)
        dys[m] = dy
        dn = dot(dy, wout[...])
        nh = normed[m].astype(F32)
        m1 = jnp.sum(dn, axis=1, keepdims=True) * (1.0 / width)
        m2 = jnp.sum(dn * nh, axis=1, keepdims=True) * (1.0 / width)
        dh[m] = (inv[m][:, 0:1] * (dn - m1 - nh * m2)).astype(BF)
        return 0

    lax.fori_loop(0, members, head, 0)

    halves = []
    left = pl.ds(0, 512)
    at = 0
    for part, held in ((part_mix, held_mix), (part_tgt, held_tgt), (part_src, held_src)):
        wide = part.shape[-1]
        halves.append(Half(place, wire, part, held, left, True, bufs[at:at + 2], bufs[at + 2]))
        halves.append(Half(place, wire, part, held, pl.ds(512, wide - 512), False,
                           bufs[at + 3:at + 5], bufs[at + 5]))
        at += 6
    mix_l, mix_r, tgt_l, tgt_r, src_l, src_r = halves

    def product(turned, right):
        return dot(turned[...], right.reshape(-1, right.shape[-1])).astype(BF)

    def mix_grad(cols):
        put(part_mix, product(agg_x, dh[:, :, cols]), cols)

    columns(mix_grad, 0, 1)
    mix_l.start()
    columns(mix_grad, 1, 2)
    put(part_mix, product(normed_x, dys[...]), pl.ds(width, FP))
    mix_r.start()

    def mix_back(cols):
        dagg = (0.125 * dot_nt(dh[...].reshape(flat, width), wmix[cols, :])).astype(BF)
        dagg = dagg.reshape(members, rows, CW)
        tgt[:, :, cols] = dagg
        dq[:, :, cols] = dagg * slope_sum[:, :, cols]

    columns(mix_back)

    def tgt_grad(cols):
        put(part_tgt, product(grid_x, dq[:, :, cols]), cols)

    columns(tgt_grad, 0, 1)
    tgt_l.start()
    columns(tgt_grad, 1, 2)
    tgt_r.start()
    mix_l.s1()
    mix_r.s1()

    def weigh(m, c):
        cols = slice(c * CW, (c + 1) * CW)
        for k in range(nbrs):
            slope[m, k, :, cols] = slope[m, k, :, cols] * tgt[m, :, cols]

    def spread(m):
        for c in range(tiles):
            cols = slice(c * CW, (c + 1) * CW)
            edges = slope[m, :, :, cols].reshape(nbrs * rows, CW)
            got_c = dot(pick_t[...], edges) + dot(hits_t[...], tgt[m, :, cols])
            dpe[m, :, cols] = got_c.astype(BF)
            if c + 1 < tiles:
                weigh(m, c + 1)
            elif m + 1 < members:
                weigh(m + 1, 0)
        for one in rim_copies(m):
            one.start()

    weigh(0, 0)
    spread(0)
    tgt_l.s1()
    tgt_r.s1()
    spread(1)
    spread(2)
    mix_l.s2()
    mix_r.s2()
    spread(3)

    def src_grad(cols):
        put(part_src, product(lat_x, dpe[:, :, cols]), cols)

    columns(src_grad, 0, 1)
    src_l.start()
    tgt_l.s2()
    tgt_r.s2()
    columns(src_grad, 1, 2)
    src_r.start()
    mix_l.s3()
    mix_r.s3()
    src_l.s1()

    def grid_back(cols):
        got = dot_nt(dq[...].reshape(flat, width), wtgt[cols, :]).reshape(members, rows, CW)
        d_grid[:, :, cols] = (dh[:, :, cols].astype(F32) + got).astype(BF)

    columns(grid_back, 0, 1)
    src_r.s1()
    columns(grid_back, 1, 2)
    tgt_l.s3()
    tgt_r.s3()
    o_mix[:, 0:512] = mix_l.s4(scale)
    last = mix_r.s4(scale)
    o_mix[:, 512:width] = last[:, 0:width - 512]
    o_out[...] = last[:, width - 512:width - 512 + fields]

    def sum_rims(m, _):
        for one in rim_copies(m):
            one.wait()
        dq[m] = (dpe[m, HALO:HALO + rows].astype(F32) + rims[m].astype(F32)).astype(BF)
        return 0

    lax.fori_loop(0, members, sum_rims, 0)

    def latent_back(cols):
        got = dot_nt(dq[...].reshape(flat, width), wsrc[cols, :]).reshape(members, rows, CW)
        d_latent[:, :, cols] = got.astype(BF)

    columns(latent_back, 0, 1)
    src_l.s2()
    columns(latent_back, 1, 2)
    src_r.s2()
    src_l.s3()
    src_r.s3()
    o_tgt[:, 0:512] = tgt_l.s4(scale)
    o_tgt[:, 512:width] = tgt_r.s4(scale)
    o_src[:, 0:512] = src_l.s4(scale)
    o_src[:, 512:width] = src_r.s4(scale)


def hand_over(arrays):
    count = len(arrays)

    def move(*refs):
        sems = refs[-1]
        moves = [pltpu.make_async_copy(refs[i], refs[count + i], sems.at[i]) for i in range(count)]
        for one in moves:
            one.start()
        for one in moves:
            one.wait()

    anywhere = pl.BlockSpec(memory_space=pl.ANY)
    return pl.pallas_call(
        move,
        out_shape=[jax.ShapeDtypeStruct(a.shape, a.dtype) for a in arrays],
        in_specs=[pl.BlockSpec(memory_space=pltpu.VMEM)] * count,
        out_specs=[anywhere] * count,
        scratch_shapes=[pltpu.SemaphoreType.DMA((count,))],
    )(*arrays)


def on_device(latent, grid_in, w_src, w_tgt, w_mix, w_out, truth, area, nbr, mask):
    members, rows, width = grid_in.shape
    nbrs = nbr.shape[0]
    fields = w_out.shape[1]
    ext = rows + 2 * HALO
    tiles = lax.axis_size("grid")
    count = members * lax.axis_size("member")
    scale = 1.0 / math.sqrt(rows * tiles * count)

    def body_(*refs):
        body(scale, *refs)

    def ring_bufs(cols):
        return [pltpu.VMEM((3, 4, 2, 16, cols), BF), pltpu.VMEM((3, 2, 16, cols), BF),
                pltpu.VMEM((3, 16, cols), BF)]

    vm = pl.BlockSpec(memory_space=pltpu.VMEM)
    hbm = pl.BlockSpec(memory_space=pl.ANY)
    sds = jax.ShapeDtypeStruct
    wide = width + FP
    halves = (512, wide - 512, 512, width - 512, 512, width - 512)
    ncopies = 10 * len(halves)
    results = pl.pallas_call(
        body_,
        out_shape=[
            sds((members, rows, width), BF),
            sds((members, rows, width), BF),
            sds((16, width), F32),
            sds((16, width), F32),
            sds((16, width), F32),
            sds((16, fields), F32),
        ],
        in_specs=[vm, vm, hbm, hbm, hbm, vm, vm, vm, vm, vm],
        out_specs=[vm] * 6,
        scratch_shapes=[
            pltpu.VMEM((width, width), BF),
            pltpu.VMEM((width, width), BF),
            pltpu.VMEM((width, width), BF),
            pltpu.VMEM((FP, width), BF),
            pltpu.VMEM((FP, rows), F32),
            pltpu.VMEM((rows, FP), F32),
            pltpu.VMEM((nbrs, rows, ext), BF),
            pltpu.VMEM((ext, nbrs * rows), BF),
            pltpu.VMEM((rows, ext), BF),
            pltpu.VMEM((ext, rows), BF),
            pltpu.VMEM((nbrs, rows, 128), BF),
            pltpu.VMEM((members, ext, width), BF),
            pltpu.VMEM((members, rows, width), BF),
            pltpu.VMEM((members, nbrs, rows, width), BF),
            pltpu.VMEM((members, rows, width), BF),
            pltpu.VMEM((members, rows, width), BF),
            pltpu.VMEM((members, rows, width), BF),
            pltpu.VMEM((members, rows, 128), F32),
            pltpu.VMEM((2 * members, rows, FP), F32),
            pltpu.VMEM((members, rows, FP), BF),
            pltpu.VMEM((members, rows, width), BF),
            pltpu.VMEM((members, rows, width), BF),
            pltpu.VMEM((members, ext, width), BF),
            pltpu.VMEM((width, members * rows), BF),
            pltpu.VMEM((width, members * rows), BF),
            pltpu.VMEM((width, members * rows), BF),
            pltpu.VMEM((width, members * ext), BF),
            pltpu.VMEM((2, nbrs * 16, width), BF),
            pltpu.VMEM((members, 2 * HALO, width), BF),
            pltpu.VMEM((members, 2 * HALO, width), BF),
            pltpu.VMEM((NC, NY, NX, NZ, 16, width), BF),
            pltpu.VMEM((NC, NY, NX, NZ, 16, width), BF),
            pltpu.VMEM((NC, NY, NX, NZ, 16, wide), BF),
            pltpu.VMEM((NY, NX, NZ, 16, width), BF),
            pltpu.VMEM((NY, NX, NZ, 16, width), BF),
            pltpu.VMEM((NY, NX, NZ, 16, wide), BF),
            *[buf for cols in halves for buf in ring_bufs(cols)],
            pltpu.SemaphoreType.DMA((ncopies,)),
            pltpu.SemaphoreType.DMA((ncopies,)),
            pltpu.SemaphoreType.DMA((2, members)),
            pltpu.SemaphoreType.DMA((2, members)),
            pltpu.SemaphoreType.DMA((2, members)),
            pltpu.SemaphoreType.DMA((2, members)),
            pltpu.SemaphoreType.DMA((members,)),
            pltpu.SemaphoreType.DMA((members,)),
            pltpu.SemaphoreType.DMA((3,)),
        ],
        compiler_params=pltpu.CompilerParams(
            collective_id=0, has_side_effects=True, vmem_limit_bytes=63 * 2**20
        ),
        cost_estimate=pl.CostEstimate(flops=40 * 10**9, bytes_accessed=30 * 10**6, transcendentals=0),
    )(latent, grid_in, w_src, w_tgt, w_mix, w_out.T, truth, area.reshape(1, rows), nbr, mask)
    return hand_over(results)


def solution(mesh):
    in_specs = (
        P("member", "grid", None), P("member", "grid", None), P(), P(), P(), P(),
        P(None, "grid"), P("grid"), P(None, "grid"), P(None, "grid"),
    )
    out_specs = (
        P("member", "grid", None), P("member", "grid", None),
        P("grid", None), P("grid", None), P("grid", None), P("grid", None),
    )
    return jax.shard_map(
        on_device, mesh=mesh, in_specs=in_specs, out_specs=out_specs, check_vma=False
    )
```

```python
import math

import jax
import jax.numpy as jnp
from jax import lax
from jax.experimental import pallas as pl
from jax.experimental.pallas import tpu as pltpu
from jax.sharding import PartitionSpec as P

HALO = 64
SMOOTH = 0.0025
FAIR = 0.95
EPS = 1e-05
BF = jnp.bfloat16
F32 = jnp.float32
MESH = pl.DeviceIdType.MESH
CW = 512
NY, NX, NZ, NC = 4, 4, 2, 2
FP = 128
MIX_CUTS = ((0, 512), (512, 512 + FP))
TGT_CUTS = ((0, 512), (512, 512))
SRC_CUTS = ((0, 256), (256, 256), (512, 256), (768, 256))


def dot(a, b):
    return lax.dot_general(a, b, (((1,), (0,)), ((), ())), preferred_element_type=F32)


def dot_nt(a, b):
    return lax.dot_general(a, b, (((1,), (1,)), ((), ())), preferred_element_type=F32)


def dot_tn(a, b):
    return lax.dot_general(a, b, (((0,), (0,)), ((), ())), preferred_element_type=F32)


class Place:
    def __init__(self):
        self.me = lax.axis_index("member")
        t = lax.axis_index("grid")
        tiles = NY * NX * NZ * NC
        self.y, self.x, self.z, self.c = t // 16, (t // 4) % 4, (t // 2) % 2, t % 2
        self.up = (self.me, (t + 1) % tiles)
        self.down = (self.me, (t + tiles - 1) % tiles)
        self.mate = (1 - self.me, t)
        self.core = self.at(c=1 - self.c)
        self.y_ring = tuple(self.at(y=(self.y + k) % 4) for k in (1, 2, 3))
        self.x_ring = tuple(self.at(x=(self.x + k) % 4) for k in (1, 2, 3))
        self.z_far = (self.me, self.at(z=1 - self.z)[1])
        self.z_both = (1 - self.me, self.z_far[1])
        self.partners = (self.up, self.down, self.core, *self.y_ring, *self.x_ring,
                         self.mate, self.z_far, self.z_both)

    def at(self, y=None, x=None, z=None, c=None):
        y = self.y if y is None else y
        x = self.x if x is None else x
        z = self.z if z is None else z
        c = self.c if c is None else c
        return (self.me, y * 16 + x * 4 + z * 2 + c)


class Wire:
    def __init__(self, send, recv):
        self.send, self.recv, self.used = send, recv, 0

    def copy(self, src, dst, device):
        at = self.used
        self.used += 1
        return pltpu.make_async_remote_copy(
            src_ref=src, dst_ref=dst, send_sem=self.send.at[at], recv_sem=self.recv.at[at],
            device_id=device, device_id_type=MESH)


def add_into(dst, *others):
    total = dst[...].astype(F32)
    for o in others:
        total = total + o[...].astype(F32)
    dst[...] = total.astype(BF)


class Swap:
    def __init__(self, wire, p, others, block, buf):
        self.wire, self.p, self.others, self.block, self.buf = wire, p, others, block, buf

    def start(self):
        self.moves = [self.wire.copy(self.block((self.p + k) % 4), self.buf.at[k - 1], self.others[k - 1])
                      for k in (1, 3, 2)]
        for one in self.moves:
            one.start()

    def finish(self):
        for one in self.moves:
            one.wait()
        add_into(self.block(self.p), *[self.buf.at[k] for k in range(3)])


class Half:
    def __init__(self, place, wire, part, held, cols, y_first, bufs, zbuf):
        self.place, self.wire, self.zbuf, self.cols = place, wire, zbuf, cols
        self.part, self.held = part, held
        y, x = place.y, place.x

        on_y, on_x = (y, place.y_ring), (x, place.x_ring)
        if y_first:
            self.one = Swap(wire, *on_y, lambda d: held.at[d, :, :, :, cols], bufs[0])
            self.two = Swap(wire, *on_x, lambda d: held.at[y, d, :, :, cols], bufs[1])
        else:
            self.one = Swap(wire, *on_x, lambda d: held.at[:, d, :, :, cols], bufs[0])
            self.two = Swap(wire, *on_y, lambda d: held.at[d, x, :, :, cols], bufs[1])

    def start(self):
        cols = self.cols
        self.cross = self.wire.copy(self.part.at[1 - self.place.c, :, :, :, :, cols],
                                    self.held.at[:, :, :, :, cols], self.place.core)
        self.cross.start()

    def s1(self):
        self.cross.wait()
        cols = self.cols

        def add(yy, _):
            add_into(self.held.at[yy, :, :, :, cols], self.part.at[self.place.c, yy, :, :, :, cols])
            return 0

        lax.fori_loop(0, NY, add, 0)
        self.one.start()

    def s2(self):
        self.one.finish()
        self.two.start()

    def s3(self):
        self.two.finish()
        p = self.place
        mine = self.held.at[p.y, p.x]
        self.last = [self.wire.copy(mine.at[p.z, :, self.cols], self.zbuf.at[0], p.mate),
                     self.wire.copy(mine.at[1 - p.z, :, self.cols], self.zbuf.at[1], p.z_far),
                     self.wire.copy(mine.at[1 - p.z, :, self.cols], self.zbuf.at[2], p.z_both)]
        for one in self.last:
            one.start()

    def s4(self, scale):
        p = self.place
        for one in self.last:
            one.wait()
        total = self.held[p.y, p.x, p.z, :, self.cols].astype(F32)
        for k in range(3):
            total = total + self.zbuf[k].astype(F32)
        return total * scale


def put(part, block, cols):
    for b in range(NY * NX * NZ * NC):
        part[b % 2, b // 16, (b // 4) % 4, (b // 2) % 2, :, cols] = block[b * 16:(b + 1) * 16]


def body(scale, lat_in, grid_in, wsrc_in, wtgt_in, wmix_in, wout_in, truth_in, area_in, nbr, mask,
         d_latent_out, d_grid_out, o_src, o_tgt, o_mix, o_out,
         lat, grid, d_latent, d_grid, wsrc, wtgt, wmix, wout, truth, area,
         pick, pick_t, hits, hits_t, maskb, proj, tgt, slope, slope_sum, agg, normed, inv, ys, dys, dh, dq, dpe,
         agg_x, normed_x, grid_x, lat_x,
         halo, rims, part_src, part_tgt, part_mix, held_src, held_tgt, held_mix, *rest):
    send_sem, recv_sem, halo_send, halo_recv, rim_send, rim_recv, y_send, y_recv, load_sem = rest[-9:]
    bufs = rest[:-9]
    members, rows, width = grid.shape
    nbrs = nbr.shape[0]
    fields = wout_in.shape[0]
    ext = rows + 2 * HALO
    tiles = width // CW
    flat = members * rows
    place = Place()
    wire = Wire(send_sem, recv_sem)

    barrier = pltpu.get_barrier_semaphore()
    for partner in place.partners:
        pl.semaphore_signal(barrier, inc=1, device_id=partner, device_id_type=MESH)
    loads = [pltpu.make_async_copy(src, dst, load_sem.at[i])
             for i, (src, dst) in enumerate(((lat_in, lat), (grid_in, grid), (wtgt_in, wtgt), (wsrc_in, wsrc),
                                             (wmix_in, wmix)))]
    for one in loads:
        one.start()

    def copies(src, low, high, dst, sems, at, cols):
        return (
            pltpu.make_async_remote_copy(
                src_ref=src.at[at[0], pl.ds(high, HALO), cols], dst_ref=dst.at[at[0], pl.ds(0, HALO), cols],
                send_sem=sems[0].at[0, *at], recv_sem=sems[1].at[0, *at],
                device_id=place.up, device_id_type=MESH),
            pltpu.make_async_remote_copy(
                src_ref=src.at[at[0], pl.ds(low, HALO), cols], dst_ref=dst.at[at[0], pl.ds(HALO, HALO), cols],
                send_sem=sems[0].at[1, *at], recv_sem=sems[1].at[1, *at],
                device_id=place.down, device_id_type=MESH),
        )

    def halo_copies(m):
        return copies(lat, 0, rows - HALO, halo, (halo_send, halo_recv), (m,), slice(None))

    def rim_copies(m, c):
        return copies(dpe, 0, HALO + rows, rims, (rim_send, rim_recv), (m, c), pl.ds(c * CW, CW))

    def y_copy(m):
        return pltpu.make_async_remote_copy(
            src_ref=ys.at[m], dst_ref=ys.at[members + m],
            send_sem=y_send.at[m], recv_sem=y_recv.at[m],
            device_id=place.mate, device_id_type=MESH)

    loads[0].wait()
    pl.semaphore_wait(barrier, len(place.partners))
    for m in range(members):
        for one in halo_copies(m):
            one.start()

    truth[...] = jnp.zeros_like(truth)
    truth[0:fields, :] = truth_in[...]
    truth[...] = truth[...].T
    area[...] = jnp.broadcast_to(area_in[...], (rows, FP)).T
    wout[...] = jnp.zeros_like(wout)
    wout[0:fields, :] = wout_in[...]

    code = jnp.where(mask[...] != 0, nbr[...], -1).astype(F32)
    code_t = jnp.concatenate([code, jnp.zeros((rows - nbrs, rows), F32)], axis=0).T
    lane = lax.broadcasted_iota(jnp.int32, (rows, ext), 1).astype(F32)
    sub = lax.broadcasted_iota(jnp.int32, (ext, rows), 0).astype(F32)
    count = jnp.zeros((rows, 1), F32)
    for k in range(nbrs):
        col = code_t[:, k:k + 1]
        on = jnp.where(col >= 0.0, 1.0, 0.0)
        one = (col == lane).astype(F32).astype(BF)
        one_t = (code[k:k + 1, :] == sub).astype(F32).astype(BF)
        pick[k] = one
        maskb[k] = jnp.broadcast_to(on, (rows, 128)).astype(BF)
        count = count + on
        pick_t[:, k * rows:(k + 1) * rows] = one_t
        if k == 0:
            hits[...] = one
            hits_t[...] = one_t
        else:
            hits[...] += one
            hits_t[...] += one_t

    def columns(step, first=0, last=tiles):
        def inner(c, _):
            step(pl.ds(pl.multiple_of(c * CW, CW), CW))
            return 0

        lax.fori_loop(first, last, inner, 0)

    def own_tgt(cols):
        got = (0.5 * dot(grid[...].reshape(flat, width), wtgt[:, cols]).astype(BF)).astype(BF)
        tgt[:, :, cols] = got.reshape(members, rows, CW)

    def own_src(cols):
        got = (0.5 * dot(lat[...].reshape(flat, width), wsrc[:, cols]).astype(BF)).astype(BF)
        proj[:, HALO:HALO + rows, cols] = got.reshape(members, rows, CW)

    loads[1].wait()
    loads[2].wait()
    columns(own_tgt)
    loads[3].wait()
    columns(own_src)

    def turn_grid(m, _):
        grid_x[:, pl.ds(pl.multiple_of(m * rows, rows), rows)] = grid[m].T
        return 0

    lax.fori_loop(0, members, turn_grid, 0)
    loads[4].wait()

    gb = 32

    def forward(m, _):
        for one in halo_copies(m):
            one.wait()
        edge = (0.5 * dot(halo[m], wsrc[...]).astype(BF)).astype(BF)
        proj[m, 0:HALO] = edge[0:HALO]
        proj[m, HALO + rows:ext] = edge[HALO:2 * HALO]

        linear = dot(hits[...], proj[m]) + count * tgt[m].astype(F32)
        for at in range(0, rows, gb):
            got = dot(pick[:, at:at + gb, :].reshape(nbrs * gb, ext), proj[m]).astype(BF)
            got = got.reshape(nbrs, gb, width)
            for c in range(0, width, 256):
                cols = slice(c, c + 256)
                base = tgt[m, at:at + gb, cols]
                acc = None
                acc_s = None
                for k in range(nbrs):
                    on = maskb[k, at:at + gb, :]
                    u = got[k, :, cols] + jnp.concatenate([on, on], axis=1) * base
                    t = jnp.tanh(u)
                    p = u * t
                    s = (t + u) - t * p
                    acc = p if k == 0 else acc + p
                    acc_s = s if k == 0 else acc_s + s
                    slope[m, k, at:at + gb, cols] = s
                total = linear[at:at + gb, cols] + acc.astype(F32)
                agg[m, at:at + gb, cols] = (0.25 * total).astype(BF)
                slope_sum[m, at:at + gb, cols] = (acc_s.astype(F32) + count[at:at + gb]).astype(BF)

        h = grid[m].astype(F32) + dot(agg[m], wmix[...])
        mean = jnp.sum(h, axis=1, keepdims=True) * (1.0 / width)
        centre = h - mean
        var = jnp.sum(centre * centre, axis=1, keepdims=True) * (1.0 / width)
        r = lax.rsqrt(var + EPS)
        inv[m] = jnp.broadcast_to(r, (rows, 128))
        normed[m] = (centre * r).astype(BF)
        ys[m] = dot_nt(normed[m], wout[...])
        y_copy(m).start()
        return 0

    lax.fori_loop(0, members, forward, 0)

    def turn(m, _):
        at = pl.ds(pl.multiple_of(m * rows, rows), rows)
        agg_x[:, at] = agg[m].T
        normed_x[:, at] = normed[m].T
        around = jnp.concatenate([halo[m, 0:HALO], lat[m], halo[m, HALO:2 * HALO]], axis=0)
        lat_x[:, pl.ds(pl.multiple_of(m * ext, ext), ext)] = around.T
        return 0

    lax.fori_loop(0, members, turn, 0)

    def y_wait(m, _):
        y_copy(m).wait()
        return 0

    lax.fori_loop(0, members, y_wait, 0)

    total = 2 * members

    def head(m, _):
        y = ys[m]
        miss = y - truth[...]
        pair = jnp.zeros_like(y)
        for o in range(total):
            diff = y - ys[o]
            pair = pair + diff * lax.rsqrt(diff * diff + SMOOTH)
        grad = miss * lax.rsqrt(miss * miss + SMOOTH) * (1.0 / total)
        dy = (area[...] * (grad - (FAIR / (total * (total - 1))) * pair)).astype(BF)
        dys[m] = dy
        dn = dot(dy, wout[...])
        nh = normed[m].astype(F32)
        m1 = jnp.sum(dn, axis=1, keepdims=True) * (1.0 / width)
        m2 = jnp.sum(dn * nh, axis=1, keepdims=True) * (1.0 / width)
        dh[m] = (inv[m][:, 0:1] * (dn - m1 - nh * m2)).astype(BF)
        return 0

    lax.fori_loop(0, members, head, 0)

    halves = []
    at = 0
    for part, held, cuts in ((part_mix, held_mix, MIX_CUTS), (part_tgt, held_tgt, TGT_CUTS),
                             (part_src, held_src, SRC_CUTS)):
        for i, (first, size) in enumerate(cuts):
            halves.append(Half(place, wire, part, held, pl.ds(first, size), i % 2 == 0,
                               bufs[at:at + 2], bufs[at + 2]))
            at += 3
    mix, tgt_sum, src = halves[:2], halves[2:4], halves[4:]

    def each(parts, step):
        for one in parts:
            getattr(one, step)()

    def product(turned, right):
        return dot(turned[...], right.reshape(-1, right.shape[-1])).astype(BF)

    def mix_grad(cols):
        put(part_mix, product(agg_x, dh[:, :, cols]), cols)

    columns(mix_grad, 0, 1)
    mix[0].start()
    columns(mix_grad, 1, 2)
    put(part_mix, product(normed_x, dys[...]), pl.ds(width, FP))
    mix[1].start()

    def mix_back(cols):
        dagg = (0.125 * dot_nt(dh[...].reshape(flat, width), wmix[cols, :])).astype(BF)
        dagg = dagg.reshape(members, rows, CW)
        tgt[:, :, cols] = dagg
        dq[:, :, cols] = dagg * slope_sum[:, :, cols]

    columns(mix_back)

    def tgt_grad(cols):
        put(part_tgt, product(grid_x, dq[:, :, cols]), cols)

    columns(tgt_grad, 0, 1)
    tgt_sum[0].start()
    columns(tgt_grad, 1, 2)
    tgt_sum[1].start()
    each(mix, "s1")

    def spread(c, first, last):
        cols = pl.ds(c * CW, CW)

        def member(m, _):
            d = tgt[m, :, cols]
            for k in range(nbrs):
                slope[m, k, :, cols] = slope[m, k, :, cols] * d
            edges = slope[m, :, :, cols].reshape(nbrs * rows, CW)
            dpe[m, :, cols] = (dot(pick_t[...], edges) + dot(hits_t[...], d)).astype(BF)
            for one in rim_copies(m, c):
                one.start()
            return 0

        lax.fori_loop(first, last, member, 0)

    def src_grad(cols):
        put(part_src, product(lat_x, dpe[:, :, cols]), cols)

    def grid_back(cols):
        got = dot_nt(dq[...].reshape(flat, width), wtgt[cols, :]).reshape(members, rows, CW)
        d_grid[:, :, cols] = (dh[:, :, cols].astype(F32) + got).astype(BF)

    spread(0, 0, 2)
    each(tgt_sum, "s1")
    spread(0, 2, 4)
    each(mix, "s2")
    columns(src_grad, 0, 1)
    each(src[:2], "start")
    spread(1, 0, 2)
    each(tgt_sum, "s2")
    each(src[:2], "s1")
    spread(1, 2, 4)
    each(mix, "s3")
    columns(src_grad, 1, 2)
    each(src[2:], "start")
    each(tgt_sum, "s3")
    columns(grid_back, 0, 1)
    each(src[2:], "s1")
    each(src[:2], "s2")
    columns(grid_back, 1, 2)
    out_grid = pltpu.make_async_copy(d_grid, d_grid_out, load_sem.at[5])
    out_grid.start()
    o_mix[:, 0:512] = mix[0].s4(scale)
    last = mix[1].s4(scale)
    o_mix[:, 512:width] = last[:, 0:width - 512]
    o_out[...] = last[:, width - 512:width - 512 + fields]

    def sum_rims(m, _):
        for c in range(tiles):
            for one in rim_copies(m, c):
                one.wait()
        dq[m] = (dpe[m, HALO:HALO + rows].astype(F32) + rims[m].astype(F32)).astype(BF)
        return 0

    lax.fori_loop(0, members, sum_rims, 0)

    def latent_back(cols):
        got = dot_nt(dq[...].reshape(flat, width), wsrc[cols, :]).reshape(members, rows, CW)
        d_latent[:, :, cols] = got.astype(BF)

    columns(latent_back, 0, 1)
    each(src[:2], "s3")
    columns(latent_back, 1, 2)
    out_latent = pltpu.make_async_copy(d_latent, d_latent_out, load_sem.at[6])
    out_latent.start()
    each(src[2:], "s2")
    for one, (first, size) in zip(tgt_sum, TGT_CUTS):
        o_tgt[:, first:first + size] = one.s4(scale)
    each(src[2:], "s3")
    out_grid.wait()
    out_latent.wait()
    for one, (first, size) in zip(src, SRC_CUTS):
        o_src[:, first:first + size] = one.s4(scale)


def hand_over(arrays):
    count = len(arrays)

    def move(*refs):
        sems = refs[-1]
        moves = [pltpu.make_async_copy(refs[i], refs[count + i], sems.at[i]) for i in range(count)]
        for one in moves:
            one.start()
        for one in moves:
            one.wait()

    anywhere = pl.BlockSpec(memory_space=pl.ANY)
    return pl.pallas_call(
        move,
        out_shape=[jax.ShapeDtypeStruct(a.shape, a.dtype) for a in arrays],
        in_specs=[pl.BlockSpec(memory_space=pltpu.VMEM)] * count,
        out_specs=[anywhere] * count,
        scratch_shapes=[pltpu.SemaphoreType.DMA((count,))],
    )(*arrays)


def on_device(latent, grid_in, w_src, w_tgt, w_mix, w_out, truth, area, nbr, mask):
    members, rows, width = grid_in.shape
    nbrs = nbr.shape[0]
    fields = w_out.shape[1]
    ext = rows + 2 * HALO
    tiles = lax.axis_size("grid")
    count = members * lax.axis_size("member")
    scale = 1.0 / math.sqrt(rows * tiles * count)

    def body_(*refs):
        body(scale, *refs)

    def ring_bufs(cols):
        return [pltpu.VMEM((3, 4, 2, 16, cols), BF), pltpu.VMEM((3, 2, 16, cols), BF),
                pltpu.VMEM((3, 16, cols), BF)]

    vm = pl.BlockSpec(memory_space=pltpu.VMEM)
    hbm = pl.BlockSpec(memory_space=pl.ANY)
    sds = jax.ShapeDtypeStruct
    wide = width + FP
    halves = [size for cuts in (MIX_CUTS, TGT_CUTS, SRC_CUTS) for _, size in cuts]
    ncopies = 10 * len(halves)
    results = pl.pallas_call(
        body_,
        out_shape=[
            sds((members, rows, width), BF),
            sds((members, rows, width), BF),
            sds((16, width), F32),
            sds((16, width), F32),
            sds((16, width), F32),
            sds((16, fields), F32),
        ],
        in_specs=[hbm, hbm, hbm, hbm, hbm, vm, vm, vm, vm, vm],
        out_specs=[hbm, hbm, vm, vm, vm, vm],
        scratch_shapes=[
            pltpu.VMEM((members, rows, width), BF),
            pltpu.VMEM((members, rows, width), BF),
            pltpu.VMEM((members, rows, width), BF),
            pltpu.VMEM((members, rows, width), BF),
            pltpu.VMEM((width, width), BF),
            pltpu.VMEM((width, width), BF),
            pltpu.VMEM((width, width), BF),
            pltpu.VMEM((FP, width), BF),
            pltpu.VMEM((FP, rows), F32),
            pltpu.VMEM((rows, FP), F32),
            pltpu.VMEM((nbrs, rows, ext), BF),
            pltpu.VMEM((ext, nbrs * rows), BF),
            pltpu.VMEM((rows, ext), BF),
            pltpu.VMEM((ext, rows), BF),
            pltpu.VMEM((nbrs, rows, 128), BF),
            pltpu.VMEM((members, ext, width), BF),
            pltpu.VMEM((members, rows, width), BF),
            pltpu.VMEM((members, nbrs, rows, width), BF),
            pltpu.VMEM((members, rows, width), BF),
            pltpu.VMEM((members, rows, width), BF),
            pltpu.VMEM((members, rows, width), BF),
            pltpu.VMEM((members, rows, 128), F32),
            pltpu.VMEM((2 * members, rows, FP), F32),
            pltpu.VMEM((members, rows, FP), BF),
            pltpu.VMEM((members, rows, width), BF),
            pltpu.VMEM((members, rows, width), BF),
            pltpu.VMEM((members, ext, width), BF),
            pltpu.VMEM((width, members * rows), BF),
            pltpu.VMEM((width, members * rows), BF),
            pltpu.VMEM((width, members * rows), BF),
            pltpu.VMEM((width, members * ext), BF),
            pltpu.VMEM((members, 2 * HALO, width), BF),
            pltpu.VMEM((members, 2 * HALO, width), BF),
            pltpu.VMEM((NC, NY, NX, NZ, 16, width), BF),
            pltpu.VMEM((NC, NY, NX, NZ, 16, width), BF),
            pltpu.VMEM((NC, NY, NX, NZ, 16, wide), BF),
            pltpu.VMEM((NY, NX, NZ, 16, width), BF),
            pltpu.VMEM((NY, NX, NZ, 16, width), BF),
            pltpu.VMEM((NY, NX, NZ, 16, wide), BF),
            *[buf for cols in halves for buf in ring_bufs(cols)],
            pltpu.SemaphoreType.DMA((ncopies,)),
            pltpu.SemaphoreType.DMA((ncopies,)),
            pltpu.SemaphoreType.DMA((2, members)),
            pltpu.SemaphoreType.DMA((2, members)),
            pltpu.SemaphoreType.DMA((2, members, width // CW)),
            pltpu.SemaphoreType.DMA((2, members, width // CW)),
            pltpu.SemaphoreType.DMA((members,)),
            pltpu.SemaphoreType.DMA((members,)),
            pltpu.SemaphoreType.DMA((8,)),
        ],
        compiler_params=pltpu.CompilerParams(
            collective_id=0, has_side_effects=True, vmem_limit_bytes=63 * 2**20
        ),
        cost_estimate=pl.CostEstimate(flops=40 * 10**9, bytes_accessed=30 * 10**6, transcendentals=0),
    )(latent, grid_in, w_src, w_tgt, w_mix, w_out.T, truth, area.reshape(1, rows), nbr, mask)
    return hand_over(results)


def solution(mesh):
    in_specs = (
        P("member", "grid", None), P("member", "grid", None), P(), P(), P(), P(),
        P(None, "grid"), P("grid"), P(None, "grid"), P(None, "grid"),
    )
    out_specs = (
        P("member", "grid", None), P("member", "grid", None),
        P("grid", None), P("grid", None), P("grid", None), P("grid", None),
    )
    return jax.shard_map(
        on_device, mesh=mesh, in_specs=in_specs, out_specs=out_specs, check_vma=False
    )
```

```python
import math

import jax
import jax.numpy as jnp
from jax import lax
from jax.experimental import pallas as pl
from jax.experimental.pallas import tpu as pltpu
from jax.sharding import PartitionSpec as P

HALO = 64
SMOOTH = 0.0025
FAIR = 0.95
EPS = 1e-05
BF = jnp.bfloat16
F32 = jnp.float32
MESH = pl.DeviceIdType.MESH
CW = 512
NY, NX, NZ, NC = 4, 4, 2, 2
FP = 128
MIX_CUTS = ((0, 512), (512, 512 + FP))
TGT_CUTS = ((0, 512), (512, 512))
SRC_CUTS = ((0, 256), (256, 256), (512, 256), (768, 256))


def dot(a, b):
    return lax.dot_general(a, b, (((1,), (0,)), ((), ())), preferred_element_type=F32)


def dot_nt(a, b):
    return lax.dot_general(a, b, (((1,), (1,)), ((), ())), preferred_element_type=F32)


def dot_tn(a, b):
    return lax.dot_general(a, b, (((0,), (0,)), ((), ())), preferred_element_type=F32)


class Place:
    def __init__(self):
        self.me = lax.axis_index("member")
        t = lax.axis_index("grid")
        tiles = NY * NX * NZ * NC
        self.y, self.x, self.z, self.c = t // 16, (t // 4) % 4, (t // 2) % 2, t % 2
        self.up = (self.me, (t + 1) % tiles)
        self.down = (self.me, (t + tiles - 1) % tiles)
        self.mate = (1 - self.me, t)
        self.core = self.at(c=1 - self.c)
        self.y_ring = tuple(self.at(y=(self.y + k) % 4) for k in (1, 2, 3))
        self.x_ring = tuple(self.at(x=(self.x + k) % 4) for k in (1, 2, 3))
        self.z_far = (self.me, self.at(z=1 - self.z)[1])
        self.z_both = (1 - self.me, self.z_far[1])
        self.partners = (self.up, self.down, self.core, *self.y_ring, *self.x_ring,
                         self.mate, self.z_far, self.z_both)

    def at(self, y=None, x=None, z=None, c=None):
        y = self.y if y is None else y
        x = self.x if x is None else x
        z = self.z if z is None else z
        c = self.c if c is None else c
        return (self.me, y * 16 + x * 4 + z * 2 + c)


class Wire:
    def __init__(self, send, recv):
        self.send, self.recv, self.used = send, recv, 0

    def copy(self, src, dst, device):
        at = self.used
        self.used += 1
        return pltpu.make_async_remote_copy(
            src_ref=src, dst_ref=dst, send_sem=self.send.at[at], recv_sem=self.recv.at[at],
            device_id=device, device_id_type=MESH)


def add_into(dst, *others):
    total = dst[...].astype(F32)
    for o in others:
        total = total + o[...].astype(F32)
    dst[...] = total.astype(BF)


class Swap:
    def __init__(self, wire, p, others, block, buf):
        self.wire, self.p, self.others, self.block, self.buf = wire, p, others, block, buf

    def start(self):
        self.moves = [self.wire.copy(self.block((self.p + k) % 4), self.buf.at[k - 1], self.others[k - 1])
                      for k in (1, 3, 2)]
        for one in self.moves:
            one.start()

    def finish(self):
        for one in self.moves:
            one.wait()
        add_into(self.block(self.p), *[self.buf.at[k] for k in range(3)])


class Half:
    def __init__(self, place, wire, y_first, part, held, wide, thin, zbuf):
        self.place, self.wire, self.zbuf = place, wire, zbuf
        self.part, self.held = part, held
        y, x = place.y, place.x
        on_y, on_x = (y, place.y_ring), (x, place.x_ring)
        if y_first:
            self.one = Swap(wire, *on_y, lambda d: held.at[d], wide)
            self.two = Swap(wire, *on_x, lambda d: held.at[y, d], thin)
        else:
            self.one = Swap(wire, *on_x, lambda d: held.at[:, d], wide)
            self.two = Swap(wire, *on_y, lambda d: held.at[d, x], thin)

    def start(self):
        self.cross = self.wire.copy(self.part.at[1 - self.place.c], self.held, self.place.core)
        self.cross.start()

    def s1(self):
        self.cross.wait()

        def add(yy, _):
            add_into(self.held.at[yy], self.part.at[self.place.c, yy])
            return 0

        lax.fori_loop(0, NY, add, 0)
        self.one.start()

    def s2(self):
        self.one.finish()
        self.two.start()

    def s3(self):
        self.two.finish()
        p = self.place
        mine = self.held.at[p.y, p.x]
        self.last = [self.wire.copy(mine.at[p.z], self.zbuf.at[0], p.mate),
                     self.wire.copy(mine.at[1 - p.z], self.zbuf.at[1], p.z_far),
                     self.wire.copy(mine.at[1 - p.z], self.zbuf.at[2], p.z_both)]
        for one in self.last:
            one.start()

    def s4(self, scale):
        p = self.place
        for one in self.last:
            one.wait()
        total = self.held[p.y, p.x, p.z].astype(F32)
        for k in range(3):
            total = total + self.zbuf[k].astype(F32)
        return total * scale


def put(part, block, first=0):
    cols = slice(first, first + block.shape[1])
    for b in range(NY * NX * NZ * NC):
        part[b % 2, b // 16, (b // 4) % 4, (b // 2) % 2, :, cols] = block[b * 16:(b + 1) * 16]


def body(scale, lat_in, grid_in, wsrc_in, wtgt_in, wmix_in, wout_in, truth_in, area_in, nbr, mask,
         d_latent_out, d_grid_out, o_src, o_tgt, o_mix, o_out,
         lat, grid, d_latent, d_grid, wsrc, wtgt, wmix, wout, truth, area,
         pick, pick_t, hits, hits_t, maskb, proj, tgt, slope, slope_sum, agg, normed, inv, ys, dys, dh, dq, dpe,
         agg_x, normed_x, grid_x, lat_x,
         halo, rims, *rest):
    send_sem, recv_sem, halo_send, halo_recv, rim_send, rim_recv, y_send, y_recv, load_sem = rest[-9:]
    bufs = rest[:-9]
    members, rows, width = grid.shape
    nbrs = nbr.shape[0]
    fields = wout_in.shape[0]
    ext = rows + 2 * HALO
    tiles = width // CW
    flat = members * rows
    place = Place()
    wire = Wire(send_sem, recv_sem)

    barrier = pltpu.get_barrier_semaphore()
    for partner in place.partners:
        pl.semaphore_signal(barrier, inc=1, device_id=partner, device_id_type=MESH)
    loads = [pltpu.make_async_copy(src, dst, load_sem.at[i])
             for i, (src, dst) in enumerate(((lat_in, lat), (grid_in, grid), (wtgt_in, wtgt), (wsrc_in, wsrc),
                                             (wmix_in, wmix)))]
    for one in loads:
        one.start()

    def copies(src, low, high, dst, sems, at, cols):
        return (
            pltpu.make_async_remote_copy(
                src_ref=src.at[at[0], pl.ds(high, HALO), cols], dst_ref=dst.at[at[0], pl.ds(0, HALO), cols],
                send_sem=sems[0].at[0, *at], recv_sem=sems[1].at[0, *at],
                device_id=place.up, device_id_type=MESH),
            pltpu.make_async_remote_copy(
                src_ref=src.at[at[0], pl.ds(low, HALO), cols], dst_ref=dst.at[at[0], pl.ds(HALO, HALO), cols],
                send_sem=sems[0].at[1, *at], recv_sem=sems[1].at[1, *at],
                device_id=place.down, device_id_type=MESH),
        )

    def halo_copies(m):
        return copies(lat, 0, rows - HALO, halo, (halo_send, halo_recv), (m,), slice(None))

    def rim_copies(m, c):
        return copies(dpe, 0, HALO + rows, rims, (rim_send, rim_recv), (m, c), pl.ds(c * CW, CW))

    def y_copy(m):
        return pltpu.make_async_remote_copy(
            src_ref=ys.at[m], dst_ref=ys.at[members + m],
            send_sem=y_send.at[m], recv_sem=y_recv.at[m],
            device_id=place.mate, device_id_type=MESH)

    loads[0].wait()
    pl.semaphore_wait(barrier, len(place.partners))
    for m in range(members):
        for one in halo_copies(m):
            one.start()

    truth[...] = jnp.zeros_like(truth)
    truth[0:fields, :] = truth_in[...]
    truth[...] = truth[...].T
    area[...] = jnp.broadcast_to(area_in[...], (rows, FP)).T
    wout[...] = jnp.zeros_like(wout)
    wout[0:fields, :] = wout_in[...]

    code = jnp.where(mask[...] != 0, nbr[...], -1).astype(F32)
    code_t = jnp.concatenate([code, jnp.zeros((rows - nbrs, rows), F32)], axis=0).T
    lane = lax.broadcasted_iota(jnp.int32, (rows, ext), 1).astype(F32)
    sub = lax.broadcasted_iota(jnp.int32, (ext, rows), 0).astype(F32)
    count = jnp.zeros((rows, 1), F32)
    for k in range(nbrs):
        col = code_t[:, k:k + 1]
        on = jnp.where(col >= 0.0, 1.0, 0.0)
        one = (col == lane).astype(F32).astype(BF)
        one_t = (code[k:k + 1, :] == sub).astype(F32).astype(BF)
        pick[k] = one
        maskb[k] = jnp.broadcast_to(on, (rows, 128)).astype(BF)
        count = count + on
        pick_t[:, k * rows:(k + 1) * rows] = one_t
        if k == 0:
            hits[...] = one
            hits_t[...] = one_t
        else:
            hits[...] += one
            hits_t[...] += one_t

    def columns(step, first=0, last=tiles):
        def inner(c, _):
            step(pl.ds(pl.multiple_of(c * CW, CW), CW))
            return 0

        lax.fori_loop(first, last, inner, 0)

    def own_tgt(cols):
        got = (0.5 * dot(grid[...].reshape(flat, width), wtgt[:, cols]).astype(BF)).astype(BF)
        tgt[:, :, cols] = got.reshape(members, rows, CW)

    def own_src(cols):
        got = (0.5 * dot(lat[...].reshape(flat, width), wsrc[:, cols]).astype(BF)).astype(BF)
        proj[:, HALO:HALO + rows, cols] = got.reshape(members, rows, CW)

    loads[1].wait()
    loads[2].wait()
    columns(own_tgt)
    loads[3].wait()
    columns(own_src)

    def turn_grid(m, _):
        grid_x[:, pl.ds(pl.multiple_of(m * rows, rows), rows)] = grid[m].T
        return 0

    lax.fori_loop(0, members, turn_grid, 0)
    loads[4].wait()

    gb = 32

    def forward(m, _):
        for one in halo_copies(m):
            one.wait()
        edge = (0.5 * dot(halo[m], wsrc[...]).astype(BF)).astype(BF)
        proj[m, 0:HALO] = edge[0:HALO]
        proj[m, HALO + rows:ext] = edge[HALO:2 * HALO]

        linear = dot(hits[...], proj[m]) + count * tgt[m].astype(F32)
        for at in range(0, rows, gb):
            got = dot(pick[:, at:at + gb, :].reshape(nbrs * gb, ext), proj[m]).astype(BF)
            got = got.reshape(nbrs, gb, width)
            for c in range(0, width, 256):
                cols = slice(c, c + 256)
                base = tgt[m, at:at + gb, cols]
                acc = None
                acc_s = None
                for k in range(nbrs):
                    on = maskb[k, at:at + gb, :]
                    u = got[k, :, cols] + jnp.concatenate([on, on], axis=1) * base
                    t = jnp.tanh(u)
                    p = u * t
                    s = (t + u) - t * p
                    acc = p if k == 0 else acc + p
                    acc_s = s if k == 0 else acc_s + s
                    slope[m, k, at:at + gb, cols] = s
                total = linear[at:at + gb, cols] + acc.astype(F32)
                agg[m, at:at + gb, cols] = (0.25 * total).astype(BF)
                slope_sum[m, at:at + gb, cols] = (acc_s.astype(F32) + count[at:at + gb]).astype(BF)

        h = grid[m].astype(F32) + dot(agg[m], wmix[...])
        mean = jnp.sum(h, axis=1, keepdims=True) * (1.0 / width)
        centre = h - mean
        var = jnp.sum(centre * centre, axis=1, keepdims=True) * (1.0 / width)
        r = lax.rsqrt(var + EPS)
        inv[m] = jnp.broadcast_to(r, (rows, 128))
        normed[m] = (centre * r).astype(BF)
        ys[m] = dot_nt(normed[m], wout[...])
        y_copy(m).start()
        return 0

    lax.fori_loop(0, members, forward, 0)

    def turn(m, _):
        at = pl.ds(pl.multiple_of(m * rows, rows), rows)
        agg_x[:, at] = agg[m].T
        normed_x[:, at] = normed[m].T
        around = jnp.concatenate([halo[m, 0:HALO], lat[m], halo[m, HALO:2 * HALO]], axis=0)
        lat_x[:, pl.ds(pl.multiple_of(m * ext, ext), ext)] = around.T
        return 0

    lax.fori_loop(0, members, turn, 0)

    def y_wait(m, _):
        y_copy(m).wait()
        return 0

    lax.fori_loop(0, members, y_wait, 0)

    total = 2 * members

    def head(m, _):
        y = ys[m]
        miss = y - truth[...]
        pair = jnp.zeros_like(y)
        for o in range(total):
            diff = y - ys[o]
            pair = pair + diff * lax.rsqrt(diff * diff + SMOOTH)
        grad = miss * lax.rsqrt(miss * miss + SMOOTH) * (1.0 / total)
        dy = (area[...] * (grad - (FAIR / (total * (total - 1))) * pair)).astype(BF)
        dys[m] = dy
        dn = dot(dy, wout[...])
        nh = normed[m].astype(F32)
        m1 = jnp.sum(dn, axis=1, keepdims=True) * (1.0 / width)
        m2 = jnp.sum(dn * nh, axis=1, keepdims=True) * (1.0 / width)
        dh[m] = (inv[m][:, 0:1] * (dn - m1 - nh * m2)).astype(BF)
        return 0

    lax.fori_loop(0, members, head, 0)

    halves = [Half(place, wire, i % 2 == 0, *bufs[5 * i:5 * i + 5]) for i in range(len(bufs) // 5)]
    mix, tgt_sum, src = halves[:2], halves[2:4], halves[4:]

    def each(parts, step):
        for one in parts:
            getattr(one, step)()

    def product(turned, right):
        return dot(turned[...], right.reshape(-1, right.shape[-1])).astype(BF)

    def mix_grad(cols):
        return product(agg_x, dh[:, :, cols])

    put(mix[0].part, mix_grad(pl.ds(0, CW)))
    mix[0].start()
    put(mix[1].part, mix_grad(pl.ds(CW, CW)))
    put(mix[1].part, product(normed_x, dys[...]), CW)
    mix[1].start()

    def mix_back(cols):
        dagg = (0.125 * dot_nt(dh[...].reshape(flat, width), wmix[cols, :])).astype(BF)
        dagg = dagg.reshape(members, rows, CW)
        tgt[:, :, cols] = dagg
        dq[:, :, cols] = dagg * slope_sum[:, :, cols]

    columns(mix_back)

    def tgt_grad(cols):
        return product(grid_x, dq[:, :, cols])

    put(tgt_sum[0].part, tgt_grad(pl.ds(0, CW)))
    tgt_sum[0].start()
    put(tgt_sum[1].part, tgt_grad(pl.ds(CW, CW)))
    tgt_sum[1].start()
    each(mix, "s1")

    def spread(c, first, last):
        cols = pl.ds(c * CW, CW)

        def member(m, _):
            d = tgt[m, :, cols]
            for k in range(nbrs):
                slope[m, k, :, cols] = slope[m, k, :, cols] * d
            edges = slope[m, :, :, cols].reshape(nbrs * rows, CW)
            dpe[m, :, cols] = (dot(pick_t[...], edges) + dot(hits_t[...], d)).astype(BF)
            for one in rim_copies(m, c):
                one.start()
            return 0

        lax.fori_loop(first, last, member, 0)

    def src_grad(c):
        block = product(lat_x, dpe[:, :, c * CW:(c + 1) * CW])
        for i in range(2):
            put(src[2 * c + i].part, block[:, i * 256:(i + 1) * 256])

    def grid_back(cols):
        got = dot_nt(dq[...].reshape(flat, width), wtgt[cols, :]).reshape(members, rows, CW)
        d_grid[:, :, cols] = (dh[:, :, cols].astype(F32) + got).astype(BF)

    spread(0, 0, 2)
    each(tgt_sum, "s1")
    spread(0, 2, 4)
    each(mix, "s2")
    src_grad(0)
    each(src[:2], "start")
    spread(1, 0, 2)
    each(tgt_sum, "s2")
    each(src[:2], "s1")
    spread(1, 2, 4)
    each(mix, "s3")
    src_grad(1)
    each(src[2:], "start")
    each(tgt_sum, "s3")
    columns(grid_back, 0, 1)
    each(src[2:], "s1")
    each(src[:2], "s2")
    columns(grid_back, 1, 2)
    out_grid = pltpu.make_async_copy(d_grid, d_grid_out, load_sem.at[5])
    out_grid.start()
    o_mix[:, 0:512] = mix[0].s4(scale)
    last = mix[1].s4(scale)
    o_mix[:, 512:width] = last[:, 0:width - 512]
    o_out[...] = last[:, width - 512:width - 512 + fields]

    def sum_rims(m, _):
        for c in range(tiles):
            for one in rim_copies(m, c):
                one.wait()
        dq[m] = (dpe[m, HALO:HALO + rows].astype(F32) + rims[m].astype(F32)).astype(BF)
        return 0

    lax.fori_loop(0, members, sum_rims, 0)

    def latent_back(cols):
        got = dot_nt(dq[...].reshape(flat, width), wsrc[cols, :]).reshape(members, rows, CW)
        d_latent[:, :, cols] = got.astype(BF)

    columns(latent_back, 0, 1)
    each(src[:2], "s3")
    columns(latent_back, 1, 2)
    out_latent = pltpu.make_async_copy(d_latent, d_latent_out, load_sem.at[6])
    out_latent.start()
    each(src[2:], "s2")
    for one, (first, size) in zip(tgt_sum, TGT_CUTS):
        o_tgt[:, first:first + size] = one.s4(scale)
    each(src[2:], "s3")
    out_grid.wait()
    out_latent.wait()
    for one, (first, size) in zip(src, SRC_CUTS):
        o_src[:, first:first + size] = one.s4(scale)


def hand_over(arrays):
    count = len(arrays)

    def move(*refs):
        sems = refs[-1]
        moves = [pltpu.make_async_copy(refs[i], refs[count + i], sems.at[i]) for i in range(count)]
        for one in moves:
            one.start()
        for one in moves:
            one.wait()

    anywhere = pl.BlockSpec(memory_space=pl.ANY)
    return pl.pallas_call(
        move,
        out_shape=[jax.ShapeDtypeStruct(a.shape, a.dtype) for a in arrays],
        in_specs=[pl.BlockSpec(memory_space=pltpu.VMEM)] * count,
        out_specs=[anywhere] * count,
        scratch_shapes=[pltpu.SemaphoreType.DMA((count,))],
    )(*arrays)


def on_device(latent, grid_in, w_src, w_tgt, w_mix, w_out, truth, area, nbr, mask):
    members, rows, width = grid_in.shape
    nbrs = nbr.shape[0]
    fields = w_out.shape[1]
    ext = rows + 2 * HALO
    tiles = lax.axis_size("grid")
    count = members * lax.axis_size("member")
    scale = 1.0 / math.sqrt(rows * tiles * count)

    def body_(*refs):
        body(scale, *refs)

    def ring_bufs(cols):
        return [pltpu.VMEM((NC, NY, NX, NZ, 16, cols), BF), pltpu.VMEM((NY, NX, NZ, 16, cols), BF),
                pltpu.VMEM((3, 4, NZ, 16, cols), BF), pltpu.VMEM((3, NZ, 16, cols), BF),
                pltpu.VMEM((3, 16, cols), BF)]

    vm = pl.BlockSpec(memory_space=pltpu.VMEM)
    hbm = pl.BlockSpec(memory_space=pl.ANY)
    sds = jax.ShapeDtypeStruct
    halves = [size for cuts in (MIX_CUTS, TGT_CUTS, SRC_CUTS) for _, size in cuts]
    ncopies = 10 * len(halves)
    results = pl.pallas_call(
        body_,
        out_shape=[
            sds((members, rows, width), BF),
            sds((members, rows, width), BF),
            sds((16, width), F32),
            sds((16, width), F32),
            sds((16, width), F32),
            sds((16, fields), F32),
        ],
        in_specs=[hbm, hbm, hbm, hbm, hbm, vm, vm, vm, vm, vm],
        out_specs=[hbm, hbm, vm, vm, vm, vm],
        scratch_shapes=[
            pltpu.VMEM((members, rows, width), BF),
            pltpu.VMEM((members, rows, width), BF),
            pltpu.VMEM((members, rows, width), BF),
            pltpu.VMEM((members, rows, width), BF),
            pltpu.VMEM((width, width), BF),
            pltpu.VMEM((width, width), BF),
            pltpu.VMEM((width, width), BF),
            pltpu.VMEM((FP, width), BF),
            pltpu.VMEM((FP, rows), F32),
            pltpu.VMEM((rows, FP), F32),
            pltpu.VMEM((nbrs, rows, ext), BF),
            pltpu.VMEM((ext, nbrs * rows), BF),
            pltpu.VMEM((rows, ext), BF),
            pltpu.VMEM((ext, rows), BF),
            pltpu.VMEM((nbrs, rows, 128), BF),
            pltpu.VMEM((members, ext, width), BF),
            pltpu.VMEM((members, rows, width), BF),
            pltpu.VMEM((members, nbrs, rows, width), BF),
            pltpu.VMEM((members, rows, width), BF),
            pltpu.VMEM((members, rows, width), BF),
            pltpu.VMEM((members, rows, width), BF),
            pltpu.VMEM((members, rows, 128), F32),
            pltpu.VMEM((2 * members, rows, FP), F32),
            pltpu.VMEM((members, rows, FP), BF),
            pltpu.VMEM((members, rows, width), BF),
            pltpu.VMEM((members, rows, width), BF),
            pltpu.VMEM((members, ext, width), BF),
            pltpu.VMEM((width, members * rows), BF),
            pltpu.VMEM((width, members * rows), BF),
            pltpu.VMEM((width, members * rows), BF),
            pltpu.VMEM((width, members * ext), BF),
            pltpu.VMEM((members, 2 * HALO, width), BF),
            pltpu.VMEM((members, 2 * HALO, width), BF),
            *[buf for cols in halves for buf in ring_bufs(cols)],
            pltpu.SemaphoreType.DMA((ncopies,)),
            pltpu.SemaphoreType.DMA((ncopies,)),
            pltpu.SemaphoreType.DMA((2, members)),
            pltpu.SemaphoreType.DMA((2, members)),
            pltpu.SemaphoreType.DMA((2, members, width // CW)),
            pltpu.SemaphoreType.DMA((2, members, width // CW)),
            pltpu.SemaphoreType.DMA((members,)),
            pltpu.SemaphoreType.DMA((members,)),
            pltpu.SemaphoreType.DMA((8,)),
        ],
        compiler_params=pltpu.CompilerParams(
            collective_id=0, has_side_effects=True, vmem_limit_bytes=63 * 2**20
        ),
        cost_estimate=pl.CostEstimate(flops=40 * 10**9, bytes_accessed=30 * 10**6, transcendentals=0),
    )(latent, grid_in, w_src, w_tgt, w_mix, w_out.T, truth, area.reshape(1, rows), nbr, mask)
    return hand_over(results)


def solution(mesh):
    in_specs = (
        P("member", "grid", None), P("member", "grid", None), P(), P(), P(), P(),
        P(None, "grid"), P("grid"), P(None, "grid"), P(None, "grid"),
    )
    out_specs = (
        P("member", "grid", None), P("member", "grid", None),
        P("grid", None), P("grid", None), P("grid", None), P("grid", None),
    )
    return jax.shard_map(
        on_device, mesh=mesh, in_specs=in_specs, out_specs=out_specs, check_vma=False
    )
```

```python
import math

import jax
import jax.numpy as jnp
from jax import lax
from jax.experimental import pallas as pl
from jax.experimental.pallas import tpu as pltpu
from jax.sharding import PartitionSpec as P

HALO = 64
SMOOTH = 0.0025
FAIR = 0.95
EPS = 1e-05
BF = jnp.bfloat16
F32 = jnp.float32
MESH = pl.DeviceIdType.MESH
CW = 512
NY, NX, NZ, NC = 4, 4, 2, 2
FP = 128
MIX_CUTS = ((0, 512), (512, 512 + FP))
TGT_CUTS = ((0, 512), (512, 512))
SRC_CUTS = ((0, 512), (512, 512))


def dot(a, b):
    return lax.dot_general(a, b, (((1,), (0,)), ((), ())), preferred_element_type=F32)


def dot_nt(a, b):
    return lax.dot_general(a, b, (((1,), (1,)), ((), ())), preferred_element_type=F32)


def dot_tn(a, b):
    return lax.dot_general(a, b, (((0,), (0,)), ((), ())), preferred_element_type=F32)


class Place:
    def __init__(self):
        self.me = lax.axis_index("member")
        t = lax.axis_index("grid")
        tiles = NY * NX * NZ * NC
        self.y, self.x, self.z, self.c = t // 16, (t // 4) % 4, (t // 2) % 2, t % 2
        step = 2 * self.c - 1
        far = (t + step + tiles) % tiles
        turned = self.at(z=1 - self.z)[1]
        self.by_mate = (1 - self.me, far)
        self.by_both = (1 - self.me, (turned + step + tiles) % tiles)
        from_both = (1 - self.me, far + 2 - 4 * ((far // 2) % 2))
        self.mate = (1 - self.me, t)
        self.core = self.at(c=1 - self.c)
        self.y_ring = tuple(self.at(y=(self.y + k) % 4) for k in (1, 2, 3))
        self.x_ring = tuple(self.at(x=(self.x + k) % 4) for k in (1, 2, 3))
        self.z_far = (self.me, self.at(z=1 - self.z)[1])
        self.z_both = (1 - self.me, self.z_far[1])
        self.partners = (self.core, *self.y_ring, *self.x_ring, self.mate, self.z_far, self.z_both,
                         self.by_mate, from_both)

    def at(self, y=None, x=None, z=None, c=None):
        y = self.y if y is None else y
        x = self.x if x is None else x
        z = self.z if z is None else z
        c = self.c if c is None else c
        return (self.me, y * 16 + x * 4 + z * 2 + c)


class Wire:
    def __init__(self, send, recv):
        self.send, self.recv, self.used = send, recv, 0

    def copy(self, src, dst, device):
        at = self.used
        self.used += 1
        return pltpu.make_async_remote_copy(
            src_ref=src, dst_ref=dst, send_sem=self.send.at[at], recv_sem=self.recv.at[at],
            device_id=device, device_id_type=MESH)


def add_into(dst, *others):
    total = dst[...].astype(F32)
    for o in others:
        total = total + o[...].astype(F32)
    dst[...] = total.astype(BF)


class Swap:
    def __init__(self, wire, p, others, block, buf):
        self.wire, self.p, self.others, self.block, self.buf = wire, p, others, block, buf

    def start(self):
        self.moves = [self.wire.copy(self.block((self.p + k) % 4), self.buf.at[k - 1], self.others[k - 1])
                      for k in (1, 3, 2)]
        for one in self.moves:
            one.start()

    def finish(self):
        for one in self.moves:
            one.wait()
        add_into(self.block(self.p), *[self.buf.at[k] for k in range(3)])


class Half:
    def __init__(self, place, wire, y_first, part, held, wide, thin, zbuf):
        self.place, self.wire, self.zbuf = place, wire, zbuf
        self.part, self.held = part, held
        y, x = place.y, place.x
        on_y, on_x = (y, place.y_ring), (x, place.x_ring)
        if y_first:
            self.one = Swap(wire, *on_y, lambda d: held.at[d], wide)
            self.two = Swap(wire, *on_x, lambda d: held.at[y, d], thin)
        else:
            self.one = Swap(wire, *on_x, lambda d: held.at[:, d], wide)
            self.two = Swap(wire, *on_y, lambda d: held.at[d, x], thin)

    def start(self):
        self.cross = self.wire.copy(self.part.at[1 - self.place.c], self.held, self.place.core)
        self.cross.start()

    def s1(self):
        self.cross.wait()

        def add(yy, _):
            add_into(self.held.at[yy], self.part.at[self.place.c, yy])
            return 0

        lax.fori_loop(0, NY, add, 0)
        self.one.start()

    def s2(self):
        self.one.finish()
        self.two.start()

    def s3(self):
        self.two.finish()
        p = self.place
        mine = self.held.at[p.y, p.x]
        self.last = [self.wire.copy(mine.at[p.z], self.zbuf.at[0], p.mate),
                     self.wire.copy(mine.at[1 - p.z], self.zbuf.at[1], p.z_far),
                     self.wire.copy(mine.at[1 - p.z], self.zbuf.at[2], p.z_both)]
        for one in self.last:
            one.start()

    def s4(self, scale):
        p = self.place
        for one in self.last:
            one.wait()
        total = self.held[p.y, p.x, p.z].astype(F32)
        for k in range(3):
            total = total + self.zbuf[k].astype(F32)
        return total * scale


def put(part, block, first=0):
    cols = slice(first, first + block.shape[1])
    for b in range(NY * NX * NZ * NC):
        part[b % 2, b // 16, (b // 4) % 4, (b // 2) % 2, :, cols] = block[b * 16:(b + 1) * 16]


def body(scale, lat_in, grid_in, wsrc_in, wtgt_in, wmix_in, wout_in, truth_in, area_in, nbr, mask,
         d_latent_out, d_grid_out, o_src, o_tgt, o_mix, o_out,
         lat, grid, wsrc, wtgt, wmix, wout, truth, area,
         pick, pick_t, hits, hits_t, maskb, proj, tgt, slope, slope_sum, agg, normed, inv, ys, dys, dh, dq, dpe,
         agg_x, normed_x, grid_x, lat_x,
         halo, rims, halo_hop, rim_hop, *rest):
    send_sem, recv_sem, halo_send, halo_recv, rim_send, rim_recv, y_send, y_recv, load_sem = rest[-9:]
    bufs = rest[:-9]
    members, rows, width = grid.shape
    nbrs = nbr.shape[0]
    fields = wout_in.shape[0]
    ext = rows + 2 * HALO
    tiles = width // CW
    flat = members * rows
    d_latent, d_grid = agg, normed
    place = Place()
    wire = Wire(send_sem, recv_sem)

    barrier = pltpu.get_barrier_semaphore()
    for partner in place.partners:
        pl.semaphore_signal(barrier, inc=1, device_id=partner, device_id_type=MESH)
    loads = [pltpu.make_async_copy(src, dst, load_sem.at[i])
             for i, (src, dst) in enumerate(((lat_in, lat), (grid_in, grid), (wtgt_in, wtgt), (wsrc_in, wsrc),
                                             (wmix_in, wmix)))]
    for one in loads:
        one.start()

    def remote(src, dst, send, recv, device):
        return pltpu.make_async_remote_copy(src_ref=src, dst_ref=dst, send_sem=send, recv_sem=recv,
                                            device_id=device, device_id_type=MESH)

    class Edge:
        def __init__(self, src, length, dst, hop, sems):
            self.src, self.dst, self.hop = src, dst, hop
            self.last = length - HALO
            self.send, self.recv = sems

        def near(self, m):
            c = place.c
            return remote(self.src.at[m, pl.ds((1 - c) * self.last, HALO)],
                          self.dst.at[m, pl.ds(c * HALO, HALO)],
                          self.send.at[0, m], self.recv.at[0, m], place.core)

        def first(self, m, r):
            part = pl.ds(place.c * self.last + r * (HALO // 2), HALO // 2)
            return remote(self.src.at[m, part], self.hop.at[r, m], self.send.at[1 + r, m], self.recv.at[1 + r, m],
                          (place.mate, place.z_both)[r])

        def second(self, m, r):
            part = pl.ds((1 - place.c) * HALO + r * (HALO // 2), HALO // 2)
            return remote(self.hop.at[r, m], self.dst.at[m, part], self.send.at[3 + r, m], self.recv.at[3 + r, m],
                          (place.by_mate, place.by_both)[r])

        def start(self, m):
            self.first(m, 0).start()
            self.first(m, 1).start()
            self.near(m).start()

        def relay(self, m):
            for r in range(2):
                self.first(m, r).wait()
                self.second(m, r).start()

        def wait(self, m):
            self.near(m).wait()
            self.second(m, 0).wait()
            self.second(m, 1).wait()

    halo_rows = Edge(lat, rows, halo, halo_hop, (halo_send, halo_recv))
    rim_rows = Edge(dpe, ext, rims, rim_hop, (rim_send, rim_recv))

    def y_copy(m):
        return pltpu.make_async_remote_copy(
            src_ref=ys.at[m], dst_ref=ys.at[members + m],
            send_sem=y_send.at[m], recv_sem=y_recv.at[m],
            device_id=place.mate, device_id_type=MESH)

    loads[0].wait()
    pl.semaphore_wait(barrier, len(place.partners))
    for m in range(members):
        halo_rows.start(m)

    truth[...] = jnp.zeros_like(truth)
    truth[0:fields, :] = truth_in[...]
    truth[...] = truth[...].T
    area[...] = jnp.broadcast_to(area_in[...], (rows, FP)).T
    wout[...] = jnp.zeros_like(wout)
    wout[0:fields, :] = wout_in[...]

    code = jnp.where(mask[...] != 0, nbr[...], -1).astype(F32)
    code_t = jnp.concatenate([code, jnp.zeros((rows - nbrs, rows), F32)], axis=0).T
    lane = lax.broadcasted_iota(jnp.int32, (rows, ext), 1).astype(F32)
    sub = lax.broadcasted_iota(jnp.int32, (ext, rows), 0).astype(F32)
    count = jnp.zeros((rows, 1), F32)
    for k in range(nbrs):
        col = code_t[:, k:k + 1]
        on = jnp.where(col >= 0.0, 1.0, 0.0)
        one = (col == lane).astype(F32).astype(BF)
        one_t = (code[k:k + 1, :] == sub).astype(F32).astype(BF)
        pick[k] = one
        maskb[k] = jnp.broadcast_to(on, (rows, 128)).astype(BF)
        count = count + on
        pick_t[:, k * rows:(k + 1) * rows] = one_t
        if k == 0:
            hits[...] = one
            hits_t[...] = one_t
        else:
            hits[...] += one
            hits_t[...] += one_t

    def columns(step, first=0, last=tiles):
        def inner(c, _):
            step(pl.ds(pl.multiple_of(c * CW, CW), CW))
            return 0

        lax.fori_loop(first, last, inner, 0)

    def own_tgt(cols):
        got = (0.5 * dot(grid[...].reshape(flat, width), wtgt[:, cols]).astype(BF)).astype(BF)
        tgt[:, :, cols] = got.reshape(members, rows, CW)

    def own_src(cols):
        got = (0.5 * dot(lat[...].reshape(flat, width), wsrc[:, cols]).astype(BF)).astype(BF)
        proj[:, HALO:HALO + rows, cols] = got.reshape(members, rows, CW)

    halo_rows.relay(0)
    loads[1].wait()
    loads[2].wait()
    columns(own_tgt)
    halo_rows.relay(1)
    loads[3].wait()
    columns(own_src)
    halo_rows.relay(2)

    def turn_grid(m, _):
        grid_x[:, pl.ds(pl.multiple_of(m * rows, rows), rows)] = grid[m].T
        return 0

    lax.fori_loop(0, members, turn_grid, 0)
    halo_rows.relay(3)
    loads[4].wait()

    gb = 32

    def forward(m, _):
        halo_rows.wait(m)
        edge = (0.5 * dot(halo[m], wsrc[...]).astype(BF)).astype(BF)
        proj[m, 0:HALO] = edge[0:HALO]
        proj[m, HALO + rows:ext] = edge[HALO:2 * HALO]

        linear = dot(hits[...], proj[m]) + count * tgt[m].astype(F32)
        for at in range(0, rows, gb):
            got = dot(pick[:, at:at + gb, :].reshape(nbrs * gb, ext), proj[m]).astype(BF)
            got = got.reshape(nbrs, gb, width)
            for c in range(0, width, 256):
                cols = slice(c, c + 256)
                base = tgt[m, at:at + gb, cols]
                acc = None
                acc_s = None
                for k in range(nbrs):
                    on = maskb[k, at:at + gb, :]
                    u = got[k, :, cols] + jnp.concatenate([on, on], axis=1) * base
                    t = jnp.tanh(u)
                    p = u * t
                    s = (t + u) - t * p
                    acc = p if k == 0 else acc + p
                    acc_s = s if k == 0 else acc_s + s
                    slope[m, k, at:at + gb, cols] = s
                total = linear[at:at + gb, cols] + acc.astype(F32)
                agg[m, at:at + gb, cols] = (0.25 * total).astype(BF)
                slope_sum[m, at:at + gb, cols] = (acc_s.astype(F32) + count[at:at + gb]).astype(BF)

        h = grid[m].astype(F32) + dot(agg[m], wmix[...])
        mean = jnp.sum(h, axis=1, keepdims=True) * (1.0 / width)
        centre = h - mean
        var = jnp.sum(centre * centre, axis=1, keepdims=True) * (1.0 / width)
        r = lax.rsqrt(var + EPS)
        inv[m] = jnp.broadcast_to(r, (rows, 128))
        normed[m] = (centre * r).astype(BF)
        ys[m] = dot_nt(normed[m], wout[...])
        y_copy(m).start()
        return 0

    lax.fori_loop(0, members, forward, 0)

    def turn(m, _):
        at = pl.ds(pl.multiple_of(m * rows, rows), rows)
        agg_x[:, at] = agg[m].T
        normed_x[:, at] = normed[m].T
        around = jnp.concatenate([halo[m, 0:HALO], lat[m], halo[m, HALO:2 * HALO]], axis=0)
        lat_x[:, pl.ds(pl.multiple_of(m * ext, ext), ext)] = around.T
        return 0

    lax.fori_loop(0, members, turn, 0)

    def y_wait(m, _):
        y_copy(m).wait()
        return 0

    lax.fori_loop(0, members, y_wait, 0)

    total = 2 * members

    def head(m, _):
        y = ys[m]
        miss = y - truth[...]
        pair = jnp.zeros_like(y)
        for o in range(total):
            diff = y - ys[o]
            pair = pair + diff * lax.rsqrt(diff * diff + SMOOTH)
        grad = miss * lax.rsqrt(miss * miss + SMOOTH) * (1.0 / total)
        dy = (area[...] * (grad - (FAIR / (total * (total - 1))) * pair)).astype(BF)
        dys[m] = dy
        dn = dot(dy, wout[...])
        nh = normed[m].astype(F32)
        m1 = jnp.sum(dn, axis=1, keepdims=True) * (1.0 / width)
        m2 = jnp.sum(dn * nh, axis=1, keepdims=True) * (1.0 / width)
        dh[m] = (inv[m][:, 0:1] * (dn - m1 - nh * m2)).astype(BF)
        return 0

    lax.fori_loop(0, members, head, 0)

    halves = [Half(place, wire, i % 2 == 0, *bufs[5 * i:5 * i + 5]) for i in range(len(bufs) // 5)]
    mix, tgt_sum, src = halves[:2], halves[2:4], halves[4:]

    def each(parts, step):
        for one in parts:
            getattr(one, step)()

    def product(turned, right):
        return dot(turned[...], right.reshape(-1, right.shape[-1])).astype(BF)

    def mix_grad(cols):
        return product(agg_x, dh[:, :, cols])

    put(mix[0].part, mix_grad(pl.ds(0, CW)))
    mix[0].start()
    put(mix[1].part, mix_grad(pl.ds(CW, CW)))
    put(mix[1].part, product(normed_x, dys[...]), CW)
    mix[1].start()

    def mix_back(cols):
        dagg = (0.125 * dot_nt(dh[...].reshape(flat, width), wmix[cols, :])).astype(BF)
        dagg = dagg.reshape(members, rows, CW)
        tgt[:, :, cols] = dagg
        dq[:, :, cols] = dagg * slope_sum[:, :, cols]

    columns(mix_back)

    def tgt_grad(cols):
        return product(grid_x, dq[:, :, cols])

    put(tgt_sum[0].part, tgt_grad(pl.ds(0, CW)))
    tgt_sum[0].start()
    put(tgt_sum[1].part, tgt_grad(pl.ds(CW, CW)))
    tgt_sum[1].start()
    each(mix, "s1")

    def spread(m):
        def column(cols):
            d = tgt[m, :, cols]
            for k in range(nbrs):
                slope[m, k, :, cols] = slope[m, k, :, cols] * d
            edges = slope[m, :, :, cols].reshape(nbrs * rows, CW)
            dpe[m, :, cols] = (dot(pick_t[...], edges) + dot(hits_t[...], d)).astype(BF)

        columns(column)
        rim_rows.start(m)

    def src_grad(c):
        put(src[c].part, product(lat_x, dpe[:, :, c * CW:(c + 1) * CW]))

    def grid_back(cols):
        got = dot_nt(dq[...].reshape(flat, width), wtgt[cols, :]).reshape(members, rows, CW)
        d_grid[:, :, cols] = (dh[:, :, cols].astype(F32) + got).astype(BF)

    spread(0)
    each(tgt_sum, "s1")
    spread(1)
    rim_rows.relay(0)
    spread(2)
    rim_rows.relay(1)
    each(mix, "s2")
    spread(3)
    rim_rows.relay(2)
    src_grad(0)
    src[0].start()
    rim_rows.relay(3)
    each(tgt_sum, "s2")
    src_grad(1)
    src[1].start()
    each(mix, "s3")
    src[0].s1()
    columns(grid_back, 0, 1)
    src[1].s1()
    columns(grid_back, 1, 2)
    each(tgt_sum, "s3")
    out_grid = pltpu.make_async_copy(d_grid, d_grid_out, load_sem.at[5])
    out_grid.start()
    o_mix[:, 0:512] = mix[0].s4(scale)
    last = mix[1].s4(scale)
    o_mix[:, 512:width] = last[:, 0:width - 512]
    o_out[...] = last[:, width - 512:width - 512 + fields]

    def sum_rims(m, _):
        rim_rows.wait(m)
        dq[m] = (dpe[m, HALO:HALO + rows].astype(F32) + rims[m].astype(F32)).astype(BF)
        return 0

    lax.fori_loop(0, members, sum_rims, 0)

    def latent_back(cols):
        got = dot_nt(dq[...].reshape(flat, width), wsrc[cols, :]).reshape(members, rows, CW)
        d_latent[:, :, cols] = got.astype(BF)

    columns(latent_back, 0, 1)
    src[0].s2()
    columns(latent_back, 1, 2)
    out_latent = pltpu.make_async_copy(d_latent, d_latent_out, load_sem.at[6])
    out_latent.start()
    src[1].s2()
    for one, (first, size) in zip(tgt_sum, TGT_CUTS):
        o_tgt[:, first:first + size] = one.s4(scale)
    each(src, "s3")
    out_grid.wait()
    out_latent.wait()
    for one, (first, size) in zip(src, SRC_CUTS):
        o_src[:, first:first + size] = one.s4(scale)


def hand_over(arrays):
    count = len(arrays)

    def move(*refs):
        sems = refs[-1]
        moves = [pltpu.make_async_copy(refs[i], refs[count + i], sems.at[i]) for i in range(count)]
        for one in moves:
            one.start()
        for one in moves:
            one.wait()

    anywhere = pl.BlockSpec(memory_space=pl.ANY)
    return pl.pallas_call(
        move,
        out_shape=[jax.ShapeDtypeStruct(a.shape, a.dtype) for a in arrays],
        in_specs=[pl.BlockSpec(memory_space=pltpu.VMEM)] * count,
        out_specs=[anywhere] * count,
        scratch_shapes=[pltpu.SemaphoreType.DMA((count,))],
    )(*arrays)


def on_device(latent, grid_in, w_src, w_tgt, w_mix, w_out, truth, area, nbr, mask):
    members, rows, width = grid_in.shape
    nbrs = nbr.shape[0]
    fields = w_out.shape[1]
    ext = rows + 2 * HALO
    tiles = lax.axis_size("grid")
    count = members * lax.axis_size("member")
    scale = 1.0 / math.sqrt(rows * tiles * count)

    def body_(*refs):
        body(scale, *refs)

    def ring_bufs(cols):
        return [pltpu.VMEM((NC, NY, NX, NZ, 16, cols), BF), pltpu.VMEM((NY, NX, NZ, 16, cols), BF),
                pltpu.VMEM((3, 4, NZ, 16, cols), BF), pltpu.VMEM((3, NZ, 16, cols), BF),
                pltpu.VMEM((3, 16, cols), BF)]

    vm = pl.BlockSpec(memory_space=pltpu.VMEM)
    hbm = pl.BlockSpec(memory_space=pl.ANY)
    sds = jax.ShapeDtypeStruct
    halves = [size for cuts in (MIX_CUTS, TGT_CUTS, SRC_CUTS) for _, size in cuts]
    ncopies = 10 * len(halves)
    results = pl.pallas_call(
        body_,
        out_shape=[
            sds((members, rows, width), BF),
            sds((members, rows, width), BF),
            sds((16, width), F32),
            sds((16, width), F32),
            sds((16, width), F32),
            sds((16, fields), F32),
        ],
        in_specs=[hbm, hbm, hbm, hbm, hbm, vm, vm, vm, vm, vm],
        out_specs=[hbm, hbm, vm, vm, vm, vm],
        scratch_shapes=[
            pltpu.VMEM((members, rows, width), BF),
            pltpu.VMEM((members, rows, width), BF),
            pltpu.VMEM((width, width), BF),
            pltpu.VMEM((width, width), BF),
            pltpu.VMEM((width, width), BF),
            pltpu.VMEM((FP, width), BF),
            pltpu.VMEM((FP, rows), F32),
            pltpu.VMEM((rows, FP), F32),
            pltpu.VMEM((nbrs, rows, ext), BF),
            pltpu.VMEM((ext, nbrs * rows), BF),
            pltpu.VMEM((rows, ext), BF),
            pltpu.VMEM((ext, rows), BF),
            pltpu.VMEM((nbrs, rows, 128), BF),
            pltpu.VMEM((members, ext, width), BF),
            pltpu.VMEM((members, rows, width), BF),
            pltpu.VMEM((members, nbrs, rows, width), BF),
            pltpu.VMEM((members, rows, width), BF),
            pltpu.VMEM((members, rows, width), BF),
            pltpu.VMEM((members, rows, width), BF),
            pltpu.VMEM((members, rows, 128), F32),
            pltpu.VMEM((2 * members, rows, FP), F32),
            pltpu.VMEM((members, rows, FP), BF),
            pltpu.VMEM((members, rows, width), BF),
            pltpu.VMEM((members, rows, width), BF),
            pltpu.VMEM((members, ext, width), BF),
            pltpu.VMEM((width, members * rows), BF),
            pltpu.VMEM((width, members * rows), BF),
            pltpu.VMEM((width, members * rows), BF),
            pltpu.VMEM((width, members * ext), BF),
            pltpu.VMEM((members, 2 * HALO, width), BF),
            pltpu.VMEM((members, 2 * HALO, width), BF),
            pltpu.VMEM((2, members, HALO // 2, width), BF),
            pltpu.VMEM((2, members, HALO // 2, width), BF),
            *[buf for cols in halves for buf in ring_bufs(cols)],
            pltpu.SemaphoreType.DMA((ncopies,)),
            pltpu.SemaphoreType.DMA((ncopies,)),
            pltpu.SemaphoreType.DMA((5, members)),
            pltpu.SemaphoreType.DMA((5, members)),
            pltpu.SemaphoreType.DMA((5, members)),
            pltpu.SemaphoreType.DMA((5, members)),
            pltpu.SemaphoreType.DMA((members,)),
            pltpu.SemaphoreType.DMA((members,)),
            pltpu.SemaphoreType.DMA((8,)),
        ],
        compiler_params=pltpu.CompilerParams(
            collective_id=0, has_side_effects=True, vmem_limit_bytes=63 * 2**20
        ),
        cost_estimate=pl.CostEstimate(flops=40 * 10**9, bytes_accessed=30 * 10**6, transcendentals=0),
    )(latent, grid_in, w_src, w_tgt, w_mix, w_out.T, truth, area.reshape(1, rows), nbr, mask)
    return hand_over(results)


def solution(mesh):
    in_specs = (
        P("member", "grid", None), P("member", "grid", None), P(), P(), P(), P(),
        P(None, "grid"), P("grid"), P(None, "grid"), P(None, "grid"),
    )
    out_specs = (
        P("member", "grid", None), P("member", "grid", None),
        P("grid", None), P("grid", None), P("grid", None), P("grid", None),
    )
    return jax.shard_map(
        on_device, mesh=mesh, in_specs=in_specs, out_specs=out_specs, check_vma=False
    )
```

```python
import math

import jax
import jax.numpy as jnp
from jax import lax
from jax.experimental import pallas as pl
from jax.experimental.pallas import tpu as pltpu
from jax.sharding import PartitionSpec as P

HALO = 64
SMOOTH = 0.0025
FAIR = 0.95
EPS = 1e-05
BF = jnp.bfloat16
F32 = jnp.float32
MESH = pl.DeviceIdType.MESH
CW = 512
NY, NX, NZ, NC = 4, 4, 2, 2
FP = 128
MIX_CUTS = ((0, 512), (512, 512 + FP))
TGT_CUTS = ((0, 512), (512, 512))
SRC_CUTS = ((0, 256), (256, 256), (512, 256), (768, 256))


def dot(a, b):
    return lax.dot_general(a, b, (((1,), (0,)), ((), ())), preferred_element_type=F32)


def dot_nt(a, b):
    return lax.dot_general(a, b, (((1,), (1,)), ((), ())), preferred_element_type=F32)


def dot_tn(a, b):
    return lax.dot_general(a, b, (((0,), (0,)), ((), ())), preferred_element_type=F32)


class Place:
    def __init__(self):
        self.me = lax.axis_index("member")
        t = lax.axis_index("grid")
        tiles = NY * NX * NZ * NC
        self.y, self.x, self.z, self.c = t // 16, (t // 4) % 4, (t // 2) % 2, t % 2
        self.up = (self.me, (t + 1) % tiles)
        self.down = (self.me, (t + tiles - 1) % tiles)
        self.mate = (1 - self.me, t)
        self.core = self.at(c=1 - self.c)
        self.y_ring = tuple(self.at(y=(self.y + k) % 4) for k in (1, 2, 3))
        self.x_ring = tuple(self.at(x=(self.x + k) % 4) for k in (1, 2, 3))
        self.z_far = (self.me, self.at(z=1 - self.z)[1])
        self.z_both = (1 - self.me, self.z_far[1])
        self.partners = (self.up, self.down, self.core, *self.y_ring, *self.x_ring,
                         self.mate, self.z_far, self.z_both)

    def at(self, y=None, x=None, z=None, c=None):
        y = self.y if y is None else y
        x = self.x if x is None else x
        z = self.z if z is None else z
        c = self.c if c is None else c
        return (self.me, y * 16 + x * 4 + z * 2 + c)


class Wire:
    def __init__(self, send, recv):
        self.send, self.recv, self.used = send, recv, 0

    def copy(self, src, dst, device):
        at = self.used
        self.used += 1
        return pltpu.make_async_remote_copy(
            src_ref=src, dst_ref=dst, send_sem=self.send.at[at], recv_sem=self.recv.at[at],
            device_id=device, device_id_type=MESH)


def add_into(dst, *others):
    total = dst[...].astype(F32)
    for o in others:
        total = total + o[...].astype(F32)
    dst[...] = total.astype(BF)


class Swap:
    def __init__(self, wire, p, others, block, buf):
        self.wire, self.p, self.others, self.block, self.buf = wire, p, others, block, buf

    def start(self):
        self.moves = [self.wire.copy(self.block((self.p + k) % 4), self.buf.at[k - 1], self.others[k - 1])
                      for k in (1, 3, 2)]
        for one in self.moves:
            one.start()

    def finish(self):
        for one in self.moves:
            one.wait()
        add_into(self.block(self.p), *[self.buf.at[k] for k in range(3)])


class Half:
    def __init__(self, place, wire, y_first, part, held, wide, thin, zbuf):
        self.place, self.wire, self.zbuf = place, wire, zbuf
        self.part, self.held = part, held
        y, x = place.y, place.x
        on_y, on_x = (y, place.y_ring), (x, place.x_ring)
        if y_first:
            self.one = Swap(wire, *on_y, lambda d: held.at[d], wide)
            self.two = Swap(wire, *on_x, lambda d: held.at[y, d], thin)
        else:
            self.one = Swap(wire, *on_x, lambda d: held.at[:, d], wide)
            self.two = Swap(wire, *on_y, lambda d: held.at[d, x], thin)

    def start(self):
        self.cross = self.wire.copy(self.part.at[1 - self.place.c], self.held, self.place.core)
        self.cross.start()

    def s1(self):
        self.cross.wait()

        def add(yy, _):
            add_into(self.held.at[yy], self.part.at[self.place.c, yy])
            return 0

        lax.fori_loop(0, NY, add, 0)
        self.one.start()

    def s2(self):
        self.one.finish()
        self.two.start()

    def s3(self):
        self.two.finish()
        p = self.place
        mine = self.held.at[p.y, p.x]
        self.last = [self.wire.copy(mine.at[p.z], self.zbuf.at[0], p.mate),
                     self.wire.copy(mine.at[1 - p.z], self.zbuf.at[1], p.z_far),
                     self.wire.copy(mine.at[1 - p.z], self.zbuf.at[2], p.z_both)]
        for one in self.last:
            one.start()

    def s4(self, scale):
        p = self.place
        for one in self.last:
            one.wait()
        total = self.held[p.y, p.x, p.z].astype(F32)
        for k in range(3):
            total = total + self.zbuf[k].astype(F32)
        return total * scale


def put(part, block, first=0):
    cols = slice(first, first + block.shape[1])
    for b in range(NY * NX * NZ * NC):
        part[b % 2, b // 16, (b // 4) % 4, (b // 2) % 2, :, cols] = block[b * 16:(b + 1) * 16]


def body(scale, lat_in, grid_in, wsrc_in, wtgt_in, wmix_in, wout_in, truth_in, area_in, nbr, mask,
         d_latent_out, d_grid_out, o_src, o_tgt, o_mix, o_out,
         lat, grid, wsrc, wtgt, wmix, wout, truth, area,
         pick, pick_t, hits, hits_t, maskb, proj, tgt, slope, slope_sum, agg, normed, inv, ys, dys, dh, dq, dpe,
         agg_x, normed_x, grid_x, lat_x,
         halo, rims, *rest):
    send_sem, recv_sem, halo_send, halo_recv, rim_send, rim_recv, y_send, y_recv, load_sem = rest[-9:]
    bufs = rest[:-9]
    members, rows, width = grid.shape
    nbrs = nbr.shape[0]
    fields = wout_in.shape[0]
    ext = rows + 2 * HALO
    tiles = width // CW
    flat = members * rows
    d_latent, d_grid = agg, normed
    place = Place()
    wire = Wire(send_sem, recv_sem)

    barrier = pltpu.get_barrier_semaphore()
    for partner in place.partners:
        pl.semaphore_signal(barrier, inc=1, device_id=partner, device_id_type=MESH)
    loads = [pltpu.make_async_copy(src, dst, load_sem.at[i])
             for i, (src, dst) in enumerate(((lat_in, lat), (grid_in, grid), (wtgt_in, wtgt), (wsrc_in, wsrc),
                                             (wmix_in, wmix)))]
    for one in loads:
        one.start()

    def copies(src, low, high, dst, sems, at, cols):
        return (
            pltpu.make_async_remote_copy(
                src_ref=src.at[at[0], pl.ds(high, HALO), cols], dst_ref=dst.at[at[0], pl.ds(0, HALO), cols],
                send_sem=sems[0].at[0, *at], recv_sem=sems[1].at[0, *at],
                device_id=place.up, device_id_type=MESH),
            pltpu.make_async_remote_copy(
                src_ref=src.at[at[0], pl.ds(low, HALO), cols], dst_ref=dst.at[at[0], pl.ds(HALO, HALO), cols],
                send_sem=sems[0].at[1, *at], recv_sem=sems[1].at[1, *at],
                device_id=place.down, device_id_type=MESH),
        )

    def halo_copies(m):
        return copies(lat, 0, rows - HALO, halo, (halo_send, halo_recv), (m,), slice(None))

    def rim_copies(m, c):
        return copies(dpe, 0, HALO + rows, rims, (rim_send, rim_recv), (m, c), pl.ds(c * CW, CW))

    def y_copy(m):
        return pltpu.make_async_remote_copy(
            src_ref=ys.at[m], dst_ref=ys.at[members + m],
            send_sem=y_send.at[m], recv_sem=y_recv.at[m],
            device_id=place.mate, device_id_type=MESH)

    loads[0].wait()
    pl.semaphore_wait(barrier, len(place.partners))
    for m in range(members):
        for one in halo_copies(m):
            one.start()

    truth[...] = jnp.zeros_like(truth)
    truth[0:fields, :] = truth_in[...]
    truth[...] = truth[...].T
    area[...] = jnp.broadcast_to(area_in[...], (rows, FP)).T
    wout[...] = jnp.zeros_like(wout)
    wout[0:fields, :] = wout_in[...]

    code = jnp.where(mask[...] != 0, nbr[...], -1).astype(F32)
    code_t = jnp.concatenate([code, jnp.zeros((rows - nbrs, rows), F32)], axis=0).T
    lane = lax.broadcasted_iota(jnp.int32, (rows, ext), 1).astype(F32)
    sub = lax.broadcasted_iota(jnp.int32, (ext, rows), 0).astype(F32)
    count = jnp.zeros((rows, 1), F32)
    for k in range(nbrs):
        col = code_t[:, k:k + 1]
        on = jnp.where(col >= 0.0, 1.0, 0.0)
        one = (col == lane).astype(F32).astype(BF)
        one_t = (code[k:k + 1, :] == sub).astype(F32).astype(BF)
        pick[k] = one
        maskb[k] = jnp.broadcast_to(on, (rows, 128))
        count = count + on
        pick_t[:, k * rows:(k + 1) * rows] = one_t
        if k == 0:
            hits[...] = one
            hits_t[...] = one_t
        else:
            hits[...] += one
            hits_t[...] += one_t

    def columns(step, first=0, last=tiles):
        def inner(c, _):
            step(pl.ds(pl.multiple_of(c * CW, CW), CW))
            return 0

        lax.fori_loop(first, last, inner, 0)

    def own_tgt(cols):
        got = (0.5 * dot(grid[...].reshape(flat, width), wtgt[:, cols]).astype(BF)).astype(BF)
        tgt[:, :, cols] = got.reshape(members, rows, CW)

    def own_src(cols):
        got = (0.5 * dot(lat[...].reshape(flat, width), wsrc[:, cols]).astype(BF)).astype(BF)
        proj[:, HALO:HALO + rows, cols] = got.reshape(members, rows, CW)

    loads[1].wait()
    loads[2].wait()
    columns(own_tgt)
    loads[3].wait()
    columns(own_src)

    def turn_grid(m, _):
        grid_x[:, pl.ds(pl.multiple_of(m * rows, rows), rows)] = grid[m].T
        return 0

    lax.fori_loop(0, members, turn_grid, 0)
    loads[4].wait()

    gb = 16

    def forward(m, _):
        for one in halo_copies(m):
            one.wait()
        edge = (0.5 * dot(halo[m], wsrc[...]).astype(BF)).astype(BF)
        proj[m, 0:HALO] = edge[0:HALO]
        proj[m, HALO + rows:ext] = edge[HALO:2 * HALO]

        linear = dot(hits[...], proj[m]) + count * tgt[m].astype(F32)
        for at in range(0, rows, gb):
            got = dot(pick[:, at:at + gb, :].reshape(nbrs * gb, ext), proj[m]).reshape(nbrs, gb, width)
            for c in range(0, width, 256):
                cols = slice(c, c + 256)
                base = tgt[m, at:at + gb, cols].astype(F32)
                acc = None
                acc_s = None
                for k in range(nbrs):
                    on = maskb[k, at:at + gb, :]
                    u = got[k, :, cols] + jnp.concatenate([on, on], axis=1) * base
                    t = jnp.tanh(u)
                    p = u * t
                    s = (t + u) - t * p
                    acc = p if k == 0 else acc + p
                    acc_s = s if k == 0 else acc_s + s
                    slope[m, k, at:at + gb, cols] = s.astype(BF)
                agg[m, at:at + gb, cols] = (0.25 * (linear[at:at + gb, cols] + acc)).astype(BF)
                slope_sum[m, at:at + gb, cols] = (acc_s + count[at:at + gb]).astype(BF)

        h = grid[m].astype(F32) + dot(agg[m], wmix[...])
        mean = jnp.sum(h, axis=1, keepdims=True) * (1.0 / width)
        centre = h - mean
        var = jnp.sum(centre * centre, axis=1, keepdims=True) * (1.0 / width)
        r = lax.rsqrt(var + EPS)
        inv[m] = jnp.broadcast_to(r, (rows, 128))
        normed[m] = (centre * r).astype(BF)
        ys[m] = dot_nt(normed[m], wout[...])
        y_copy(m).start()
        return 0

    lax.fori_loop(0, members, forward, 0)

    def turn(m, _):
        at = pl.ds(pl.multiple_of(m * rows, rows), rows)
        agg_x[:, at] = agg[m].T
        normed_x[:, at] = normed[m].T
        around = jnp.concatenate([halo[m, 0:HALO], lat[m], halo[m, HALO:2 * HALO]], axis=0)
        lat_x[:, pl.ds(pl.multiple_of(m * ext, ext), ext)] = around.T
        return 0

    lax.fori_loop(0, members, turn, 0)

    def y_wait(m, _):
        y_copy(m).wait()
        return 0

    lax.fori_loop(0, members, y_wait, 0)

    total = 2 * members

    def head(m, _):
        y = ys[m]
        miss = y - truth[...]
        pair = jnp.zeros_like(y)
        for o in range(total):
            diff = y - ys[o]
            pair = pair + diff * lax.rsqrt(diff * diff + SMOOTH)
        grad = miss * lax.rsqrt(miss * miss + SMOOTH) * (1.0 / total)
        dy = (area[...] * (grad - (FAIR / (total * (total - 1))) * pair)).astype(BF)
        dys[m] = dy
        dn = dot(dy, wout[...])
        nh = normed[m].astype(F32)
        m1 = jnp.sum(dn, axis=1, keepdims=True) * (1.0 / width)
        m2 = jnp.sum(dn * nh, axis=1, keepdims=True) * (1.0 / width)
        dh[m] = (inv[m][:, 0:1] * (dn - m1 - nh * m2)).astype(BF)
        return 0

    lax.fori_loop(0, members, head, 0)

    halves = [Half(place, wire, i % 2 == 0, *bufs[5 * i:5 * i + 5]) for i in range(len(bufs) // 5)]
    mix, tgt_sum, src = halves[:2], halves[2:4], halves[4:]

    def each(parts, step):
        for one in parts:
            getattr(one, step)()

    def product(turned, right):
        return dot(turned[...], right.reshape(-1, right.shape[-1])).astype(BF)

    def mix_grad(cols):
        return product(agg_x, dh[:, :, cols])

    put(mix[0].part, mix_grad(pl.ds(0, CW)))
    mix[0].start()
    put(mix[1].part, mix_grad(pl.ds(CW, CW)))
    put(mix[1].part, product(normed_x, dys[...]), CW)
    mix[1].start()

    def mix_back(cols):
        dagg = (0.125 * dot_nt(dh[...].reshape(flat, width), wmix[cols, :])).astype(BF)
        dagg = dagg.reshape(members, rows, CW)
        tgt[:, :, cols] = dagg
        dq[:, :, cols] = dagg * slope_sum[:, :, cols]

    columns(mix_back)

    def tgt_grad(cols):
        return product(grid_x, dq[:, :, cols])

    put(tgt_sum[0].part, tgt_grad(pl.ds(0, CW)))
    tgt_sum[0].start()
    put(tgt_sum[1].part, tgt_grad(pl.ds(CW, CW)))
    tgt_sum[1].start()
    each(mix, "s1")

    def spread(c, first, last):
        cols = pl.ds(c * CW, CW)

        def member(m, _):
            d = tgt[m, :, cols]
            for k in range(nbrs):
                slope[m, k, :, cols] = slope[m, k, :, cols] * d
            edges = slope[m, :, :, cols].reshape(nbrs * rows, CW)
            dpe[m, :, cols] = (dot(pick_t[...], edges) + dot(hits_t[...], d)).astype(BF)
            for one in rim_copies(m, c):
                one.start()
            return 0

        lax.fori_loop(first, last, member, 0)

    def src_grad(c):
        block = product(lat_x, dpe[:, :, c * CW:(c + 1) * CW])
        for i in range(2):
            put(src[2 * c + i].part, block[:, i * 256:(i + 1) * 256])

    def grid_back(cols):
        got = dot_nt(dq[...].reshape(flat, width), wtgt[cols, :]).reshape(members, rows, CW)
        d_grid[:, :, cols] = (dh[:, :, cols].astype(F32) + got).astype(BF)

    spread(0, 0, 2)
    each(tgt_sum, "s1")
    spread(0, 2, 4)
    each(mix, "s2")
    src_grad(0)
    each(src[:2], "start")
    spread(1, 0, 2)
    each(tgt_sum, "s2")
    each(src[:2], "s1")
    spread(1, 2, 4)
    each(mix, "s3")
    src_grad(1)
    each(src[2:], "start")
    each(tgt_sum, "s3")
    columns(grid_back, 0, 1)
    each(src[2:], "s1")
    each(src[:2], "s2")
    columns(grid_back, 1, 2)
    out_grid = pltpu.make_async_copy(d_grid, d_grid_out, load_sem.at[5])
    out_grid.start()
    o_mix[:, 0:512] = mix[0].s4(scale)
    last = mix[1].s4(scale)
    o_mix[:, 512:width] = last[:, 0:width - 512]
    o_out[...] = last[:, width - 512:width - 512 + fields]

    def sum_rims(m, _):
        for c in range(tiles):
            for one in rim_copies(m, c):
                one.wait()
        dq[m] = (dpe[m, HALO:HALO + rows].astype(F32) + rims[m].astype(F32)).astype(BF)
        return 0

    lax.fori_loop(0, members, sum_rims, 0)

    def latent_back(cols):
        got = dot_nt(dq[...].reshape(flat, width), wsrc[cols, :]).reshape(members, rows, CW)
        d_latent[:, :, cols] = got.astype(BF)

    columns(latent_back, 0, 1)
    each(src[:2], "s3")
    columns(latent_back, 1, 2)
    out_latent = pltpu.make_async_copy(d_latent, d_latent_out, load_sem.at[6])
    out_latent.start()
    each(src[2:], "s2")
    for one, (first, size) in zip(tgt_sum, TGT_CUTS):
        o_tgt[:, first:first + size] = one.s4(scale)
    each(src[2:], "s3")
    out_grid.wait()
    out_latent.wait()
    for one, (first, size) in zip(src, SRC_CUTS):
        o_src[:, first:first + size] = one.s4(scale)


def hand_over(arrays):
    count = len(arrays)

    def move(*refs):
        sems = refs[-1]
        moves = [pltpu.make_async_copy(refs[i], refs[count + i], sems.at[i]) for i in range(count)]
        for one in moves:
            one.start()
        for one in moves:
            one.wait()

    anywhere = pl.BlockSpec(memory_space=pl.ANY)
    return pl.pallas_call(
        move,
        out_shape=[jax.ShapeDtypeStruct(a.shape, a.dtype) for a in arrays],
        in_specs=[pl.BlockSpec(memory_space=pltpu.VMEM)] * count,
        out_specs=[anywhere] * count,
        scratch_shapes=[pltpu.SemaphoreType.DMA((count,))],
    )(*arrays)


def on_device(latent, grid_in, w_src, w_tgt, w_mix, w_out, truth, area, nbr, mask):
    members, rows, width = grid_in.shape
    nbrs = nbr.shape[0]
    fields = w_out.shape[1]
    ext = rows + 2 * HALO
    tiles = lax.axis_size("grid")
    count = members * lax.axis_size("member")
    scale = 1.0 / math.sqrt(rows * tiles * count)

    def body_(*refs):
        body(scale, *refs)

    def ring_bufs(cols):
        return [pltpu.VMEM((NC, NY, NX, NZ, 16, cols), BF), pltpu.VMEM((NY, NX, NZ, 16, cols), BF),
                pltpu.VMEM((3, 4, NZ, 16, cols), BF), pltpu.VMEM((3, NZ, 16, cols), BF),
                pltpu.VMEM((3, 16, cols), BF)]

    vm = pl.BlockSpec(memory_space=pltpu.VMEM)
    hbm = pl.BlockSpec(memory_space=pl.ANY)
    sds = jax.ShapeDtypeStruct
    halves = [size for cuts in (MIX_CUTS, TGT_CUTS, SRC_CUTS) for _, size in cuts]
    ncopies = 10 * len(halves)
    results = pl.pallas_call(
        body_,
        out_shape=[
            sds((members, rows, width), BF),
            sds((members, rows, width), BF),
            sds((16, width), F32),
            sds((16, width), F32),
            sds((16, width), F32),
            sds((16, fields), F32),
        ],
        in_specs=[hbm, hbm, hbm, hbm, hbm, vm, vm, vm, vm, vm],
        out_specs=[hbm, hbm, vm, vm, vm, vm],
        scratch_shapes=[
            pltpu.VMEM((members, rows, width), BF),
            pltpu.VMEM((members, rows, width), BF),
            pltpu.VMEM((width, width), BF),
            pltpu.VMEM((width, width), BF),
            pltpu.VMEM((width, width), BF),
            pltpu.VMEM((FP, width), BF),
            pltpu.VMEM((FP, rows), F32),
            pltpu.VMEM((rows, FP), F32),
            pltpu.VMEM((nbrs, rows, ext), BF),
            pltpu.VMEM((ext, nbrs * rows), BF),
            pltpu.VMEM((rows, ext), BF),
            pltpu.VMEM((ext, rows), BF),
            pltpu.VMEM((nbrs, rows, 128), F32),
            pltpu.VMEM((members, ext, width), BF),
            pltpu.VMEM((members, rows, width), BF),
            pltpu.VMEM((members, nbrs, rows, width), BF),
            pltpu.VMEM((members, rows, width), BF),
            pltpu.VMEM((members, rows, width), BF),
            pltpu.VMEM((members, rows, width), BF),
            pltpu.VMEM((members, rows, 128), F32),
            pltpu.VMEM((2 * members, rows, FP), F32),
            pltpu.VMEM((members, rows, FP), BF),
            pltpu.VMEM((members, rows, width), BF),
            pltpu.VMEM((members, rows, width), BF),
            pltpu.VMEM((members, ext, width), BF),
            pltpu.VMEM((width, members * rows), BF),
            pltpu.VMEM((width, members * rows), BF),
            pltpu.VMEM((width, members * rows), BF),
            pltpu.VMEM((width, members * ext), BF),
            pltpu.VMEM((members, 2 * HALO, width), BF),
            pltpu.VMEM((members, 2 * HALO, width), BF),
            *[buf for cols in halves for buf in ring_bufs(cols)],
            pltpu.SemaphoreType.DMA((ncopies,)),
            pltpu.SemaphoreType.DMA((ncopies,)),
            pltpu.SemaphoreType.DMA((2, members)),
            pltpu.SemaphoreType.DMA((2, members)),
            pltpu.SemaphoreType.DMA((2, members, width // CW)),
            pltpu.SemaphoreType.DMA((2, members, width // CW)),
            pltpu.SemaphoreType.DMA((members,)),
            pltpu.SemaphoreType.DMA((members,)),
            pltpu.SemaphoreType.DMA((8,)),
        ],
        compiler_params=pltpu.CompilerParams(
            collective_id=0, has_side_effects=True, vmem_limit_bytes=63 * 2**20
        ),
        cost_estimate=pl.CostEstimate(flops=40 * 10**9, bytes_accessed=30 * 10**6, transcendentals=0),
    )(latent, grid_in, w_src, w_tgt, w_mix, w_out.T, truth, area.reshape(1, rows), nbr, mask)
    return hand_over(results)


def solution(mesh):
    in_specs = (
        P("member", "grid", None), P("member", "grid", None), P(), P(), P(), P(),
        P(None, "grid"), P("grid"), P(None, "grid"), P(None, "grid"),
    )
    out_specs = (
        P("member", "grid", None), P("member", "grid", None),
        P("grid", None), P("grid", None), P("grid", None), P("grid", None),
    )
    return jax.shard_map(
        on_device, mesh=mesh, in_specs=in_specs, out_specs=out_specs, check_vma=False
    )
```

```python
import math

import jax
import jax.numpy as jnp
from jax import lax
from jax.experimental import pallas as pl
from jax.experimental.pallas import tpu as pltpu
from jax.sharding import PartitionSpec as P

HALO = 64
SMOOTH = 0.0025
FAIR = 0.95
EPS = 1e-05
BF = jnp.bfloat16
F32 = jnp.float32
MESH = pl.DeviceIdType.MESH
CW = 512
NY, NX, NZ, NC = 4, 4, 2, 2
FP = 128
MIX_CUTS = ((0, 512), (512, 512 + FP))
TGT_CUTS = ((0, 512), (512, 512))
SRC_CUTS = ((0, 256), (256, 256), (512, 256), (768, 256))


def dot(a, b):
    return lax.dot_general(a, b, (((1,), (0,)), ((), ())), preferred_element_type=F32)


def dot_nt(a, b):
    return lax.dot_general(a, b, (((1,), (1,)), ((), ())), preferred_element_type=F32)


def dot_tn(a, b):
    return lax.dot_general(a, b, (((0,), (0,)), ((), ())), preferred_element_type=F32)


class Place:
    def __init__(self):
        self.me = lax.axis_index("member")
        t = lax.axis_index("grid")
        tiles = NY * NX * NZ * NC
        self.y, self.x, self.z, self.c = t // 16, (t // 4) % 4, (t // 2) % 2, t % 2
        self.up = (self.me, (t + 1) % tiles)
        self.down = (self.me, (t + tiles - 1) % tiles)
        self.mate = (1 - self.me, t)
        self.core = self.at(c=1 - self.c)
        self.y_ring = tuple(self.at(y=(self.y + k) % 4) for k in (1, 2, 3))
        self.x_ring = tuple(self.at(x=(self.x + k) % 4) for k in (1, 2, 3))
        self.z_far = (self.me, self.at(z=1 - self.z)[1])
        self.z_both = (1 - self.me, self.z_far[1])
        self.partners = (self.up, self.down, self.core, *self.y_ring, *self.x_ring,
                         self.mate, self.z_far, self.z_both)

    def at(self, y=None, x=None, z=None, c=None):
        y = self.y if y is None else y
        x = self.x if x is None else x
        z = self.z if z is None else z
        c = self.c if c is None else c
        return (self.me, y * 16 + x * 4 + z * 2 + c)


class Wire:
    def __init__(self, send, recv):
        self.send, self.recv, self.used = send, recv, 0

    def copy(self, src, dst, device):
        at = self.used
        self.used += 1
        return pltpu.make_async_remote_copy(
            src_ref=src, dst_ref=dst, send_sem=self.send.at[at], recv_sem=self.recv.at[at],
            device_id=device, device_id_type=MESH)


def add_into(dst, *others):
    total = dst[...].astype(F32)
    for o in others:
        total = total + o[...].astype(F32)
    dst[...] = total.astype(BF)


class Swap:
    def __init__(self, wire, p, others, block, buf):
        self.wire, self.p, self.others, self.block, self.buf = wire, p, others, block, buf

    def start(self):
        self.moves = [self.wire.copy(self.block((self.p + k) % 4), self.buf.at[k - 1], self.others[k - 1])
                      for k in (1, 3, 2)]
        for one in self.moves:
            one.start()

    def finish(self):
        for one in self.moves:
            one.wait()
        add_into(self.block(self.p), *[self.buf.at[k] for k in range(3)])


class Half:
    def __init__(self, place, wire, y_first, part, held, wide, thin, zbuf):
        self.place, self.wire, self.zbuf = place, wire, zbuf
        self.part, self.held = part, held
        y, x = place.y, place.x
        on_y, on_x = (y, place.y_ring), (x, place.x_ring)
        if y_first:
            self.one = Swap(wire, *on_y, lambda d: held.at[d], wide)
            self.two = Swap(wire, *on_x, lambda d: held.at[y, d], thin)
        else:
            self.one = Swap(wire, *on_x, lambda d: held.at[:, d], wide)
            self.two = Swap(wire, *on_y, lambda d: held.at[d, x], thin)

    def start(self):
        self.cross = self.wire.copy(self.part.at[1 - self.place.c], self.held, self.place.core)
        self.cross.start()

    def s1(self):
        self.cross.wait()

        def add(yy, _):
            add_into(self.held.at[yy], self.part.at[self.place.c, yy])
            return 0

        lax.fori_loop(0, NY, add, 0)
        self.one.start()

    def s2(self):
        self.one.finish()
        self.two.start()

    def s3(self):
        self.two.finish()
        p = self.place
        mine = self.held.at[p.y, p.x]
        self.last = [self.wire.copy(mine.at[p.z], self.zbuf.at[0], p.mate),
                     self.wire.copy(mine.at[1 - p.z], self.zbuf.at[1], p.z_far),
                     self.wire.copy(mine.at[1 - p.z], self.zbuf.at[2], p.z_both)]
        for one in self.last:
            one.start()

    def s4(self, scale):
        p = self.place
        for one in self.last:
            one.wait()
        total = self.held[p.y, p.x, p.z].astype(F32)
        for k in range(3):
            total = total + self.zbuf[k].astype(F32)
        return total * scale


def put(part, block, first=0):
    cols = slice(first, first + block.shape[1])
    for b in range(NY * NX * NZ * NC):
        part[b % 2, b // 16, (b // 4) % 4, (b // 2) % 2, :, cols] = block[b * 16:(b + 1) * 16]


def body(scale, lat_in, grid_in, wsrc_in, wtgt_in, wmix_in, wout_in, truth_in, area_in, nbr, mask,
         d_latent_out, d_grid_out, o_src, o_tgt, o_mix, o_out,
         lat, grid, wsrc, wtgt, wmix, wout, truth, area,
         pick, pick_t, hits_t, maskb, proj, tgt, slope, slope_sum, agg, normed, inv, ys, dys, dh, dq, dpe,
         agg_x, grid_x, lat_x,
         halo, rims, *rest):
    send_sem, recv_sem, halo_send, halo_recv, rim_send, rim_recv, y_send, y_recv, load_sem = rest[-9:]
    bufs = rest[:-9]
    members, rows, width = grid.shape
    nbrs = nbr.shape[0]
    fields = wout_in.shape[0]
    ext = rows + 2 * HALO
    tiles = width // CW
    flat = members * rows
    d_latent, d_grid = agg, normed
    place = Place()
    wire = Wire(send_sem, recv_sem)

    barrier = pltpu.get_barrier_semaphore()
    for partner in place.partners:
        pl.semaphore_signal(barrier, inc=1, device_id=partner, device_id_type=MESH)
    loads = [pltpu.make_async_copy(src, dst, load_sem.at[i])
             for i, (src, dst) in enumerate(((lat_in, lat), (grid_in, grid), (wtgt_in, wtgt), (wsrc_in, wsrc),
                                             (wmix_in, wmix)))]
    for one in loads:
        one.start()

    def copies(src, low, high, dst, sems, at, cols):
        return (
            pltpu.make_async_remote_copy(
                src_ref=src.at[at[0], pl.ds(high, HALO), cols], dst_ref=dst.at[at[0], pl.ds(0, HALO), cols],
                send_sem=sems[0].at[0, *at], recv_sem=sems[1].at[0, *at],
                device_id=place.up, device_id_type=MESH),
            pltpu.make_async_remote_copy(
                src_ref=src.at[at[0], pl.ds(low, HALO), cols], dst_ref=dst.at[at[0], pl.ds(HALO, HALO), cols],
                send_sem=sems[0].at[1, *at], recv_sem=sems[1].at[1, *at],
                device_id=place.down, device_id_type=MESH),
        )

    def halo_copies(m):
        return copies(lat, 0, rows - HALO, halo, (halo_send, halo_recv), (m,), slice(None))

    def rim_copies(m, c):
        return copies(dpe, rows, rows + HALO, rims, (rim_send, rim_recv), (m, c), pl.ds(c * CW, CW))

    def y_copy(m):
        return pltpu.make_async_remote_copy(
            src_ref=ys.at[m], dst_ref=ys.at[members + m],
            send_sem=y_send.at[m], recv_sem=y_recv.at[m],
            device_id=place.mate, device_id_type=MESH)

    loads[0].wait()
    pl.semaphore_wait(barrier, len(place.partners))
    for m in range(members):
        for one in halo_copies(m):
            one.start()

    truth[...] = jnp.zeros_like(truth)
    truth[0:fields, :] = truth_in[...]
    truth[...] = truth[...].T
    area[...] = jnp.broadcast_to(area_in[...], (rows, FP)).T
    wout[...] = jnp.zeros_like(wout)
    wout[0:fields, :] = wout_in[...]

    near = jnp.where(nbr[...] < HALO, nbr[...] + rows, jnp.where(nbr[...] < HALO + rows, nbr[...] - HALO, nbr[...]))
    code = jnp.where(mask[...] != 0, near, -1).astype(F32)
    code_t = jnp.concatenate([code, jnp.zeros((rows - nbrs, rows), F32)], axis=0).T
    lane = lax.broadcasted_iota(jnp.int32, (rows, ext), 1).astype(F32)
    sub = lax.broadcasted_iota(jnp.int32, (ext, rows), 0).astype(F32)
    count = jnp.zeros((rows, 1), F32)
    for k in range(nbrs):
        col = code_t[:, k:k + 1]
        on = jnp.where(col >= 0.0, 1.0, 0.0)
        one = (col == lane).astype(F32).astype(BF)
        one_t = (code[k:k + 1, :] == sub).astype(F32).astype(BF)
        pick[k] = one
        maskb[k] = jnp.broadcast_to(on, (rows, 128)).astype(BF)
        count = count + on
        pick_t[:, k * rows:(k + 1) * rows] = one_t
        if k == 0:
            pick[nbrs] = one
            hits_t[...] = one_t
        else:
            pick[nbrs] += one
            hits_t[...] += one_t

    def columns(step, first=0, last=tiles):
        def inner(c, _):
            step(pl.ds(pl.multiple_of(c * CW, CW), CW))
            return 0

        lax.fori_loop(first, last, inner, 0)

    def own_tgt(cols):
        got = (0.5 * dot(grid[...].reshape(flat, width), wtgt[:, cols]).astype(BF)).astype(BF)
        tgt[:, :, cols] = got.reshape(members, rows, CW)

    def own_src(cols):
        got = (0.5 * dot(lat[...].reshape(flat, width), wsrc[:, cols]).astype(BF)).astype(BF)
        proj[:, 0:rows, cols] = got.reshape(members, rows, CW)

    loads[1].wait()
    loads[2].wait()
    columns(own_tgt)
    loads[3].wait()
    columns(own_src)

    def turn_grid(m, _):
        grid_x[:, pl.ds(pl.multiple_of(m * rows, rows), rows)] = grid[m].T
        lat_x[:, pl.ds(pl.multiple_of(m * ext, ext), rows)] = lat[m].T
        return 0

    lax.fori_loop(0, members, turn_grid, 0)
    loads[4].wait()

    gb = 32

    def gather(m, _):
        for at in range(0, rows, gb):
            both = dot(pick[:, at:at + gb, :].reshape((nbrs + 1) * gb, ext), proj[m])
            got = both[0:nbrs * gb].astype(BF).reshape(nbrs, gb, width)
            linear = both[nbrs * gb:] + count[at:at + gb] * tgt[m, at:at + gb, :].astype(F32)
            for c in range(0, width, 256):
                cols = slice(c, c + 256)
                base = tgt[m, at:at + gb, cols]
                acc = None
                acc_s = None
                for k in range(nbrs):
                    on = maskb[k, at:at + gb, :]
                    u = got[k, :, cols] + jnp.concatenate([on, on], axis=1) * base
                    t = jnp.tanh(u)
                    p = u * t
                    s = (t + u) - t * p
                    acc = p if k == 0 else acc + p
                    acc_s = s if k == 0 else acc_s + s
                    slope[m, k, at:at + gb, cols] = s
                total = linear[:, cols] + acc.astype(F32)
                agg[m, at:at + gb, cols] = (0.25 * total).astype(BF)
                slope_sum[m, at:at + gb, cols] = (acc_s.astype(F32) + count[at:at + gb]).astype(BF)

        return 0

    def forward(i, _):
        two = pl.ds(2 * i, 2)
        for j in range(2):
            for one in halo_copies(2 * i + j):
                one.wait()
        edge = (0.5 * dot(halo[two].reshape(2 * rows, width), wsrc[...]).astype(BF)).astype(BF)
        proj[two, rows:ext] = edge.reshape(2, rows, width)
        lax.fori_loop(2 * i, 2 * i + 2, gather, 0)
        h = dot(agg[two].reshape(2 * rows, width), wmix[...]) + grid[two].reshape(2 * rows, width).astype(F32)
        mean = jnp.sum(h, axis=1, keepdims=True) * (1.0 / width)
        centre = h - mean
        var = jnp.sum(centre * centre, axis=1, keepdims=True) * (1.0 / width)
        r = lax.rsqrt(var + EPS)
        inv[two] = jnp.broadcast_to(r, (2 * rows, 128)).reshape(2, rows, 128)
        unit = (centre * r).astype(BF)
        normed[two] = unit.reshape(2, rows, width)
        ys[two] = dot_nt(unit, wout[...]).reshape(2, rows, FP)
        for j in range(2):
            y_copy(2 * i + j).start()
        return 0

    lax.fori_loop(0, members // 2, forward, 0)

    def turn(m, _):
        at = pl.ds(pl.multiple_of(m * rows, rows), rows)
        agg_x[:, at] = agg[m].T
        lat_x[:, pl.ds(pl.multiple_of(m * ext + rows, rows), rows)] = halo[m].T
        return 0

    lax.fori_loop(0, members, turn, 0)

    def y_wait(m, _):
        y_copy(m).wait()
        return 0

    lax.fori_loop(0, members, y_wait, 0)

    total = 2 * members

    def head(m, _):
        y = ys[m]
        miss = y - truth[...]
        pair = jnp.zeros_like(y)
        for o in range(total):
            diff = y - ys[o]
            pair = pair + diff * lax.rsqrt(diff * diff + SMOOTH)
        grad = miss * lax.rsqrt(miss * miss + SMOOTH) * (1.0 / total)
        dy = (area[...] * (grad - (FAIR / (total * (total - 1))) * pair)).astype(BF)
        dys[m] = dy
        dn = dot(dy, wout[...])
        nh = normed[m].astype(F32)
        m1 = jnp.sum(dn, axis=1, keepdims=True) * (1.0 / width)
        m2 = jnp.sum(dn * nh, axis=1, keepdims=True) * (1.0 / width)
        dh[m] = (inv[m][:, 0:1] * (dn - m1 - nh * m2)).astype(BF)
        return 0

    lax.fori_loop(0, members, head, 0)

    halves = [Half(place, wire, i % 2 == 0, *bufs[5 * i:5 * i + 5]) for i in range(len(bufs) // 5)]
    mix, tgt_sum, src = halves[:2], halves[2:4], halves[4:]

    def each(parts, step):
        for one in parts:
            getattr(one, step)()

    def product(turned, right):
        return dot(turned[...], right.reshape(-1, right.shape[-1])).astype(BF)

    def mix_grad(cols):
        return product(agg_x, dh[:, :, cols])

    put(mix[0].part, mix_grad(pl.ds(0, CW)))
    mix[0].start()
    put(mix[1].part, mix_grad(pl.ds(CW, CW)))
    turned = jnp.concatenate([dys[m].T for m in range(members)], axis=1)
    put(mix[1].part, dot(turned, normed[...].reshape(flat, width)).T.astype(BF), CW)
    mix[1].start()

    def mix_back(cols):
        dagg = (0.125 * dot_nt(dh[...].reshape(flat, width), wmix[cols, :])).astype(BF)
        dagg = dagg.reshape(members, rows, CW)
        tgt[:, :, cols] = dagg
        dq[:, :, cols] = dagg * slope_sum[:, :, cols]

    columns(mix_back)

    def tgt_grad(cols):
        return product(grid_x, dq[:, :, cols])

    put(tgt_sum[0].part, tgt_grad(pl.ds(0, CW)))
    tgt_sum[0].start()
    put(tgt_sum[1].part, tgt_grad(pl.ds(CW, CW)))
    tgt_sum[1].start()
    each(mix, "s1")

    def spread(c, first, last):
        cols = pl.ds(c * CW, CW)

        def member(m, _):
            d = tgt[m, :, cols]
            for k in range(nbrs):
                slope[m, k, :, cols] = slope[m, k, :, cols] * d
            edges = slope[m, :, :, cols].reshape(nbrs * rows, CW)
            dpe[m, :, cols] = (dot(pick_t[...], edges) + dot(hits_t[...], d)).astype(BF)
            for one in rim_copies(m, c):
                one.start()
            return 0

        lax.fori_loop(first, last, member, 0)

    def src_grad(c):
        block = product(lat_x, dpe[:, :, c * CW:(c + 1) * CW])
        for i in range(2):
            put(src[2 * c + i].part, block[:, i * 256:(i + 1) * 256])

    def grid_back(cols):
        got = dot_nt(dq[...].reshape(flat, width), wtgt[cols, :]).reshape(members, rows, CW)
        d_grid[:, :, cols] = (dh[:, :, cols].astype(F32) + got).astype(BF)

    spread(0, 0, 2)
    each(tgt_sum, "s1")
    spread(0, 2, 4)
    each(mix, "s2")
    src_grad(0)
    each(src[:2], "start")
    spread(1, 0, 2)
    each(tgt_sum, "s2")
    each(src[:2], "s1")
    spread(1, 2, 4)
    each(mix, "s3")
    src_grad(1)
    each(src[2:], "start")
    each(tgt_sum, "s3")
    columns(grid_back, 0, 1)
    each(src[2:], "s1")
    each(src[:2], "s2")
    columns(grid_back, 1, 2)
    out_grid = pltpu.make_async_copy(d_grid, d_grid_out, load_sem.at[5])
    out_grid.start()
    o_mix[:, 0:512] = mix[0].s4(scale)
    last = mix[1].s4(scale)
    o_mix[:, 512:width] = last[:, 0:width - 512]
    o_out[...] = last[:, width - 512:width - 512 + fields]

    def sum_rims(m, _):
        for c in range(tiles):
            for one in rim_copies(m, c):
                one.wait()
        dq[m] = (dpe[m, 0:rows].astype(F32) + rims[m].astype(F32)).astype(BF)
        return 0

    lax.fori_loop(0, members, sum_rims, 0)

    def latent_back(cols):
        got = dot_nt(dq[...].reshape(flat, width), wsrc[cols, :]).reshape(members, rows, CW)
        d_latent[:, :, cols] = got.astype(BF)

    columns(latent_back, 0, 1)
    each(src[:2], "s3")
    columns(latent_back, 1, 2)
    out_latent = pltpu.make_async_copy(d_latent, d_latent_out, load_sem.at[6])
    out_latent.start()
    each(src[2:], "s2")
    for one, (first, size) in zip(tgt_sum, TGT_CUTS):
        o_tgt[:, first:first + size] = one.s4(scale)
    each(src[2:], "s3")
    out_grid.wait()
    out_latent.wait()
    for one, (first, size) in zip(src, SRC_CUTS):
        o_src[:, first:first + size] = one.s4(scale)


def hand_over(arrays):
    count = len(arrays)
    steps = arrays[0].shape[0]

    def move(*refs):
        for i in range(count):
            refs[count + i][...] = refs[i][...]

    def spec(a):
        if a.ndim == 3:
            return pl.BlockSpec((1, *a.shape[1:]), lambda i: (i, 0, 0))
        return pl.BlockSpec(a.shape, lambda i: (0, 0))

    return pl.pallas_call(
        move,
        grid=(steps,),
        out_shape=[jax.ShapeDtypeStruct(a.shape, a.dtype) for a in arrays],
        in_specs=[spec(a) for a in arrays],
        out_specs=[spec(a) for a in arrays],
    )(*arrays)


def on_device(latent, grid_in, w_src, w_tgt, w_mix, w_out, truth, area, nbr, mask):
    members, rows, width = grid_in.shape
    nbrs = nbr.shape[0]
    fields = w_out.shape[1]
    ext = rows + 2 * HALO
    tiles = lax.axis_size("grid")
    count = members * lax.axis_size("member")
    scale = 1.0 / math.sqrt(rows * tiles * count)

    def body_(*refs):
        body(scale, *refs)

    def ring_bufs(cols):
        return [pltpu.VMEM((NC, NY, NX, NZ, 16, cols), BF), pltpu.VMEM((NY, NX, NZ, 16, cols), BF),
                pltpu.VMEM((3, 4, NZ, 16, cols), BF), pltpu.VMEM((3, NZ, 16, cols), BF),
                pltpu.VMEM((3, 16, cols), BF)]

    vm = pl.BlockSpec(memory_space=pltpu.VMEM)
    hbm = pl.BlockSpec(memory_space=pl.ANY)
    sds = jax.ShapeDtypeStruct
    halves = [size for cuts in (MIX_CUTS, TGT_CUTS, SRC_CUTS) for _, size in cuts]
    ncopies = 10 * len(halves)
    results = pl.pallas_call(
        body_,
        out_shape=[
            sds((members, rows, width), BF),
            sds((members, rows, width), BF),
            sds((16, width), F32),
            sds((16, width), F32),
            sds((16, width), F32),
            sds((16, fields), F32),
        ],
        in_specs=[hbm, hbm, hbm, hbm, hbm, vm, vm, vm, vm, vm],
        out_specs=[hbm, hbm, vm, vm, vm, vm],
        scratch_shapes=[
            pltpu.VMEM((members, rows, width), BF),
            pltpu.VMEM((members, rows, width), BF),
            pltpu.VMEM((width, width), BF),
            pltpu.VMEM((width, width), BF),
            pltpu.VMEM((width, width), BF),
            pltpu.VMEM((FP, width), BF),
            pltpu.VMEM((FP, rows), F32),
            pltpu.VMEM((rows, FP), F32),
            pltpu.VMEM((nbrs + 1, rows, ext), BF),
            pltpu.VMEM((ext, nbrs * rows), BF),
            pltpu.VMEM((ext, rows), BF),
            pltpu.VMEM((nbrs, rows, 128), BF),
            pltpu.VMEM((members, ext, width), BF),
            pltpu.VMEM((members, rows, width), BF),
            pltpu.VMEM((members, nbrs, rows, width), BF),
            pltpu.VMEM((members, rows, width), BF),
            pltpu.VMEM((members, rows, width), BF),
            pltpu.VMEM((members, rows, width), BF),
            pltpu.VMEM((members, rows, 128), F32),
            pltpu.VMEM((2 * members, rows, FP), F32),
            pltpu.VMEM((members, rows, FP), BF),
            pltpu.VMEM((members, rows, width), BF),
            pltpu.VMEM((members, rows, width), BF),
            pltpu.VMEM((members, ext, width), BF),
            pltpu.VMEM((width, members * rows), BF),
            pltpu.VMEM((width, members * rows), BF),
            pltpu.VMEM((width, members * ext), BF),
            pltpu.VMEM((members, 2 * HALO, width), BF),
            pltpu.VMEM((members, 2 * HALO, width), BF),
            *[buf for cols in halves for buf in ring_bufs(cols)],
            pltpu.SemaphoreType.DMA((ncopies,)),
            pltpu.SemaphoreType.DMA((ncopies,)),
            pltpu.SemaphoreType.DMA((2, members)),
            pltpu.SemaphoreType.DMA((2, members)),
            pltpu.SemaphoreType.DMA((2, members, width // CW)),
            pltpu.SemaphoreType.DMA((2, members, width // CW)),
            pltpu.SemaphoreType.DMA((members,)),
            pltpu.SemaphoreType.DMA((members,)),
            pltpu.SemaphoreType.DMA((8,)),
        ],
        compiler_params=pltpu.CompilerParams(
            collective_id=0, has_side_effects=True, vmem_limit_bytes=63 * 2**20
        ),
        cost_estimate=pl.CostEstimate(flops=40 * 10**9, bytes_accessed=30 * 10**6, transcendentals=0),
    )(latent, grid_in, w_src, w_tgt, w_mix, w_out.T, truth, area.reshape(1, rows), nbr, mask)
    return hand_over(results)


def solution(mesh):
    in_specs = (
        P("member", "grid", None), P("member", "grid", None), P(), P(), P(), P(),
        P(None, "grid"), P("grid"), P(None, "grid"), P(None, "grid"),
    )
    out_specs = (
        P("member", "grid", None), P("member", "grid", None),
        P("grid", None), P("grid", None), P("grid", None), P("grid", None),
    )
    return jax.shard_map(
        on_device, mesh=mesh, in_specs=in_specs, out_specs=out_specs, check_vma=False
    )
```

```python
import math

import jax
import jax.numpy as jnp
from jax import lax
from jax.experimental import pallas as pl
from jax.experimental.pallas import tpu as pltpu
from jax.sharding import PartitionSpec as P

HALO = 64
SMOOTH = 0.0025
FAIR = 0.95
EPS = 1e-05
BF = jnp.bfloat16
F32 = jnp.float32
MESH = pl.DeviceIdType.MESH
CW = 512
NY, NX, NZ, NC = 4, 4, 2, 2
FP = 128
MIX_CUTS = ((0, 512), (512, 512 + FP))
TGT_CUTS = ((0, 512), (512, 512))
SRC_CUTS = ((0, 256), (256, 256), (512, 256), (768, 256))


def dot(a, b):
    return lax.dot_general(a, b, (((1,), (0,)), ((), ())), preferred_element_type=F32)


def dot_nt(a, b):
    return lax.dot_general(a, b, (((1,), (1,)), ((), ())), preferred_element_type=F32)


def dot_tn(a, b):
    return lax.dot_general(a, b, (((0,), (0,)), ((), ())), preferred_element_type=F32)


class Place:
    def __init__(self):
        self.me = lax.axis_index("member")
        t = lax.axis_index("grid")
        tiles = NY * NX * NZ * NC
        self.y, self.x, self.z, self.c = t // 16, (t // 4) % 4, (t // 2) % 2, t % 2
        self.up = (self.me, (t + 1) % tiles)
        self.down = (self.me, (t + tiles - 1) % tiles)
        self.mate = (1 - self.me, t)
        self.core = self.at(c=1 - self.c)
        self.y_ring = tuple(self.at(y=(self.y + k) % 4) for k in (1, 2, 3))
        self.x_ring = tuple(self.at(x=(self.x + k) % 4) for k in (1, 2, 3))
        self.z_far = (self.me, self.at(z=1 - self.z)[1])
        self.z_both = (1 - self.me, self.z_far[1])
        self.partners = (self.up, self.down, self.core, *self.y_ring, *self.x_ring,
                         self.mate, self.z_far, self.z_both)

    def at(self, y=None, x=None, z=None, c=None):
        y = self.y if y is None else y
        x = self.x if x is None else x
        z = self.z if z is None else z
        c = self.c if c is None else c
        return (self.me, y * 16 + x * 4 + z * 2 + c)


class Wire:
    def __init__(self, send, recv):
        self.send, self.recv, self.used = send, recv, 0

    def copy(self, src, dst, device):
        at = self.used
        self.used += 1
        return pltpu.make_async_remote_copy(
            src_ref=src, dst_ref=dst, send_sem=self.send.at[at], recv_sem=self.recv.at[at],
            device_id=device, device_id_type=MESH)


def add_into(dst, *others):
    total = dst[...].astype(F32)
    for o in others:
        total = total + o[...].astype(F32)
    dst[...] = total.astype(BF)


class Swap:
    def __init__(self, wire, p, others, block, buf):
        self.wire, self.p, self.others, self.block, self.buf = wire, p, others, block, buf

    def start(self):
        self.moves = [self.wire.copy(self.block((self.p + k) % 4), self.buf.at[k - 1], self.others[k - 1])
                      for k in (1, 3, 2)]
        for one in self.moves:
            one.start()

    def finish(self):
        for one in self.moves:
            one.wait()
        add_into(self.block(self.p), *[self.buf.at[k] for k in range(3)])


class Half:
    def __init__(self, place, wire, y_first, part, held, wide, thin, zbuf):
        self.place, self.wire, self.zbuf = place, wire, zbuf
        self.part, self.held = part, held
        y, x = place.y, place.x
        on_y, on_x = (y, place.y_ring), (x, place.x_ring)
        if y_first:
            self.one = Swap(wire, *on_y, lambda d: held.at[d], wide)
            self.two = Swap(wire, *on_x, lambda d: held.at[y, d], thin)
        else:
            self.one = Swap(wire, *on_x, lambda d: held.at[:, d], wide)
            self.two = Swap(wire, *on_y, lambda d: held.at[d, x], thin)

    def start(self):
        self.cross = self.wire.copy(self.part.at[1 - self.place.c], self.held, self.place.core)
        self.cross.start()

    def s1(self):
        self.cross.wait()

        def add(yy, _):
            add_into(self.held.at[yy], self.part.at[self.place.c, yy])
            return 0

        lax.fori_loop(0, NY, add, 0)
        self.one.start()

    def s2(self):
        self.one.finish()
        self.two.start()

    def s3(self):
        self.two.finish()
        p = self.place
        mine = self.held.at[p.y, p.x]
        self.last = [self.wire.copy(mine.at[p.z], self.zbuf.at[0], p.mate),
                     self.wire.copy(mine.at[1 - p.z], self.zbuf.at[1], p.z_far),
                     self.wire.copy(mine.at[1 - p.z], self.zbuf.at[2], p.z_both)]
        for one in self.last:
            one.start()

    def s4(self, scale):
        p = self.place
        for one in self.last:
            one.wait()
        total = self.held[p.y, p.x, p.z].astype(F32)
        for k in range(3):
            total = total + self.zbuf[k].astype(F32)
        return total * scale


def put(part, block, first=0):
    cols = slice(first, first + block.shape[1])
    for b in range(NY * NX * NZ * NC):
        part[b % 2, b // 16, (b // 4) % 4, (b // 2) % 2, :, cols] = block[b * 16:(b + 1) * 16]


def body(scale, lat_in, grid_in, wsrc_in, wtgt_in, wmix_in, wout_in, truth_in, area_in, nbr, mask,
         d_latent_out, d_grid_out, o_src, o_tgt, o_mix, o_out,
         lat, grid, wsrc, wtgt, wmix, wout, truth, area,
         pick, pick_t, hits, hits_t, maskb, proj, tgt, slope, slope_sum, agg, normed, inv, ys, dys, dh, dq, dpe,
         agg_x, grid_x, lat_x,
         halo, rims, *rest):
    send_sem, recv_sem, halo_send, halo_recv, rim_send, rim_recv, y_send, y_recv, load_sem = rest[-9:]
    bufs = rest[:-9]
    members, rows, width = grid.shape
    nbrs = nbr.shape[0]
    fields = wout_in.shape[0]
    ext = rows + 2 * HALO
    tiles = width // CW
    flat = members * rows
    d_latent, d_grid = agg, normed
    place = Place()
    wire = Wire(send_sem, recv_sem)

    barrier = pltpu.get_barrier_semaphore()
    for partner in place.partners:
        pl.semaphore_signal(barrier, inc=1, device_id=partner, device_id_type=MESH)
    loads = [pltpu.make_async_copy(src, dst, load_sem.at[i])
             for i, (src, dst) in enumerate(((lat_in, lat), (grid_in, grid), (wtgt_in, wtgt), (wsrc_in, wsrc),
                                             (wmix_in, wmix)))]
    for one in loads:
        one.start()

    def copies(src, low, high, dst, sems, at, cols):
        return (
            pltpu.make_async_remote_copy(
                src_ref=src.at[at[0], pl.ds(high, HALO), cols], dst_ref=dst.at[at[0], pl.ds(0, HALO), cols],
                send_sem=sems[0].at[0, *at], recv_sem=sems[1].at[0, *at],
                device_id=place.up, device_id_type=MESH),
            pltpu.make_async_remote_copy(
                src_ref=src.at[at[0], pl.ds(low, HALO), cols], dst_ref=dst.at[at[0], pl.ds(HALO, HALO), cols],
                send_sem=sems[0].at[1, *at], recv_sem=sems[1].at[1, *at],
                device_id=place.down, device_id_type=MESH),
        )

    def halo_copies(m):
        return copies(lat, 0, rows - HALO, halo, (halo_send, halo_recv), (m,), slice(None))

    def rim_copies(m, c):
        return copies(dpe, rows, rows + HALO, rims, (rim_send, rim_recv), (m, c), pl.ds(c * CW, CW))

    def y_copy(m):
        return pltpu.make_async_remote_copy(
            src_ref=ys.at[m], dst_ref=ys.at[members + m],
            send_sem=y_send.at[m], recv_sem=y_recv.at[m],
            device_id=place.mate, device_id_type=MESH)

    loads[0].wait()
    pl.semaphore_wait(barrier, len(place.partners))

    def send_halo(m):
        for one in halo_copies(m):
            one.start()

    send_halo(0)

    truth[...] = jnp.zeros_like(truth)
    truth[0:fields, :] = truth_in[...]
    truth[...] = truth[...].T
    area[...] = jnp.broadcast_to(area_in[...], (rows, FP)).T
    wout[...] = jnp.zeros_like(wout)
    wout[0:fields, :] = wout_in[...]

    near = jnp.where(nbr[...] < HALO, nbr[...] + rows, jnp.where(nbr[...] < HALO + rows, nbr[...] - HALO, nbr[...]))
    code = jnp.where(mask[...] != 0, near, -1).astype(F32)
    code_t = jnp.concatenate([code, jnp.zeros((rows - nbrs, rows), F32)], axis=0).T
    lane = lax.broadcasted_iota(jnp.int32, (rows, ext), 1).astype(F32)
    sub = lax.broadcasted_iota(jnp.int32, (ext, rows), 0).astype(F32)
    count = jnp.zeros((rows, 1), F32)
    for k in range(nbrs):
        col = code_t[:, k:k + 1]
        on = jnp.where(col >= 0.0, 1.0, 0.0)
        one = (col == lane).astype(F32).astype(BF)
        one_t = (code[k:k + 1, :] == sub).astype(F32).astype(BF)
        pick[k] = one
        maskb[k] = jnp.broadcast_to(on, (rows, 128)).astype(BF)
        count = count + on
        pick_t[:, k * rows:(k + 1) * rows] = one_t
        if k == 0:
            hits[...] = one
            hits_t[...] = one_t
        else:
            hits[...] += one
            hits_t[...] += one_t

    def columns(step, first=0, last=tiles):
        def inner(c, _):
            step(pl.ds(pl.multiple_of(c * CW, CW), CW))
            return 0

        lax.fori_loop(first, last, inner, 0)

    def own_tgt(cols):
        got = (0.5 * dot(grid[...].reshape(flat, width), wtgt[:, cols]).astype(BF)).astype(BF)
        tgt[:, :, cols] = got.reshape(members, rows, CW)

    def own_src(cols):
        got = (0.5 * dot(lat[...].reshape(flat, width), wsrc[:, cols]).astype(BF)).astype(BF)
        proj[:, 0:rows, cols] = got.reshape(members, rows, CW)

    send_halo(1)
    loads[1].wait()
    loads[2].wait()
    columns(own_tgt)
    send_halo(2)
    loads[3].wait()
    columns(own_src)
    send_halo(3)

    def turn_grid(m, _):
        grid_x[:, pl.ds(pl.multiple_of(m * rows, rows), rows)] = grid[m].T
        lat_x[:, pl.ds(pl.multiple_of(m * ext, ext), rows)] = lat[m].T
        return 0

    lax.fori_loop(0, members, turn_grid, 0)
    loads[4].wait()

    gb = 32

    def forward(m, _):
        for one in halo_copies(m):
            one.wait()
        edge = (0.5 * dot(halo[m], wsrc[...]).astype(BF)).astype(BF)
        proj[m, rows:ext] = edge

        linear = dot(hits[...], proj[m]) + count * tgt[m].astype(F32)
        for at in range(0, rows, gb):
            got = dot(pick[:, at:at + gb, :].reshape(nbrs * gb, ext), proj[m]).astype(BF)
            got = got.reshape(nbrs, gb, width)
            for c in range(0, width, 256):
                cols = slice(c, c + 256)
                base = tgt[m, at:at + gb, cols]
                acc = None
                acc_s = None
                for k in range(nbrs):
                    on = maskb[k, at:at + gb, :]
                    u = got[k, :, cols] + jnp.concatenate([on, on], axis=1) * base
                    t = jnp.tanh(u)
                    p = u * t
                    s = (t + u) - t * p
                    acc = p if k == 0 else acc + p
                    acc_s = s if k == 0 else acc_s + s
                    slope[m, k, at:at + gb, cols] = s
                total = linear[at:at + gb, cols] + acc.astype(F32)
                agg[m, at:at + gb, cols] = (0.25 * total).astype(BF)
                slope_sum[m, at:at + gb, cols] = (acc_s.astype(F32) + count[at:at + gb]).astype(BF)

        h = grid[m].astype(F32) + dot(agg[m], wmix[...])
        mean = jnp.sum(h, axis=1, keepdims=True) * (1.0 / width)
        centre = h - mean
        var = jnp.sum(centre * centre, axis=1, keepdims=True) * (1.0 / width)
        r = lax.rsqrt(var + EPS)
        inv[m] = jnp.broadcast_to(r, (rows, 128))
        normed[m] = (centre * r).astype(BF)
        ys[m] = dot_nt(normed[m], wout[...])
        y_copy(m).start()
        return 0

    lax.fori_loop(0, members, forward, 0)

    def turn(m, _):
        at = pl.ds(pl.multiple_of(m * rows, rows), rows)
        agg_x[:, at] = agg[m].T
        lat_x[:, pl.ds(pl.multiple_of(m * ext + rows, rows), rows)] = halo[m].T
        return 0

    lax.fori_loop(0, members, turn, 0)

    def y_wait(m, _):
        y_copy(m).wait()
        return 0

    lax.fori_loop(0, members, y_wait, 0)

    total = 2 * members

    def head(m, _):
        y = ys[m]
        miss = y - truth[...]
        pair = jnp.zeros_like(y)
        for o in range(total):
            diff = y - ys[o]
            pair = pair + diff * lax.rsqrt(diff * diff + SMOOTH)
        grad = miss * lax.rsqrt(miss * miss + SMOOTH) * (1.0 / total)
        dy = (area[...] * (grad - (FAIR / (total * (total - 1))) * pair)).astype(BF)
        dys[m] = dy
        dn = dot(dy, wout[...])
        nh = normed[m].astype(F32)
        m1 = jnp.sum(dn, axis=1, keepdims=True) * (1.0 / width)
        m2 = jnp.sum(dn * nh, axis=1, keepdims=True) * (1.0 / width)
        dh[m] = (inv[m][:, 0:1] * (dn - m1 - nh * m2)).astype(BF)
        return 0

    lax.fori_loop(0, members, head, 0)

    halves = [Half(place, wire, i % 2 == 0, *bufs[5 * i:5 * i + 5]) for i in range(len(bufs) // 5)]
    mix, tgt_sum, src = halves[:2], halves[2:4], halves[4:]

    def each(parts, step):
        for one in parts:
            getattr(one, step)()

    def product(turned, right):
        return dot(turned[...], right.reshape(-1, right.shape[-1])).astype(BF)

    def mix_grad(cols):
        return product(agg_x, dh[:, :, cols])

    put(mix[0].part, mix_grad(pl.ds(0, CW)))
    mix[0].start()
    put(mix[1].part, mix_grad(pl.ds(CW, CW)))
    turned = jnp.concatenate([dys[m].T for m in range(members)], axis=1)
    put(mix[1].part, dot(turned, normed[...].reshape(flat, width)).T.astype(BF), CW)
    mix[1].start()

    def mix_back(cols):
        dagg = (0.125 * dot_nt(dh[...].reshape(flat, width), wmix[cols, :])).astype(BF)
        dagg = dagg.reshape(members, rows, CW)
        tgt[:, :, cols] = dagg
        dq[:, :, cols] = dagg * slope_sum[:, :, cols]

    columns(mix_back)

    def tgt_grad(cols):
        return product(grid_x, dq[:, :, cols])

    put(tgt_sum[0].part, tgt_grad(pl.ds(0, CW)))
    tgt_sum[0].start()
    put(tgt_sum[1].part, tgt_grad(pl.ds(CW, CW)))
    tgt_sum[1].start()
    each(mix, "s1")

    def spread(c, first, last):
        cols = pl.ds(c * CW, CW)

        def member(m, _):
            d = tgt[m, :, cols]
            for k in range(nbrs):
                slope[m, k, :, cols] = slope[m, k, :, cols] * d
            edges = slope[m, :, :, cols].reshape(nbrs * rows, CW)
            dpe[m, :, cols] = (dot(pick_t[...], edges) + dot(hits_t[...], d)).astype(BF)
            for one in rim_copies(m, c):
                one.start()
            return 0

        lax.fori_loop(first, last, member, 0)

    def src_grad(c):
        block = product(lat_x, dpe[:, :, c * CW:(c + 1) * CW])
        for i in range(2):
            put(src[2 * c + i].part, block[:, i * 256:(i + 1) * 256])

    def grid_back(cols):
        got = dot_nt(dq[...].reshape(flat, width), wtgt[cols, :]).reshape(members, rows, CW)
        d_grid[:, :, cols] = (dh[:, :, cols].astype(F32) + got).astype(BF)

    spread(0, 0, 2)
    each(tgt_sum, "s1")
    spread(0, 2, 4)
    each(mix, "s2")
    src_grad(0)
    each(src[:2], "start")
    spread(1, 0, 2)
    each(tgt_sum, "s2")
    each(src[:2], "s1")
    spread(1, 2, 4)
    each(mix, "s3")
    src_grad(1)
    each(src[2:], "start")
    each(tgt_sum, "s3")
    columns(grid_back, 0, 1)
    each(src[2:], "s1")
    each(src[:2], "s2")
    columns(grid_back, 1, 2)
    out_grid = pltpu.make_async_copy(d_grid, d_grid_out, load_sem.at[5])
    out_grid.start()
    o_mix[:, 0:512] = mix[0].s4(scale)
    last = mix[1].s4(scale)
    o_mix[:, 512:width] = last[:, 0:width - 512]
    o_out[...] = last[:, width - 512:width - 512 + fields]

    def sum_rims(m, _):
        for c in range(tiles):
            for one in rim_copies(m, c):
                one.wait()
        dq[m] = (dpe[m, 0:rows].astype(F32) + rims[m].astype(F32)).astype(BF)
        return 0

    lax.fori_loop(0, members, sum_rims, 0)

    def latent_back(cols):
        got = dot_nt(dq[...].reshape(flat, width), wsrc[cols, :]).reshape(members, rows, CW)
        d_latent[:, :, cols] = got.astype(BF)

    columns(latent_back, 0, 1)
    each(src[:2], "s3")
    columns(latent_back, 1, 2)
    out_latent = pltpu.make_async_copy(d_latent, d_latent_out, load_sem.at[6])
    out_latent.start()
    each(src[2:], "s2")
    for one, (first, size) in zip(tgt_sum, TGT_CUTS):
        o_tgt[:, first:first + size] = one.s4(scale)
    each(src[2:], "s3")
    out_grid.wait()
    out_latent.wait()
    for one, (first, size) in zip(src, SRC_CUTS):
        o_src[:, first:first + size] = one.s4(scale)


def hand_over(arrays):
    count = len(arrays)

    def move(*refs):
        sems = refs[-1]
        moves = [pltpu.make_async_copy(refs[i], refs[count + i], sems.at[i]) for i in range(count)]
        for one in moves:
            one.start()
        for one in moves:
            one.wait()

    anywhere = pl.BlockSpec(memory_space=pl.ANY)
    return pl.pallas_call(
        move,
        out_shape=[jax.ShapeDtypeStruct(a.shape, a.dtype) for a in arrays],
        in_specs=[pl.BlockSpec(memory_space=pltpu.VMEM)] * count,
        out_specs=[anywhere] * count,
        scratch_shapes=[pltpu.SemaphoreType.DMA((count,))],
    )(*arrays)


def on_device(latent, grid_in, w_src, w_tgt, w_mix, w_out, truth, area, nbr, mask):
    members, rows, width = grid_in.shape
    nbrs = nbr.shape[0]
    fields = w_out.shape[1]
    ext = rows + 2 * HALO
    tiles = lax.axis_size("grid")
    count = members * lax.axis_size("member")
    scale = 1.0 / math.sqrt(rows * tiles * count)

    def body_(*refs):
        body(scale, *refs)

    def ring_bufs(cols):
        return [pltpu.VMEM((NC, NY, NX, NZ, 16, cols), BF), pltpu.VMEM((NY, NX, NZ, 16, cols), BF),
                pltpu.VMEM((3, 4, NZ, 16, cols), BF), pltpu.VMEM((3, NZ, 16, cols), BF),
                pltpu.VMEM((3, 16, cols), BF)]

    vm = pl.BlockSpec(memory_space=pltpu.VMEM)
    hbm = pl.BlockSpec(memory_space=pl.ANY)
    sds = jax.ShapeDtypeStruct
    halves = [size for cuts in (MIX_CUTS, TGT_CUTS, SRC_CUTS) for _, size in cuts]
    ncopies = 10 * len(halves)
    results = pl.pallas_call(
        body_,
        out_shape=[
            sds((members, rows, width), BF),
            sds((members, rows, width), BF),
            sds((16, width), F32),
            sds((16, width), F32),
            sds((16, width), F32),
            sds((16, fields), F32),
        ],
        in_specs=[hbm, hbm, hbm, hbm, hbm, vm, vm, vm, vm, vm],
        out_specs=[hbm, hbm, vm, vm, vm, vm],
        scratch_shapes=[
            pltpu.VMEM((members, rows, width), BF),
            pltpu.VMEM((members, rows, width), BF),
            pltpu.VMEM((width, width), BF),
            pltpu.VMEM((width, width), BF),
            pltpu.VMEM((width, width), BF),
            pltpu.VMEM((FP, width), BF),
            pltpu.VMEM((FP, rows), F32),
            pltpu.VMEM((rows, FP), F32),
            pltpu.VMEM((nbrs, rows, ext), BF),
            pltpu.VMEM((ext, nbrs * rows), BF),
            pltpu.VMEM((rows, ext), BF),
            pltpu.VMEM((ext, rows), BF),
            pltpu.VMEM((nbrs, rows, 128), BF),
            pltpu.VMEM((members, ext, width), BF),
            pltpu.VMEM((members, rows, width), BF),
            pltpu.VMEM((members, nbrs, rows, width), BF),
            pltpu.VMEM((members, rows, width), BF),
            pltpu.VMEM((members, rows, width), BF),
            pltpu.VMEM((members, rows, width), BF),
            pltpu.VMEM((members, rows, 128), F32),
            pltpu.VMEM((2 * members, rows, FP), F32),
            pltpu.VMEM((members, rows, FP), BF),
            pltpu.VMEM((members, rows, width), BF),
            pltpu.VMEM((members, rows, width), BF),
            pltpu.VMEM((members, ext, width), BF),
            pltpu.VMEM((width, members * rows), BF),
            pltpu.VMEM((width, members * rows), BF),
            pltpu.VMEM((width, members * ext), BF),
            pltpu.VMEM((members, 2 * HALO, width), BF),
            pltpu.VMEM((members, 2 * HALO, width), BF),
            *[buf for cols in halves for buf in ring_bufs(cols)],
            pltpu.SemaphoreType.DMA((ncopies,)),
            pltpu.SemaphoreType.DMA((ncopies,)),
            pltpu.SemaphoreType.DMA((2, members)),
            pltpu.SemaphoreType.DMA((2, members)),
            pltpu.SemaphoreType.DMA((2, members, width // CW)),
            pltpu.SemaphoreType.DMA((2, members, width // CW)),
            pltpu.SemaphoreType.DMA((members,)),
            pltpu.SemaphoreType.DMA((members,)),
            pltpu.SemaphoreType.DMA((8,)),
        ],
        compiler_params=pltpu.CompilerParams(
            collective_id=0, has_side_effects=True, vmem_limit_bytes=63 * 2**20
        ),
        cost_estimate=pl.CostEstimate(flops=40 * 10**9, bytes_accessed=30 * 10**6, transcendentals=0),
    )(latent, grid_in, w_src, w_tgt, w_mix, w_out.T, truth, area.reshape(1, rows), nbr, mask)
    return hand_over(results)


def solution(mesh):
    in_specs = (
        P("member", "grid", None), P("member", "grid", None), P(), P(), P(), P(),
        P(None, "grid"), P("grid"), P(None, "grid"), P(None, "grid"),
    )
    out_specs = (
        P("member", "grid", None), P("member", "grid", None),
        P("grid", None), P("grid", None), P("grid", None), P("grid", None),
    )
    return jax.shard_map(
        on_device, mesh=mesh, in_specs=in_specs, out_specs=out_specs, check_vma=False
    )
```

```python
import math

import jax
import jax.numpy as jnp
from jax import lax
from jax.experimental import pallas as pl
from jax.experimental.pallas import tpu as pltpu
from jax.sharding import PartitionSpec as P

HALO = 64
SMOOTH = 0.0025
FAIR = 0.95
EPS = 1e-05
BF = jnp.bfloat16
F32 = jnp.float32
MESH = pl.DeviceIdType.MESH
CW = 512
NY, NX, NZ, NC = 4, 4, 2, 2
FP = 128
MIX_CUTS = ((0, 512), (512, 512 + FP))
TGT_CUTS = ((0, 512), (512, 512))
SRC_CUTS = ((0, 512), (512, 512))


def dot(a, b):
    return lax.dot_general(a, b, (((1,), (0,)), ((), ())), preferred_element_type=F32)


def dot_nt(a, b):
    return lax.dot_general(a, b, (((1,), (1,)), ((), ())), preferred_element_type=F32)


def dot_tn(a, b):
    return lax.dot_general(a, b, (((0,), (0,)), ((), ())), preferred_element_type=F32)


class Place:
    def __init__(self):
        self.me = lax.axis_index("member")
        t = lax.axis_index("grid")
        tiles = NY * NX * NZ * NC
        self.y, self.x, self.z, self.c = t // 16, (t // 4) % 4, (t // 2) % 2, t % 2
        self.up = (self.me, (t + 1) % tiles)
        self.down = (self.me, (t + tiles - 1) % tiles)
        self.mate = (1 - self.me, t)
        self.core = self.at(c=1 - self.c)
        self.y_ring = tuple(self.at(y=(self.y + k) % 4) for k in (1, 2, 3))
        self.x_ring = tuple(self.at(x=(self.x + k) % 4) for k in (1, 2, 3))
        self.z_far = (self.me, self.at(z=1 - self.z)[1])
        self.z_both = (1 - self.me, self.z_far[1])
        self.partners = (self.up, self.down, self.core, *self.y_ring, *self.x_ring,
                         self.mate, self.z_far, self.z_both)

    def at(self, y=None, x=None, z=None, c=None):
        y = self.y if y is None else y
        x = self.x if x is None else x
        z = self.z if z is None else z
        c = self.c if c is None else c
        return (self.me, y * 16 + x * 4 + z * 2 + c)


class Wire:
    def __init__(self, send, recv):
        self.send, self.recv, self.used = send, recv, 0

    def copy(self, src, dst, device):
        at = self.used
        self.used += 1
        return pltpu.make_async_remote_copy(
            src_ref=src, dst_ref=dst, send_sem=self.send.at[at], recv_sem=self.recv.at[at],
            device_id=device, device_id_type=MESH)


def add_into(dst, *others):
    total = dst[...].astype(F32)
    for o in others:
        total = total + o[...].astype(F32)
    dst[...] = total.astype(BF)


class Swap:
    def __init__(self, wire, p, others, block, buf):
        self.wire, self.p, self.others, self.block, self.buf = wire, p, others, block, buf

    def start(self):
        self.moves = [self.wire.copy(self.block((self.p + k) % 4), self.buf.at[k - 1], self.others[k - 1])
                      for k in (1, 3, 2)]
        for one in self.moves:
            one.start()

    def finish(self):
        for one in self.moves:
            one.wait()
        add_into(self.block(self.p), *[self.buf.at[k] for k in range(3)])


class Half:
    def __init__(self, place, wire, y_first, part, held, wide, thin, zbuf):
        self.place, self.wire, self.zbuf = place, wire, zbuf
        self.part, self.held = part, held
        y, x = place.y, place.x
        on_y, on_x = (y, place.y_ring), (x, place.x_ring)
        if y_first:
            self.one = Swap(wire, *on_y, lambda d: held.at[d], wide)
            self.two = Swap(wire, *on_x, lambda d: held.at[y, d], thin)
        else:
            self.one = Swap(wire, *on_x, lambda d: held.at[:, d], wide)
            self.two = Swap(wire, *on_y, lambda d: held.at[d, x], thin)

    def start(self):
        self.cross = self.wire.copy(self.part.at[1 - self.place.c], self.held, self.place.core)
        self.cross.start()

    def s1(self):
        self.cross.wait()

        def add(yy, _):
            add_into(self.held.at[yy], self.part.at[self.place.c, yy])
            return 0

        lax.fori_loop(0, NY, add, 0)
        self.one.start()

    def s2(self):
        self.one.finish()
        self.two.start()

    def s3(self):
        self.two.finish()
        p = self.place
        mine = self.held.at[p.y, p.x]
        self.last = [self.wire.copy(mine.at[p.z], self.zbuf.at[0], p.mate),
                     self.wire.copy(mine.at[1 - p.z], self.zbuf.at[1], p.z_far),
                     self.wire.copy(mine.at[1 - p.z], self.zbuf.at[2], p.z_both)]
        for one in self.last:
            one.start()

    def s4(self, scale):
        p = self.place
        for one in self.last:
            one.wait()
        total = self.held[p.y, p.x, p.z].astype(F32)
        for k in range(3):
            total = total + self.zbuf[k].astype(F32)
        return total * scale


def put(part, block, first=0):
    cols = slice(first, first + block.shape[1])
    for b in range(NY * NX * NZ * NC):
        part[b % 2, b // 16, (b // 4) % 4, (b // 2) % 2, :, cols] = block[b * 16:(b + 1) * 16]


def body(scale, lat_in, grid_in, wsrc_in, wtgt_in, wmix_in, wout_in, truth_in, area_in, nbr, mask,
         d_latent_out, d_grid_out, o_src, o_tgt, o_mix, o_out,
         lat, grid, wsrc, wtgt, wmix, wout, truth, area,
         pick, pick_t, hits, hits_t, maskb, proj, tgt, slope, slope_sum, agg, normed, inv, ys, dys, dh, dq, dpe,
         agg_x, grid_x, lat_x,
         halo, rims, *rest):
    send_sem, recv_sem, halo_send, halo_recv, rim_send, rim_recv, y_send, y_recv, load_sem = rest[-9:]
    bufs = rest[:-9]
    members, rows, width = grid.shape
    nbrs = nbr.shape[0]
    fields = wout_in.shape[0]
    ext = rows + 2 * HALO
    tiles = width // CW
    flat = members * rows
    d_latent, d_grid = agg, normed
    place = Place()
    wire = Wire(send_sem, recv_sem)

    barrier = pltpu.get_barrier_semaphore()
    for partner in place.partners:
        pl.semaphore_signal(barrier, inc=1, device_id=partner, device_id_type=MESH)
    loads = [pltpu.make_async_copy(src, dst, load_sem.at[i])
             for i, (src, dst) in enumerate(((lat_in, lat), (grid_in, grid), (wtgt_in, wtgt), (wsrc_in, wsrc),
                                             (wmix_in, wmix)))]
    for one in loads:
        one.start()

    def copies(src, low, high, dst, sems, at, cols):
        return (
            pltpu.make_async_remote_copy(
                src_ref=src.at[at[0], pl.ds(high, HALO), cols], dst_ref=dst.at[at[0], pl.ds(0, HALO), cols],
                send_sem=sems[0].at[0, *at], recv_sem=sems[1].at[0, *at],
                device_id=place.up, device_id_type=MESH),
            pltpu.make_async_remote_copy(
                src_ref=src.at[at[0], pl.ds(low, HALO), cols], dst_ref=dst.at[at[0], pl.ds(HALO, HALO), cols],
                send_sem=sems[0].at[1, *at], recv_sem=sems[1].at[1, *at],
                device_id=place.down, device_id_type=MESH),
        )

    def halo_copies(m):
        return copies(lat, 0, rows - HALO, halo, (halo_send, halo_recv), (m,), slice(None))

    def rim_copies(m):
        return copies(dpe, rows, rows + HALO, rims, (rim_send, rim_recv), (m,), slice(None))

    def y_copy(m):
        return pltpu.make_async_remote_copy(
            src_ref=ys.at[m], dst_ref=ys.at[members + m],
            send_sem=y_send.at[m], recv_sem=y_recv.at[m],
            device_id=place.mate, device_id_type=MESH)

    loads[0].wait()
    pl.semaphore_wait(barrier, len(place.partners))

    def send_halo(m):
        for one in halo_copies(m):
            one.start()

    send_halo(0)

    truth[...] = jnp.zeros_like(truth)
    truth[0:fields, :] = truth_in[...]
    truth[...] = truth[...].T
    area[...] = jnp.broadcast_to(area_in[...], (rows, FP)).T
    wout[...] = jnp.zeros_like(wout)
    wout[0:fields, :] = wout_in[...]

    near = jnp.where(nbr[...] < HALO, nbr[...] + rows, jnp.where(nbr[...] < HALO + rows, nbr[...] - HALO, nbr[...]))
    code = jnp.where(mask[...] != 0, near, -1).astype(F32)
    code_t = jnp.concatenate([code, jnp.zeros((rows - nbrs, rows), F32)], axis=0).T
    lane = lax.broadcasted_iota(jnp.int32, (rows, ext), 1).astype(F32)
    sub = lax.broadcasted_iota(jnp.int32, (ext, rows), 0).astype(F32)
    count = jnp.zeros((rows, 1), F32)
    for k in range(nbrs):
        col = code_t[:, k:k + 1]
        on = jnp.where(col >= 0.0, 1.0, 0.0)
        one = (col == lane).astype(F32).astype(BF)
        one_t = (code[k:k + 1, :] == sub).astype(F32).astype(BF)
        pick[k] = one
        maskb[k] = jnp.broadcast_to(on, (rows, 128)).astype(BF)
        count = count + on
        pick_t[:, k * rows:(k + 1) * rows] = one_t
        if k == 0:
            hits[...] = one
            hits_t[...] = one_t
        else:
            hits[...] += one
            hits_t[...] += one_t

    def columns(step, first=0, last=tiles):
        def inner(c, _):
            step(pl.ds(pl.multiple_of(c * CW, CW), CW))
            return 0

        lax.fori_loop(first, last, inner, 0)

    def own_tgt(cols):
        got = (0.5 * dot(grid[...].reshape(flat, width), wtgt[:, cols]).astype(BF)).astype(BF)
        tgt[:, :, cols] = got.reshape(members, rows, CW)

    def own_src(cols):
        got = (0.5 * dot(lat[...].reshape(flat, width), wsrc[:, cols]).astype(BF)).astype(BF)
        proj[:, 0:rows, cols] = got.reshape(members, rows, CW)

    send_halo(1)
    loads[1].wait()
    loads[2].wait()
    columns(own_tgt)
    send_halo(2)
    loads[3].wait()
    columns(own_src)
    send_halo(3)

    def turn_grid(m, _):
        grid_x[:, pl.ds(pl.multiple_of(m * rows, rows), rows)] = grid[m].T
        lat_x[:, pl.ds(pl.multiple_of(m * ext, ext), rows)] = lat[m].T
        return 0

    lax.fori_loop(0, members, turn_grid, 0)
    loads[4].wait()

    gb = 32

    def forward(m, _):
        for one in halo_copies(m):
            one.wait()
        edge = (0.5 * dot(halo[m], wsrc[...]).astype(BF)).astype(BF)
        proj[m, rows:ext] = edge

        linear = dot(hits[...], proj[m]) + count * tgt[m].astype(F32)
        for at in range(0, rows, gb):
            got = dot(pick[:, at:at + gb, :].reshape(nbrs * gb, ext), proj[m]).astype(BF)
            got = got.reshape(nbrs, gb, width)
            for c in range(0, width, 256):
                cols = slice(c, c + 256)
                base = tgt[m, at:at + gb, cols]
                acc = None
                acc_s = None
                for k in range(nbrs):
                    on = maskb[k, at:at + gb, :]
                    u = got[k, :, cols] + jnp.concatenate([on, on], axis=1) * base
                    t = jnp.tanh(u)
                    p = u * t
                    s = (t + u) - t * p
                    acc = p if k == 0 else acc + p
                    acc_s = s if k == 0 else acc_s + s
                    slope[m, k, at:at + gb, cols] = s
                total = linear[at:at + gb, cols] + acc.astype(F32)
                agg[m, at:at + gb, cols] = (0.25 * total).astype(BF)
                slope_sum[m, at:at + gb, cols] = (acc_s.astype(F32) + count[at:at + gb]).astype(BF)

        h = grid[m].astype(F32) + dot(agg[m], wmix[...])
        mean = jnp.sum(h, axis=1, keepdims=True) * (1.0 / width)
        centre = h - mean
        var = jnp.sum(centre * centre, axis=1, keepdims=True) * (1.0 / width)
        r = lax.rsqrt(var + EPS)
        inv[m] = jnp.broadcast_to(r, (rows, 128))
        normed[m] = (centre * r).astype(BF)
        ys[m] = dot_nt(normed[m], wout[...])
        y_copy(m).start()
        return 0

    lax.fori_loop(0, members, forward, 0)

    def turn(m, _):
        at = pl.ds(pl.multiple_of(m * rows, rows), rows)
        agg_x[:, at] = agg[m].T
        lat_x[:, pl.ds(pl.multiple_of(m * ext + rows, rows), rows)] = halo[m].T
        return 0

    lax.fori_loop(0, members, turn, 0)

    def y_wait(m, _):
        y_copy(m).wait()
        return 0

    lax.fori_loop(0, members, y_wait, 0)

    total = 2 * members

    def head(m, _):
        y = ys[m]
        miss = y - truth[...]
        pair = jnp.zeros_like(y)
        for o in range(total):
            diff = y - ys[o]
            pair = pair + diff * lax.rsqrt(diff * diff + SMOOTH)
        grad = miss * lax.rsqrt(miss * miss + SMOOTH) * (1.0 / total)
        dy = (area[...] * (grad - (FAIR / (total * (total - 1))) * pair)).astype(BF)
        dys[m] = dy
        dn = dot(dy, wout[...])
        nh = normed[m].astype(F32)
        m1 = jnp.sum(dn, axis=1, keepdims=True) * (1.0 / width)
        m2 = jnp.sum(dn * nh, axis=1, keepdims=True) * (1.0 / width)
        dh[m] = (inv[m][:, 0:1] * (dn - m1 - nh * m2)).astype(BF)
        return 0

    lax.fori_loop(0, members, head, 0)

    halves = [Half(place, wire, i % 2 == 0, *bufs[5 * i:5 * i + 5]) for i in range(len(bufs) // 5)]
    mix, tgt_sum, src = halves[:2], halves[2:4], halves[4:]

    def each(parts, step):
        for one in parts:
            getattr(one, step)()

    def product(turned, right):
        return dot(turned[...], right.reshape(-1, right.shape[-1])).astype(BF)

    def mix_grad(cols):
        return product(agg_x, dh[:, :, cols])

    put(mix[0].part, mix_grad(pl.ds(0, CW)))
    mix[0].start()
    put(mix[1].part, mix_grad(pl.ds(CW, CW)))
    turned = jnp.concatenate([dys[m].T for m in range(members)], axis=1)
    put(mix[1].part, dot(turned, normed[...].reshape(flat, width)).T.astype(BF), CW)
    mix[1].start()

    def mix_back(cols):
        dagg = (0.125 * dot_nt(dh[...].reshape(flat, width), wmix[cols, :])).astype(BF)
        dagg = dagg.reshape(members, rows, CW)
        tgt[:, :, cols] = dagg
        dq[:, :, cols] = dagg * slope_sum[:, :, cols]

    columns(mix_back)

    def tgt_grad(cols):
        return product(grid_x, dq[:, :, cols])

    put(tgt_sum[0].part, tgt_grad(pl.ds(0, CW)))
    tgt_sum[0].start()
    put(tgt_sum[1].part, tgt_grad(pl.ds(CW, CW)))
    tgt_sum[1].start()
    each(mix, "s1")

    def spread(m):
        def column(cols):
            d = tgt[m, :, cols]
            for k in range(nbrs):
                slope[m, k, :, cols] = slope[m, k, :, cols] * d
            edges = slope[m, :, :, cols].reshape(nbrs * rows, CW)
            dpe[m, :, cols] = (dot(pick_t[...], edges) + dot(hits_t[...], d)).astype(BF)

        columns(column)
        for one in rim_copies(m):
            one.start()

    def src_grad(c):
        put(src[c].part, product(lat_x, dpe[:, :, c * CW:(c + 1) * CW]))

    def grid_back(cols):
        got = dot_nt(dq[...].reshape(flat, width), wtgt[cols, :]).reshape(members, rows, CW)
        d_grid[:, :, cols] = (dh[:, :, cols].astype(F32) + got).astype(BF)

    spread(0)
    each(tgt_sum, "s1")
    spread(1)
    spread(2)
    each(mix, "s2")
    spread(3)
    src_grad(0)
    src[0].start()
    each(tgt_sum, "s2")
    src_grad(1)
    src[1].start()
    each(mix, "s3")
    src[0].s1()
    columns(grid_back, 0, 1)
    src[1].s1()
    columns(grid_back, 1, 2)
    each(tgt_sum, "s3")
    out_grid = pltpu.make_async_copy(d_grid, d_grid_out, load_sem.at[5])
    out_grid.start()
    o_mix[:, 0:512] = mix[0].s4(scale)
    last = mix[1].s4(scale)
    o_mix[:, 512:width] = last[:, 0:width - 512]
    o_out[...] = last[:, width - 512:width - 512 + fields]

    def sum_rims(m, _):
        for one in rim_copies(m):
            one.wait()
        dq[m] = (dpe[m, 0:rows].astype(F32) + rims[m].astype(F32)).astype(BF)
        return 0

    lax.fori_loop(0, members, sum_rims, 0)

    def latent_back(cols):
        got = dot_nt(dq[...].reshape(flat, width), wsrc[cols, :]).reshape(members, rows, CW)
        d_latent[:, :, cols] = got.astype(BF)

    columns(latent_back, 0, 1)
    src[0].s2()
    columns(latent_back, 1, 2)
    out_latent = pltpu.make_async_copy(d_latent, d_latent_out, load_sem.at[6])
    out_latent.start()
    src[1].s2()
    for one, (first, size) in zip(tgt_sum, TGT_CUTS):
        o_tgt[:, first:first + size] = one.s4(scale)
    each(src, "s3")
    out_grid.wait()
    out_latent.wait()
    for one, (first, size) in zip(src, SRC_CUTS):
        o_src[:, first:first + size] = one.s4(scale)


def hand_over(arrays):
    count = len(arrays)
    pieces = [(i, m) for i, a in enumerate(arrays) for m in range(a.shape[0] if a.ndim == 3 else 1)]

    def move(*refs):
        held, (came, went) = refs[2 * count:3 * count], refs[3 * count:]

        def at(ref, i, m):
            return ref.at[m] if arrays[i].ndim == 3 else ref

        ins = [pltpu.make_async_copy(at(refs[i], i, m), at(held[i], i, m), came.at[n])
               for n, (i, m) in enumerate(pieces)]
        outs = [pltpu.make_async_copy(at(held[i], i, m), at(refs[count + i], i, m), went.at[n])
                for n, (i, m) in enumerate(pieces)]
        for one in ins:
            one.start()
        for one, other in zip(ins, outs):
            one.wait()
            other.start()
        for one in outs:
            one.wait()

    anywhere = pl.BlockSpec(memory_space=pl.ANY)
    return pl.pallas_call(
        move,
        out_shape=[jax.ShapeDtypeStruct(a.shape, a.dtype) for a in arrays],
        in_specs=[anywhere] * count,
        out_specs=[anywhere] * count,
        scratch_shapes=[*[pltpu.VMEM(a.shape, a.dtype) for a in arrays],
                        pltpu.SemaphoreType.DMA((len(pieces),)), pltpu.SemaphoreType.DMA((len(pieces),))],
    )(*arrays)


def on_device(latent, grid_in, w_src, w_tgt, w_mix, w_out, truth, area, nbr, mask):
    members, rows, width = grid_in.shape
    nbrs = nbr.shape[0]
    fields = w_out.shape[1]
    ext = rows + 2 * HALO
    tiles = lax.axis_size("grid")
    count = members * lax.axis_size("member")
    scale = 1.0 / math.sqrt(rows * tiles * count)

    def body_(*refs):
        body(scale, *refs)

    def ring_bufs(cols):
        return [pltpu.VMEM((NC, NY, NX, NZ, 16, cols), BF), pltpu.VMEM((NY, NX, NZ, 16, cols), BF),
                pltpu.VMEM((3, 4, NZ, 16, cols), BF), pltpu.VMEM((3, NZ, 16, cols), BF),
                pltpu.VMEM((3, 16, cols), BF)]

    vm = pl.BlockSpec(memory_space=pltpu.VMEM)
    hbm = pl.BlockSpec(memory_space=pl.ANY)
    sds = jax.ShapeDtypeStruct
    halves = [size for cuts in (MIX_CUTS, TGT_CUTS, SRC_CUTS) for _, size in cuts]
    ncopies = 10 * len(halves)
    results = pl.pallas_call(
        body_,
        out_shape=[
            sds((members, rows, width), BF),
            sds((members, rows, width), BF),
            sds((16, width), F32),
            sds((16, width), F32),
            sds((16, width), F32),
            sds((16, fields), F32),
        ],
        in_specs=[hbm, hbm, hbm, hbm, hbm, vm, vm, vm, vm, vm],
        out_specs=[hbm, hbm, vm, vm, vm, vm],
        scratch_shapes=[
            pltpu.VMEM((members, rows, width), BF),
            pltpu.VMEM((members, rows, width), BF),
            pltpu.VMEM((width, width), BF),
            pltpu.VMEM((width, width), BF),
            pltpu.VMEM((width, width), BF),
            pltpu.VMEM((FP, width), BF),
            pltpu.VMEM((FP, rows), F32),
            pltpu.VMEM((rows, FP), F32),
            pltpu.VMEM((nbrs, rows, ext), BF),
            pltpu.VMEM((ext, nbrs * rows), BF),
            pltpu.VMEM((rows, ext), BF),
            pltpu.VMEM((ext, rows), BF),
            pltpu.VMEM((nbrs, rows, 128), BF),
            pltpu.VMEM((members, ext, width), BF),
            pltpu.VMEM((members, rows, width), BF),
            pltpu.VMEM((members, nbrs, rows, width), BF),
            pltpu.VMEM((members, rows, width), BF),
            pltpu.VMEM((members, rows, width), BF),
            pltpu.VMEM((members, rows, width), BF),
            pltpu.VMEM((members, rows, 128), F32),
            pltpu.VMEM((2 * members, rows, FP), F32),
            pltpu.VMEM((members, rows, FP), BF),
            pltpu.VMEM((members, rows, width), BF),
            pltpu.VMEM((members, rows, width), BF),
            pltpu.VMEM((members, ext, width), BF),
            pltpu.VMEM((width, members * rows), BF),
            pltpu.VMEM((width, members * rows), BF),
            pltpu.VMEM((width, members * ext), BF),
            pltpu.VMEM((members, 2 * HALO, width), BF),
            pltpu.VMEM((members, 2 * HALO, width), BF),
            *[buf for cols in halves for buf in ring_bufs(cols)],
            pltpu.SemaphoreType.DMA((ncopies,)),
            pltpu.SemaphoreType.DMA((ncopies,)),
            pltpu.SemaphoreType.DMA((2, members)),
            pltpu.SemaphoreType.DMA((2, members)),
            pltpu.SemaphoreType.DMA((2, members)),
            pltpu.SemaphoreType.DMA((2, members)),
            pltpu.SemaphoreType.DMA((members,)),
            pltpu.SemaphoreType.DMA((members,)),
            pltpu.SemaphoreType.DMA((8,)),
        ],
        compiler_params=pltpu.CompilerParams(
            collective_id=0, has_side_effects=True, vmem_limit_bytes=63 * 2**20
        ),
        cost_estimate=pl.CostEstimate(flops=40 * 10**9, bytes_accessed=30 * 10**6, transcendentals=0),
    )(latent, grid_in, w_src, w_tgt, w_mix, w_out.T, truth, area.reshape(1, rows), nbr, mask)
    return hand_over(results)


def solution(mesh):
    in_specs = (
        P("member", "grid", None), P("member", "grid", None), P(), P(), P(), P(),
        P(None, "grid"), P("grid"), P(None, "grid"), P(None, "grid"),
    )
    out_specs = (
        P("member", "grid", None), P("member", "grid", None),
        P("grid", None), P("grid", None), P("grid", None), P("grid", None),
    )
    return jax.shard_map(
        on_device, mesh=mesh, in_specs=in_specs, out_specs=out_specs, check_vma=False
    )
```

```python
import math

import jax
import jax.numpy as jnp
from jax import lax
from jax.experimental import pallas as pl
from jax.experimental.pallas import tpu as pltpu
from jax.sharding import PartitionSpec as P

HALO = 64
SMOOTH = 0.0025
FAIR = 0.95
EPS = 1e-05
BF = jnp.bfloat16
F32 = jnp.float32
MESH = pl.DeviceIdType.MESH
CW = 512
NY, NX, NZ, NC = 4, 4, 2, 2
FP = 128
MIX_CUTS = ((0, 512), (512, 512 + FP))
TGT_CUTS = ((0, 512), (512, 512))
SRC_CUTS = ((0, 512), (512, 512))


def dot(a, b):
    return lax.dot_general(a, b, (((1,), (0,)), ((), ())), preferred_element_type=F32)


def dot_nt(a, b):
    return lax.dot_general(a, b, (((1,), (1,)), ((), ())), preferred_element_type=F32)


def dot_tn(a, b):
    return lax.dot_general(a, b, (((0,), (0,)), ((), ())), preferred_element_type=F32)


class Place:
    def __init__(self):
        self.me = lax.axis_index("member")
        t = lax.axis_index("grid")
        tiles = NY * NX * NZ * NC
        self.y, self.x, self.z, self.c = t // 16, (t // 4) % 4, (t // 2) % 2, t % 2
        self.up = (self.me, (t + 1) % tiles)
        self.down = (self.me, (t + tiles - 1) % tiles)
        self.mate = (1 - self.me, t)
        self.core = self.at(c=1 - self.c)
        self.y_ring = tuple(self.at(y=(self.y + k) % 4) for k in (1, 2, 3))
        self.x_ring = tuple(self.at(x=(self.x + k) % 4) for k in (1, 2, 3))
        self.z_far = (self.me, self.at(z=1 - self.z)[1])
        self.z_both = (1 - self.me, self.z_far[1])
        self.partners = (self.up, self.down, self.core, *self.y_ring, *self.x_ring,
                         self.mate, self.z_far, self.z_both)

    def at(self, y=None, x=None, z=None, c=None):
        y = self.y if y is None else y
        x = self.x if x is None else x
        z = self.z if z is None else z
        c = self.c if c is None else c
        return (self.me, y * 16 + x * 4 + z * 2 + c)


class Wire:
    def __init__(self, send, recv):
        self.send, self.recv, self.used = send, recv, 0

    def copy(self, src, dst, device):
        at = self.used
        self.used += 1
        return pltpu.make_async_remote_copy(
            src_ref=src, dst_ref=dst, send_sem=self.send.at[at], recv_sem=self.recv.at[at],
            device_id=device, device_id_type=MESH)


def add_into(dst, *others):
    total = dst[...].astype(F32)
    for o in others:
        total = total + o[...].astype(F32)
    dst[...] = total.astype(BF)


class Swap:
    def __init__(self, wire, p, others, block, buf):
        self.wire, self.p, self.others, self.block, self.buf = wire, p, others, block, buf

    def start(self):
        self.moves = [self.wire.copy(self.block((self.p + k) % 4), self.buf.at[k - 1], self.others[k - 1])
                      for k in (1, 3, 2)]
        for one in self.moves:
            one.start()

    def finish(self):
        for one in self.moves:
            one.wait()
        add_into(self.block(self.p), *[self.buf.at[k] for k in range(3)])


class Half:
    def __init__(self, place, wire, y_first, part, held, wide, thin, zbuf):
        self.place, self.wire, self.zbuf = place, wire, zbuf
        self.part, self.held = part, held
        y, x = place.y, place.x
        on_y, on_x = (y, place.y_ring), (x, place.x_ring)
        if y_first:
            self.one = Swap(wire, *on_y, lambda d: held.at[d], wide)
            self.two = Swap(wire, *on_x, lambda d: held.at[y, d], thin)
        else:
            self.one = Swap(wire, *on_x, lambda d: held.at[:, d], wide)
            self.two = Swap(wire, *on_y, lambda d: held.at[d, x], thin)

    def start(self):
        self.cross = self.wire.copy(self.part.at[1 - self.place.c], self.held, self.place.core)
        self.cross.start()

    def s1(self):
        self.cross.wait()

        def add(yy, _):
            add_into(self.held.at[yy], self.part.at[self.place.c, yy])
            return 0

        lax.fori_loop(0, NY, add, 0)
        self.one.start()

    def s2(self):
        self.one.finish()
        self.two.start()

    def s3(self):
        self.two.finish()
        p = self.place
        mine = self.held.at[p.y, p.x]
        self.last = [self.wire.copy(mine.at[p.z], self.zbuf.at[0], p.mate),
                     self.wire.copy(mine.at[1 - p.z], self.zbuf.at[1], p.z_far),
                     self.wire.copy(mine.at[1 - p.z], self.zbuf.at[2], p.z_both)]
        for one in self.last:
            one.start()

    def s4(self, scale):
        p = self.place
        for one in self.last:
            one.wait()
        total = self.held[p.y, p.x, p.z].astype(F32)
        for k in range(3):
            total = total + self.zbuf[k].astype(F32)
        return total * scale


def put(part, block, first=0):
    cols = slice(first, first + block.shape[1])
    for b in range(NY * NX * NZ * NC):
        part[b % 2, b // 16, (b // 4) % 4, (b // 2) % 2, :, cols] = block[b * 16:(b + 1) * 16]


def body(scale, lat_in, grid_in, wsrc_in, wtgt_in, wmix_in, wout_in, truth_in, area_in, nbr, mask,
         d_latent_out, d_grid_out, o_src, o_tgt, o_mix, o_out,
         lat, grid, wsrc, wtgt, wmix, wout, truth, area,
         pick, pick_t, hits, hits_t, maskb, proj, tgt, slope, slope_sum, agg, normed, inv, ys, dys, dh, dq, dpe,
         agg_x, grid_x, lat_x,
         halo, rims, *rest):
    send_sem, recv_sem, halo_send, halo_recv, rim_send, rim_recv, y_send, y_recv, load_sem = rest[-9:]
    bufs = rest[:-9]
    members, rows, width = grid.shape
    nbrs = nbr.shape[0]
    fields = wout_in.shape[0]
    ext = rows + 2 * HALO
    tiles = width // CW
    flat = members * rows
    d_latent, d_grid = agg, normed
    place = Place()
    wire = Wire(send_sem, recv_sem)

    barrier = pltpu.get_barrier_semaphore()
    for partner in place.partners:
        pl.semaphore_signal(barrier, inc=1, device_id=partner, device_id_type=MESH)
    loads = [pltpu.make_async_copy(src, dst, load_sem.at[i])
             for i, (src, dst) in enumerate(((lat_in, lat), (grid_in, grid), (wtgt_in, wtgt), (wsrc_in, wsrc),
                                             (wmix_in, wmix)))]
    for one in loads:
        one.start()

    def copies(src, low, high, dst, sems, at, cols):
        return (
            pltpu.make_async_remote_copy(
                src_ref=src.at[at[0], pl.ds(high, HALO), cols], dst_ref=dst.at[at[0], pl.ds(0, HALO), cols],
                send_sem=sems[0].at[0, *at], recv_sem=sems[1].at[0, *at],
                device_id=place.up, device_id_type=MESH),
            pltpu.make_async_remote_copy(
                src_ref=src.at[at[0], pl.ds(low, HALO), cols], dst_ref=dst.at[at[0], pl.ds(HALO, HALO), cols],
                send_sem=sems[0].at[1, *at], recv_sem=sems[1].at[1, *at],
                device_id=place.down, device_id_type=MESH),
        )

    def halo_copies(m):
        return copies(lat, 0, rows - HALO, halo, (halo_send, halo_recv), (m,), slice(None))

    def rim_copies(m):
        return copies(dpe, rows, rows + HALO, rims, (rim_send, rim_recv), (m,), slice(None))

    def y_copy(m):
        return pltpu.make_async_remote_copy(
            src_ref=ys.at[m], dst_ref=ys.at[members + m],
            send_sem=y_send.at[m], recv_sem=y_recv.at[m],
            device_id=place.mate, device_id_type=MESH)

    loads[0].wait()
    pl.semaphore_wait(barrier, len(place.partners))

    def send_halo(m):
        for one in halo_copies(m):
            one.start()

    send_halo(0)

    truth[...] = jnp.zeros_like(truth)
    truth[0:fields, :] = truth_in[...]
    truth[...] = truth[...].T
    area[...] = jnp.broadcast_to(area_in[...], (rows, FP)).T
    wout[...] = jnp.zeros_like(wout)
    wout[0:fields, :] = wout_in[...]

    near = jnp.where(nbr[...] < HALO, nbr[...] + rows, jnp.where(nbr[...] < HALO + rows, nbr[...] - HALO, nbr[...]))
    code = jnp.where(mask[...] != 0, near, -1).astype(F32)
    code_t = jnp.concatenate([code, jnp.zeros((rows - nbrs, rows), F32)], axis=0).T
    lane = lax.broadcasted_iota(jnp.int32, (rows, ext), 1).astype(F32)
    sub = lax.broadcasted_iota(jnp.int32, (ext, rows), 0).astype(F32)
    count = jnp.zeros((rows, 1), F32)
    for k in range(nbrs):
        col = code_t[:, k:k + 1]
        on = jnp.where(col >= 0.0, 1.0, 0.0)
        one = (col == lane).astype(F32).astype(BF)
        one_t = (code[k:k + 1, :] == sub).astype(F32).astype(BF)
        pick[k] = one
        maskb[k] = jnp.broadcast_to(on, (rows, 128)).astype(BF)
        count = count + on
        pick_t[:, k * rows:(k + 1) * rows] = one_t
        if k == 0:
            hits[...] = one
            hits_t[...] = one_t
        else:
            hits[...] += one
            hits_t[...] += one_t

    def columns(step, first=0, last=tiles):
        def inner(c, _):
            step(pl.ds(pl.multiple_of(c * CW, CW), CW))
            return 0

        lax.fori_loop(first, last, inner, 0)

    def own_tgt(cols):
        got = (0.5 * dot(grid[...].reshape(flat, width), wtgt[:, cols]).astype(BF)).astype(BF)
        tgt[:, :, cols] = got.reshape(members, rows, CW)

    def own_src(cols):
        got = (0.5 * dot(lat[...].reshape(flat, width), wsrc[:, cols]).astype(BF)).astype(BF)
        proj[:, 0:rows, cols] = got.reshape(members, rows, CW)

    send_halo(1)
    loads[1].wait()
    loads[2].wait()
    columns(own_tgt)
    send_halo(2)
    loads[3].wait()
    columns(own_src)
    send_halo(3)

    def turn_grid(m, _):
        grid_x[:, pl.ds(pl.multiple_of(m * rows, rows), rows)] = grid[m].T
        lat_x[:, pl.ds(pl.multiple_of(m * ext, ext), rows)] = lat[m].T
        return 0

    lax.fori_loop(0, members, turn_grid, 0)
    loads[4].wait()

    gb = 32

    def forward(m, _):
        for one in halo_copies(m):
            one.wait()
        edge = (0.5 * dot(halo[m], wsrc[...]).astype(BF)).astype(BF)
        proj[m, rows:ext] = edge

        linear = dot(hits[...], proj[m]) + count * tgt[m].astype(F32)
        for at in range(0, rows, gb):
            got = dot(pick[:, at:at + gb, :].reshape(nbrs * gb, ext), proj[m]).astype(BF)
            got = got.reshape(nbrs, gb, width)
            for c in range(0, width, 256):
                cols = slice(c, c + 256)
                base = tgt[m, at:at + gb, cols]
                acc = None
                acc_s = None
                for k in range(nbrs):
                    on = maskb[k, at:at + gb, :]
                    u = got[k, :, cols] + jnp.concatenate([on, on], axis=1) * base
                    t = jnp.tanh(u)
                    p = u * t
                    s = (t + u) - t * p
                    acc = p if k == 0 else acc + p
                    acc_s = s if k == 0 else acc_s + s
                    slope[m, k, at:at + gb, cols] = s
                total = linear[at:at + gb, cols] + acc.astype(F32)
                agg[m, at:at + gb, cols] = (0.25 * total).astype(BF)
                slope_sum[m, at:at + gb, cols] = (acc_s.astype(F32) + count[at:at + gb]).astype(BF)

        h = grid[m].astype(F32) + dot(agg[m], wmix[...])
        mean = jnp.sum(h, axis=1, keepdims=True) * (1.0 / width)
        centre = h - mean
        var = jnp.sum(centre * centre, axis=1, keepdims=True) * (1.0 / width)
        r = lax.rsqrt(var + EPS)
        inv[m] = jnp.broadcast_to(r, (rows, 128))
        normed[m] = (centre * r).astype(BF)
        ys[m] = dot_nt(normed[m], wout[...])
        y_copy(m).start()
        return 0

    lax.fori_loop(0, members, forward, 0)

    def turn(m, _):
        at = pl.ds(pl.multiple_of(m * rows, rows), rows)
        agg_x[:, at] = agg[m].T
        lat_x[:, pl.ds(pl.multiple_of(m * ext + rows, rows), rows)] = halo[m].T
        return 0

    lax.fori_loop(0, members, turn, 0)

    def y_wait(m, _):
        y_copy(m).wait()
        return 0

    lax.fori_loop(0, members, y_wait, 0)

    total = 2 * members

    def head(m, _):
        y = ys[m]
        miss = y - truth[...]
        pair = jnp.zeros_like(y)
        for o in range(total):
            diff = y - ys[o]
            pair = pair + diff * lax.rsqrt(diff * diff + SMOOTH)
        grad = miss * lax.rsqrt(miss * miss + SMOOTH) * (1.0 / total)
        dy = (area[...] * (grad - (FAIR / (total * (total - 1))) * pair)).astype(BF)
        dys[m] = dy
        dn = dot(dy, wout[...])
        nh = normed[m].astype(F32)
        m1 = jnp.sum(dn, axis=1, keepdims=True) * (1.0 / width)
        m2 = jnp.sum(dn * nh, axis=1, keepdims=True) * (1.0 / width)
        dh[m] = (inv[m][:, 0:1] * (dn - m1 - nh * m2)).astype(BF)
        return 0

    lax.fori_loop(0, members, head, 0)

    halves = [Half(place, wire, i % 2 == 0, *bufs[5 * i:5 * i + 5]) for i in range(len(bufs) // 5)]
    mix, tgt_sum, src = halves[:2], halves[2:4], halves[4:]

    def each(parts, step):
        for one in parts:
            getattr(one, step)()

    def product(turned, right):
        return dot(turned[...], right.reshape(-1, right.shape[-1])).astype(BF)

    def mix_grad(cols):
        return product(agg_x, dh[:, :, cols])

    put(mix[0].part, mix_grad(pl.ds(0, CW)))
    mix[0].start()
    put(mix[1].part, mix_grad(pl.ds(CW, CW)))
    turned = jnp.concatenate([dys[m].T for m in range(members)], axis=1)
    put(mix[1].part, dot(turned, normed[...].reshape(flat, width)).T.astype(BF), CW)
    mix[1].start()

    def mix_back(cols):
        dagg = (0.125 * dot_nt(dh[...].reshape(flat, width), wmix[cols, :])).astype(BF)
        dagg = dagg.reshape(members, rows, CW)
        tgt[:, :, cols] = dagg
        dq[:, :, cols] = dagg * slope_sum[:, :, cols]

    columns(mix_back)

    def tgt_grad(cols):
        return product(grid_x, dq[:, :, cols])

    put(tgt_sum[0].part, tgt_grad(pl.ds(0, CW)))
    tgt_sum[0].start()
    put(tgt_sum[1].part, tgt_grad(pl.ds(CW, CW)))
    tgt_sum[1].start()
    each(mix, "s1")

    def spread(m):
        def column(cols):
            d = tgt[m, :, cols]
            for k in range(nbrs):
                slope[m, k, :, cols] = slope[m, k, :, cols] * d
            edges = slope[m, :, :, cols].reshape(nbrs * rows, CW)
            dpe[m, :, cols] = (dot(pick_t[...], edges) + dot(hits_t[...], d)).astype(BF)

        columns(column)
        for one in rim_copies(m):
            one.start()

    def src_grad(c):
        put(src[c].part, product(lat_x, dpe[:, :, c * CW:(c + 1) * CW]))

    def grid_back(cols):
        got = dot_nt(dq[...].reshape(flat, width), wtgt[cols, :]).reshape(members, rows, CW)
        d_grid[:, :, cols] = (dh[:, :, cols].astype(F32) + got).astype(BF)

    spread(0)
    each(tgt_sum, "s1")
    spread(1)
    each(mix, "s2")
    spread(2)
    spread(3)
    each(tgt_sum, "s2")
    src_grad(0)
    src[0].start()
    each(mix, "s3")
    src_grad(1)
    src[1].start()
    src[0].s1()
    columns(grid_back, 0, 1)
    src[1].s1()
    columns(grid_back, 1, 2)
    each(tgt_sum, "s3")
    out_grid = pltpu.make_async_copy(d_grid, d_grid_out, load_sem.at[5])
    out_grid.start()
    o_mix[:, 0:512] = mix[0].s4(scale)
    last = mix[1].s4(scale)
    o_mix[:, 512:width] = last[:, 0:width - 512]
    o_out[...] = last[:, width - 512:width - 512 + fields]

    def sum_rims(m, _):
        for one in rim_copies(m):
            one.wait()
        dq[m] = (dpe[m, 0:rows].astype(F32) + rims[m].astype(F32)).astype(BF)
        return 0

    lax.fori_loop(0, members, sum_rims, 0)

    def latent_back(cols):
        got = dot_nt(dq[...].reshape(flat, width), wsrc[cols, :]).reshape(members, rows, CW)
        d_latent[:, :, cols] = got.astype(BF)

    columns(latent_back, 0, 1)
    src[0].s2()
    columns(latent_back, 1, 2)
    out_latent = pltpu.make_async_copy(d_latent, d_latent_out, load_sem.at[6])
    out_latent.start()
    src[1].s2()
    for one, (first, size) in zip(tgt_sum, TGT_CUTS):
        o_tgt[:, first:first + size] = one.s4(scale)
    each(src, "s3")
    out_grid.wait()
    out_latent.wait()
    for one, (first, size) in zip(src, SRC_CUTS):
        o_src[:, first:first + size] = one.s4(scale)


def hand_over(arrays):
    count = len(arrays)
    pieces = [(i, m) for i, a in enumerate(arrays) for m in range(a.shape[0] if a.ndim == 3 else 1)]

    def move(*refs):
        held, (came, went) = refs[2 * count:3 * count], refs[3 * count:]

        def at(ref, i, m):
            return ref.at[m] if arrays[i].ndim == 3 else ref

        ins = [pltpu.make_async_copy(at(refs[i], i, m), at(held[i], i, m), came.at[n])
               for n, (i, m) in enumerate(pieces)]
        outs = [pltpu.make_async_copy(at(held[i], i, m), at(refs[count + i], i, m), went.at[n])
                for n, (i, m) in enumerate(pieces)]
        for one in ins:
            one.start()
        for one, other in zip(ins, outs):
            one.wait()
            other.start()
        for one in outs:
            one.wait()

    anywhere = pl.BlockSpec(memory_space=pl.ANY)
    return pl.pallas_call(
        move,
        out_shape=[jax.ShapeDtypeStruct(a.shape, a.dtype) for a in arrays],
        in_specs=[anywhere] * count,
        out_specs=[anywhere] * count,
        scratch_shapes=[*[pltpu.VMEM(a.shape, a.dtype) for a in arrays],
                        pltpu.SemaphoreType.DMA((len(pieces),)), pltpu.SemaphoreType.DMA((len(pieces),))],
    )(*arrays)


def on_device(latent, grid_in, w_src, w_tgt, w_mix, w_out, truth, area, nbr, mask):
    members, rows, width = grid_in.shape
    nbrs = nbr.shape[0]
    fields = w_out.shape[1]
    ext = rows + 2 * HALO
    tiles = lax.axis_size("grid")
    count = members * lax.axis_size("member")
    scale = 1.0 / math.sqrt(rows * tiles * count)

    def body_(*refs):
        body(scale, *refs)

    def ring_bufs(cols):
        return [pltpu.VMEM((NC, NY, NX, NZ, 16, cols), BF), pltpu.VMEM((NY, NX, NZ, 16, cols), BF),
                pltpu.VMEM((3, 4, NZ, 16, cols), BF), pltpu.VMEM((3, NZ, 16, cols), BF),
                pltpu.VMEM((3, 16, cols), BF)]

    vm = pl.BlockSpec(memory_space=pltpu.VMEM)
    hbm = pl.BlockSpec(memory_space=pl.ANY)
    sds = jax.ShapeDtypeStruct
    halves = [size for cuts in (MIX_CUTS, TGT_CUTS, SRC_CUTS) for _, size in cuts]
    ncopies = 10 * len(halves)
    results = pl.pallas_call(
        body_,
        out_shape=[
            sds((members, rows, width), BF),
            sds((members, rows, width), BF),
            sds((16, width), F32),
            sds((16, width), F32),
            sds((16, width), F32),
            sds((16, fields), F32),
        ],
        in_specs=[hbm, hbm, hbm, hbm, hbm, vm, vm, vm, vm, vm],
        out_specs=[hbm, hbm, vm, vm, vm, vm],
        scratch_shapes=[
            pltpu.VMEM((members, rows, width), BF),
            pltpu.VMEM((members, rows, width), BF),
            pltpu.VMEM((width, width), BF),
            pltpu.VMEM((width, width), BF),
            pltpu.VMEM((width, width), BF),
            pltpu.VMEM((FP, width), BF),
            pltpu.VMEM((FP, rows), F32),
            pltpu.VMEM((rows, FP), F32),
            pltpu.VMEM((nbrs, rows, ext), BF),
            pltpu.VMEM((ext, nbrs * rows), BF),
            pltpu.VMEM((rows, ext), BF),
            pltpu.VMEM((ext, rows), BF),
            pltpu.VMEM((nbrs, rows, 128), BF),
            pltpu.VMEM((members, ext, width), BF),
            pltpu.VMEM((members, rows, width), BF),
            pltpu.VMEM((members, nbrs, rows, width), BF),
            pltpu.VMEM((members, rows, width), BF),
            pltpu.VMEM((members, rows, width), BF),
            pltpu.VMEM((members, rows, width), BF),
            pltpu.VMEM((members, rows, 128), F32),
            pltpu.VMEM((2 * members, rows, FP), F32),
            pltpu.VMEM((members, rows, FP), BF),
            pltpu.VMEM((members, rows, width), BF),
            pltpu.VMEM((members, rows, width), BF),
            pltpu.VMEM((members, ext, width), BF),
            pltpu.VMEM((width, members * rows), BF),
            pltpu.VMEM((width, members * rows), BF),
            pltpu.VMEM((width, members * ext), BF),
            pltpu.VMEM((members, 2 * HALO, width), BF),
            pltpu.VMEM((members, 2 * HALO, width), BF),
            *[buf for cols in halves for buf in ring_bufs(cols)],
            pltpu.SemaphoreType.DMA((ncopies,)),
            pltpu.SemaphoreType.DMA((ncopies,)),
            pltpu.SemaphoreType.DMA((2, members)),
            pltpu.SemaphoreType.DMA((2, members)),
            pltpu.SemaphoreType.DMA((2, members)),
            pltpu.SemaphoreType.DMA((2, members)),
            pltpu.SemaphoreType.DMA((members,)),
            pltpu.SemaphoreType.DMA((members,)),
            pltpu.SemaphoreType.DMA((8,)),
        ],
        compiler_params=pltpu.CompilerParams(
            collective_id=0, has_side_effects=True, vmem_limit_bytes=63 * 2**20
        ),
        cost_estimate=pl.CostEstimate(flops=40 * 10**9, bytes_accessed=30 * 10**6, transcendentals=0),
    )(latent, grid_in, w_src, w_tgt, w_mix, w_out.T, truth, area.reshape(1, rows), nbr, mask)
    return hand_over(results)


def solution(mesh):
    in_specs = (
        P("member", "grid", None), P("member", "grid", None), P(), P(), P(), P(),
        P(None, "grid"), P("grid"), P(None, "grid"), P(None, "grid"),
    )
    out_specs = (
        P("member", "grid", None), P("member", "grid", None),
        P("grid", None), P("grid", None), P("grid", None), P("grid", None),
    )
    return jax.shard_map(
        on_device, mesh=mesh, in_specs=in_specs, out_specs=out_specs, check_vma=False
    )
```
